128 devices in a mesh: ctx: 32 (over z, y_hi, x), seq: 4 (over y_lo, core).
Axes of the slice: x: 4, y: 4 (y_hi: 2, y_lo: 2; y = y_hi * 2 + y_lo), z: 4, core: 2. Of those that a mesh axis runs over, the one named last changes fastest.
Arguments:
- projected: bfloat16 [4, 3, 4096, 4096], P('seq', None, 'ctx'), may hold values from -6 to 6
- cotangent: bfloat16 [4, 4096, 4096], P('seq', 'ctx'), may hold values from -6 to 6
- short_filter: float32 [3, 7, 256], replicated, may hold values from -2.4 to 2.4
- residue: float32 [16, 256], replicated, may hold values from -0.09 to 0.09
- decay_rate: float32 [16, 256], replicated, may hold values from 7.927418e-06 to 0.3
Outputs:
- gated_output: bfloat16 [4, 4096, 4096], P('seq', 'ctx')
- grad_projected: bfloat16 [4, 3, 4096, 4096], P('seq', None, 'ctx')
- grad_short: float32 [3, 7, 256], replicated
- grad_residue: float32 [16, 256], replicated
- grad_log_decay: float32 [16, 256], replicated
The draws below stay inside these ranges and needn't reach their ends.
All inputs are finite; a program needn't handle non-finite values.
Results may differ from the reference program's by a relative error of at most 0.001.
Values may be sent and summed in bfloat16 or wider, within the bound.
A program may use at most 192 MiB of HBM per device.

```python
import math
from functools import partial
import jax
import jax.numpy as jnp
from jax import lax

C = 4096
GROUP = 16
MODES = 16
TAPS = 7
G = 256
TOKENS = 4096
GENOMES = 4


def draw_decay_rate(key, part):
    key = jax.random.fold_in(key, 7)
    order_key, spot_key = jax.random.split(key)
    stratum_rank = jnp.broadcast_to(jnp.arange(MODES, dtype=jnp.int32)[:, None], (MODES, G))
    stratum_rank = jax.random.permutation(order_key, stratum_rank, axis=0, independent=True)
    within = jax.random.uniform(spot_key, (MODES, G), jnp.float32)
    half_count = MODES // 2
    low_log = math.log(min(0.003, 133.0 / (TOKENS * TOKENS)))
    pivot_log = math.log(2.0 / TOKENS)
    high_log = math.log(0.3)
    in_lower = stratum_rank < half_count
    slot_place = (stratum_rank % half_count).astype(jnp.float32)
    fraction = (slot_place + within) / float(half_count)
    lower_log = low_log + fraction * (pivot_log - low_log)
    upper_log = pivot_log + fraction * (high_log - pivot_log)
    return jnp.exp(jnp.where(in_lower, lower_log, upper_log)).astype(jnp.float32)


def level_of(own_key, dims, shards, least, largest):
    def one(axis_at, shards_of):
        steps = jax.random.uniform(jax.random.fold_in(jax.random.fold_in(own_key, 6), axis_at), (shards_of,), jnp.float32, least / len(shards), largest / len(shards))
        return jnp.repeat(jnp.exp(steps), dims[axis_at] // shards_of).reshape((-1,) + (1,) * (len(dims) - axis_at - 1))

    loudness = one(*shards[0])
    for cut in shards[1:]:
        loudness = loudness * one(*cut)
    return loudness


def noise(own_key, dims, scale, reach, cuts=(), kind=jnp.bfloat16):
    factor_of = level_of(own_key, dims, cuts, -0.22, 0.18) if cuts else 1.0
    entries = jax.random.normal(own_key, dims, jnp.float32) * scale * factor_of
    return jnp.minimum(jnp.maximum(entries, -reach), reach).astype(kind)


def setup_inputs(seed: int = 0) -> dict:
    streams_of = jax.random.split(jax.random.key(seed), 6)
    projected = noise(streams_of[0], (GENOMES, 3, TOKENS, C), 1.0, 6.0, ((0, 4), (2, 32)))
    cotangent = noise(streams_of[1], (GENOMES, TOKENS, C), 1.0, 6.0, ((0, 4), (1, 32)))
    short_filter = noise(streams_of[2], (3, TAPS, G), 0.4, 2.4, (), jnp.float32)
    residue = noise(streams_of[3], (MODES, G), 0.015, 0.09, (), jnp.float32)
    decay_rate = draw_decay_rate(jax.random.fold_in(streams_of[5], 71), 0)
    return {"projected": projected, "cotangent": cotangent, "short_filter": short_filter, "residue": residue, "decay_rate": decay_rate}


HIGHEST_PRECISION = lax.Precision.HIGHEST


def featurize(padded, per_channel, row_count):
    reach_len = per_channel.shape[1] - 1
    summed = jnp.zeros((padded.shape[0], row_count, padded.shape[2]), jnp.float32)
    for tap_index in range(per_channel.shape[1]):
        window = padded[:, reach_len - tap_index:reach_len - tap_index + row_count, :]
        summed = summed + per_channel[:, tap_index, None, :] * window
    return summed


def transpose_featurize(extended, per_channel, row_count):
    summed = jnp.zeros((extended.shape[0], row_count, extended.shape[2]), jnp.float32)
    for tap_index in range(per_channel.shape[1]):
        summed = summed + per_channel[:, tap_index, None, :] * extended[:, tap_index:tap_index + row_count, :]
    return summed


def filter_terms(feat_grad, padded, row_count):
    reach_len = padded.shape[1] - row_count
    columns = []
    for tap_index in range(reach_len + 1):
        window = padded[:, reach_len - tap_index:reach_len - tap_index + row_count, :]
        columns.append(jnp.sum(feat_grad * window, axis=1))
    return jnp.stack(columns, axis=1)


def make_tables(residue, decay_rate, block_len):
    ramp_vec = jnp.arange(block_len, dtype=jnp.float32)
    ramp_col = ramp_vec[:, None, None]
    powers = jnp.exp(-decay_rate[None] * ramp_col)
    inverse = jnp.exp(decay_rate[None] * ramp_col)
    powers_next = jnp.exp(-decay_rate[None] * (ramp_col + 1.0))
    tail_pow = jnp.exp(-decay_rate[None] * (block_len - 1.0 - ramp_col))
    tail_lag = tail_pow * (block_len - 1.0 - ramp_col)
    back_pow = jnp.exp(-decay_rate[None] * (block_len - ramp_col))
    block_decay = jnp.exp(-decay_rate * block_len)[:, :, None]
    causal = (ramp_vec[:, None] >= ramp_vec[None, :]).astype(jnp.float32)
    toeplitz = jnp.einsum("img,jmg->gij", residue[None] * powers, inverse, precision=HIGHEST_PRECISION) * causal[None]
    return (ramp_vec, powers, inverse, powers_next, tail_pow, tail_lag, back_pow, block_decay, causal, toeplitz)


def block_forward(running, mixer_block, tables_all, residue):
    ramp_vec, powers, inverse, powers_next, tail_pow, tail_lag, back_pow, block_decay, causal, toeplitz = tables_all
    state_x, state_w = running
    block_len = mixer_block.shape[0]
    inside = jnp.einsum("gij,jgc->igc", toeplitz, mixer_block, precision=HIGHEST_PRECISION)
    carried = jnp.einsum("img,mgc->igc", residue[None] * powers_next, state_x, precision=HIGHEST_PRECISION)
    next_x = block_decay * state_x + jnp.einsum("jmg,jgc->mgc", tail_pow, mixer_block, precision=HIGHEST_PRECISION)
    next_w = block_decay * (state_w + block_len * state_x) + jnp.einsum("jmg,jgc->mgc", tail_lag, mixer_block, precision=HIGHEST_PRECISION)
    return (next_x, next_w), (inside + carried, state_x, state_w)


def block_backward(running, inputs_block, tables_all, residue):
    ramp_vec, powers, inverse, powers_next, tail_pow, tail_lag, back_pow, block_decay, causal, toeplitz = tables_all
    adjoint, grad_res, grad_lag = running
    conv_grad, mixer_block, start_x, start_w = inputs_block
    inside = jnp.einsum("gij,igc->jgc", toeplitz, conv_grad, precision=HIGHEST_PRECISION)
    carried = jnp.einsum("jmg,mgc->jgc", residue[None] * back_pow, adjoint, precision=HIGHEST_PRECISION)
    next_adj = block_decay * adjoint + jnp.einsum("img,igc->mgc", powers, conv_grad, precision=HIGHEST_PRECISION)
    pair_sums = jnp.einsum("igc,jgc->gij", conv_grad, mixer_block, precision=HIGHEST_PRECISION) * causal[None]
    inner_one = jnp.einsum("gij,jmg->gim", pair_sums, inverse, precision=HIGHEST_PRECISION)
    inner_two = jnp.einsum("gij,jmg->gim", pair_sums, inverse * ramp_vec[:, None, None], precision=HIGHEST_PRECISION)
    local_res = jnp.einsum("gim,img->mg", inner_one, powers, precision=HIGHEST_PRECISION)
    local_lag = jnp.einsum("gim,img->mg", inner_one * ramp_vec[None, :, None] - inner_two, powers, precision=HIGHEST_PRECISION)
    meets_x = jnp.einsum("igc,mgc->img", conv_grad, start_x, precision=HIGHEST_PRECISION)
    meets_w = jnp.einsum("igc,mgc->img", conv_grad, start_w, precision=HIGHEST_PRECISION)
    cross_res = jnp.sum(powers_next * meets_x, axis=0)
    cross_lag = jnp.sum((ramp_vec[:, None, None] + 1.0) * powers_next * meets_x + powers_next * meets_w, axis=0)
    return (next_adj, grad_res + local_res + cross_res, grad_lag + local_lag + cross_lag), inside + carried


def one_genome(tokens, cotangent, per_channel, residue, decay_rate, block_len):
    reach_len = per_channel.shape[1] - 1
    row_count = tokens.shape[1]
    channels = tokens.shape[2]
    groups = residue.shape[1]
    mode_count = residue.shape[0]
    block_count = row_count // block_len
    padded = jnp.concatenate([jnp.zeros((3, reach_len, channels), tokens.dtype), tokens], axis=1)
    features = featurize(padded, per_channel, row_count)
    mixer_in = features[1] * features[2]
    tables_all = make_tables(residue, decay_rate, block_len)
    mixer_blocks = mixer_in.reshape(block_count, block_len, groups, GROUP)
    blank = jnp.zeros((mode_count, groups, GROUP), jnp.float32)
    ending, (conv_blocks, start_x, start_w) = lax.scan(partial(block_forward, tables_all=tables_all, residue=residue), (blank, blank), mixer_blocks)
    long_conv = conv_blocks.reshape(row_count, channels)
    gated_output = (features[0] * long_conv).astype(jnp.bfloat16)
    conv_grad = cotangent * features[0]
    first_grad = cotangent * long_conv
    grad_zero = jnp.zeros((mode_count, groups), jnp.float32)
    (start_adj, grad_res, grad_lag), mixer_grad = lax.scan(partial(block_backward, tables_all=tables_all, residue=residue), (blank, grad_zero, grad_zero), (conv_grad.reshape(block_count, block_len, groups, GROUP), mixer_blocks, start_x, start_w), reverse=True)
    mixer_grad = mixer_grad.reshape(row_count, channels)
    feat_grad = jnp.stack([first_grad, mixer_grad * features[2], mixer_grad * features[1]])
    extended = jnp.concatenate([feat_grad, jnp.zeros((3, reach_len, channels), jnp.float32)], axis=1)
    grad_tokens = transpose_featurize(extended, per_channel, row_count).astype(jnp.bfloat16)
    short_terms = filter_terms(feat_grad, padded, row_count)
    return gated_output, grad_tokens, short_terms, grad_res, grad_lag


def reference(projected, cotangent, short_filter, residue, decay_rate):
    per_channel = jnp.repeat(short_filter, GROUP, axis=2)
    block_len = math.gcd(TOKENS, 32)

    def genome(inputs_pair):
        return one_genome(inputs_pair[0], inputs_pair[1], per_channel, residue, decay_rate, block_len)

    gated_output, grad_projected, short_terms, grad_res, grad_lag = lax.map(genome, (projected, cotangent))
    total_tokens = float(TOKENS * GENOMES)
    short_sum = jnp.sum(short_terms, axis=0)
    grad_short = short_sum.reshape(3, short_sum.shape[1], short_filter.shape[2], GROUP).sum(axis=3) / total_tokens
    grad_residue = jnp.sum(grad_res, axis=0) / total_tokens
    grad_log_decay = -residue * decay_rate * jnp.sum(grad_lag, axis=0) / total_tokens
    return (gated_output, grad_projected, grad_short, grad_residue, grad_log_decay)
```

```python
from functools import partial

import jax
import jax.numpy as jnp
from jax import lax
from jax.experimental import pallas as pl
from jax.experimental.pallas import tpu as pltpu
from jax.sharding import PartitionSpec as P

GROUP = 16
MODES = 16
TAPS = 7
LANES = 128
TILE_GROUPS = LANES // GROUP
ROWS = 128
F32, BF16 = jnp.float32, jnp.bfloat16
MESH = pl.DeviceIdType.MESH

DECAY, RESIDUE, SHORT, DECAY_GM, RESIDUE_GM, TABLE_ROWS = 0, 16, 32, 53, 54, 56


def split(value):
    high = value.astype(BF16)
    return high, (value - high.astype(F32)).astype(BF16)


def iota(shape, dim):
    return lax.broadcasted_iota(jnp.int32, shape, dim)


def dot(left, right):
    return jnp.dot(left, right, preferred_element_type=F32)


def in_group(rows, width, group):
    return (iota((rows, width), 1) % LANES) // GROUP == group


def flip_matrix():
    return (iota((ROWS, ROWS), 0) + iota((ROWS, ROWS), 1) == ROWS - 1).astype(BF16)


def load_tokens(pad, proj_ref, before_ref, lanes):
    for i in range(3):
        pad[i, 0:8, :] = before_ref[i, :, lanes]
        pad[i, 8 : 8 + ROWS, :] = proj_ref[i, :, lanes].astype(F32)


def feature(pad, taps, i, start, count):
    total = None
    for j in range(TAPS):
        term = taps[TAPS * i + j] * pad[i, 8 + start - j : 8 + start - j + count, :]
        total = term if total is None else total + term
    return total


def tap_rows(wide_ref, lanes):
    return [wide_ref[SHORT + k : SHORT + k + 1, lanes] for k in range(3 * TAPS)]


def halo_kernel(
    n, proj_ref, cot_ref, before_ref, after_ref, rows_tail, rows_head, out_f, out_b, got_f, got_b,
    load_sem, send_sem, recv_sem,
):
    me = lax.axis_index("ctx")
    right, left = lax.rem(me + 1, n), lax.rem(me + n - 1, n)
    loads = [
        pltpu.make_async_copy(proj_ref.at[:, pl.ds(ROWS - 16, 16), :], rows_tail, load_sem.at[0]),
        pltpu.make_async_copy(
            proj_ref.at[:, pl.ds(0, 16), :], rows_head.at[pl.ds(0, 3)], load_sem.at[1]
        ),
        pltpu.make_async_copy(cot_ref.at[pl.ds(0, 16), :], rows_head.at[3], load_sem.at[2]),
    ]
    for load in loads:
        load.start()
    barrier = pltpu.get_barrier_semaphore()
    for neighbour in (left, right):
        pl.semaphore_signal(barrier, inc=1, device_id={"ctx": neighbour}, device_id_type=MESH)
    for load in loads:
        load.wait()
    half = rows_tail.shape[2] // 2
    for i in range(3):
        tail = rows_tail[i].astype(F32)[8:16]
        out_f[i] = jnp.concatenate([tail[:, :half], tail[:, half:]], axis=0).astype(BF16)
    for i in range(4):
        head = rows_head[i].astype(F32)[0:8]
        out_b[i] = jnp.concatenate([head[:, :half], head[:, half:]], axis=0).astype(BF16)
    pl.semaphore_wait(barrier, 2)
    copies = [
        pltpu.make_async_remote_copy(
            src_ref=source,
            dst_ref=target,
            send_sem=send_sem.at[k],
            recv_sem=recv_sem.at[k],
            device_id={"ctx": to},
            device_id_type=MESH,
        )
        for k, (source, target, to) in enumerate([(out_f, got_f, right), (out_b, got_b, left)])
    ]
    for copy in copies:
        copy.start()
    for copy in copies:
        copy.wait()
    first, last = me == 0, me == n - 1
    for i in range(3):
        part = jnp.where(first, 0.0, got_f[i].astype(F32))
        before_ref[i, :, 0:half] = part[0:8]
        before_ref[i, :, half : 2 * half] = part[8:16]
    for i in range(4):
        part = jnp.where(last, 0.0, got_b[i].astype(F32))
        after_ref[i, :, 0:half] = part[0:8]
        after_ref[i, :, half : 2 * half] = part[8:16]


def exchange_halo(n, tokens, cotangent):
    channels = tokens.shape[2]
    half = channels // 2
    return pl.pallas_call(
        partial(halo_kernel, n),
        out_shape=[
            jax.ShapeDtypeStruct((3, 8, channels), F32),
            jax.ShapeDtypeStruct((4, 8, channels), F32),
        ],
        in_specs=[pl.BlockSpec(memory_space=pl.ANY)] * 2,
        out_specs=[pl.BlockSpec(memory_space=pltpu.VMEM)] * 2,
        scratch_shapes=[
            pltpu.VMEM((3, 16, channels), BF16),
            pltpu.VMEM((4, 16, channels), BF16),
            pltpu.VMEM((3, 16, half), BF16),
            pltpu.VMEM((4, 16, half), BF16),
            pltpu.VMEM((3, 16, half), BF16),
            pltpu.VMEM((4, 16, half), BF16),
            pltpu.SemaphoreType.DMA((3,)),
            pltpu.SemaphoreType.DMA((2,)),
            pltpu.SemaphoreType.DMA((2,)),
        ],
        compiler_params=pltpu.CompilerParams(
            collective_id=0, has_side_effects=True, vmem_limit_bytes=32 * 2**20
        ),
        name="halo",
    )(tokens, cotangent)


def local_kernel(
    tiles, proj_ref, cot_ref, before_ref, wide_ref, ends_ref, local_ref, feat_ref, near_ref,
    pad, parts, left, right, left_pair, right_pair,
):
    def one_tile(tile, carry):
        lanes = pl.ds(pl.multiple_of(tile * LANES, LANES), LANES)
        load_tokens(pad, proj_ref, before_ref, lanes)
        taps = tap_rows(wide_ref, lanes)
        step = 32
        for start in range(0, ROWS, step):
            rows = slice(start, start + step)
            f = [feature(pad, taps, i, start, step) for i in range(3)]
            for i in range(3):
                feat_ref[i, rows, lanes] = f[i]
            high, low = split(f[1] * f[2])
            right[rows, 0:LANES] = high
            right[ROWS + start : ROWS + start + step, 0:LANES] = high
            right[2 * ROWS + start : 2 * ROWS + start + step, 0:LANES] = low
            right_pair[rows, 0:LANES] = high
            right_pair[rows, LANES : 2 * LANES] = high
            right_pair[ROWS + start : ROWS + start + step, 0:LANES] = low
            right_pair[ROWS + start : ROWS + start + step, LANES : 2 * LANES] = low
            high, low = split(cot_ref[rows, lanes].astype(F32) * f[0])
            parts[rows, 0:LANES] = high
            parts[rows, LANES : 2 * LANES] = low
        flipped = dot(flip_matrix(), parts[...]).astype(BF16)
        right[0:ROWS, LANES : 2 * LANES] = flipped[:, 0:LANES]
        right[ROWS : 2 * ROWS, LANES : 2 * LANES] = flipped[:, 0:LANES]
        right[2 * ROWS : 3 * ROWS, LANES : 2 * LANES] = flipped[:, LANES : 2 * LANES]

        decay = wide_ref[DECAY : DECAY + MODES, lanes]
        residue = wide_ref[RESIDUE : RESIDUE + MODES, lanes]
        back = (LANES - 1 - iota((MODES, LANES), 1)).astype(F32)
        powers = []
        for g in range(TILE_GROUPS):
            column = GROUP * g
            power = jnp.exp(-decay[:, column : column + 1] * back)
            powers.append(power)
            filter_row = jnp.sum(residue[:, column : column + 1] * power, axis=0, keepdims=True)
            base = pltpu.roll(
                jnp.broadcast_to(filter_row, (8, LANES)), 1, 1, stride=1, stride_axis=0
            )
            for q in range(0, ROWS, 16):
                block = jnp.concatenate(
                    [pltpu.roll(base, q, 1) if q else base, pltpu.roll(base, q + 8, 1)], axis=0
                )
                keep = iota((16, LANES), 1) <= iota((16, LANES), 0) + q
                high, low = split(jnp.where(keep, block, 0.0))
                at = slice(ROWS * g + q, ROWS * g + q + 16)
                left[at, 0:LANES] = high
                left[at, LANES : 2 * LANES] = low
                left[at, 2 * LANES : 3 * LANES] = high
            for k, value in enumerate((power, back * power)):
                high, low = split(value)
                begin = TILE_GROUPS * (ROWS + k * MODES) + MODES * g
                at = slice(begin, begin + MODES)
                left[at, 0:LANES] = high
                left[at, LANES : 2 * LANES] = low
                left[at, 2 * LANES : 3 * LANES] = high
            left_pair[ROWS * g : ROWS * (g + 1), :] = jnp.where(
                in_group(ROWS, 2 * LANES, g), flipped, jnp.zeros_like(flipped)
            )
        product = dot(left[...], right[...])

        def gather(begin, count):
            total = product[begin : begin + count]
            for g in range(1, TILE_GROUPS):
                at = begin + g * count
                total = jnp.where(in_group(count, 2 * LANES, g), product[at : at + count], total)
            return total

        near = gather(0, ROWS)
        near_ref[0, :, lanes] = near[:, 0:LANES]
        near_ref[1, :, lanes] = near[:, LANES : 2 * LANES]
        ends = gather(TILE_GROUPS * ROWS, MODES)
        ends_ref[tile, 0:MODES, :] = ends[:, 0:LANES]
        ends_ref[tile, MODES : 2 * MODES, :] = ends[:, LANES : 2 * LANES]
        lags = gather(TILE_GROUPS * (ROWS + MODES), MODES)
        local_ref[tile, 0:MODES, :] = lags[:, 0:LANES]
        local_ref[tile, MODES : 2 * MODES, :] = lags[:, LANES : 2 * LANES]

        pairs = lax.dot_general(
            left_pair[...], right_pair[...], (((1,), (1,)), ((), ())), preferred_element_type=F32
        )
        res_sum = jnp.zeros((MODES, LANES), F32)
        lag_sum = jnp.zeros((MODES, LANES), F32)
        lane = iota((MODES, LANES), 1)
        for g in range(TILE_GROUPS):
            total = None
            for q in range(0, ROWS, 8):
                at = slice(ROWS * g + q, ROWS * g + q + 8)
                block = pairs[at, 0:LANES] + pairs[at, LANES : 2 * LANES]
                keep = iota((8, LANES), 1) + iota((8, LANES), 0) <= ROWS - 1 - q
                block = jnp.where(keep, block, 0.0)
                if q:
                    block = pltpu.roll(block, q, 1)
                total = block if total is None else total + block
            by_lag = jnp.sum(
                pltpu.roll(total, 0, 1, stride=1, stride_axis=0), axis=0, keepdims=True
            )
            weighted = powers[g] * by_lag
            res_sum = jnp.where(
                lane == GROUP * g, jnp.sum(weighted, axis=1, keepdims=True), res_sum
            )
            lag_sum = jnp.where(
                lane == GROUP * g, jnp.sum(back * weighted, axis=1, keepdims=True), lag_sum
            )
        local_ref[tile, 2 * MODES : 3 * MODES, :] = res_sum
        local_ref[tile, 3 * MODES : 4 * MODES, :] = lag_sum
        return carry

    lax.fori_loop(0, tiles, one_tile, 0)


def local_part(tokens, cotangent, before, wide, block):
    channels = tokens.shape[2]
    tiles = block // LANES
    count = channels // LANES
    return pl.pallas_call(
        partial(local_kernel, tiles),
        grid=(channels // block,),
        in_specs=[
            pl.BlockSpec((3, ROWS, block), lambda t: (0, 0, t)),
            pl.BlockSpec((ROWS, block), lambda t: (0, t)),
            pl.BlockSpec((3, 8, block), lambda t: (0, 0, t)),
            pl.BlockSpec((TABLE_ROWS, block), lambda t: (0, t)),
        ],
        out_specs=[
            pl.BlockSpec((tiles, 2 * MODES, LANES), lambda t: (t, 0, 0)),
            pl.BlockSpec((tiles, 4 * MODES, LANES), lambda t: (t, 0, 0)),
            pl.BlockSpec((3, ROWS, block), lambda t: (0, 0, t)),
            pl.BlockSpec((2, ROWS, block), lambda t: (0, 0, t)),
        ],
        out_shape=[
            jax.ShapeDtypeStruct((count, 2 * MODES, LANES), F32),
            jax.ShapeDtypeStruct((count, 4 * MODES, LANES), F32),
            jax.ShapeDtypeStruct((3, ROWS, channels), F32),
            jax.ShapeDtypeStruct((2, ROWS, channels), F32),
        ],
        scratch_shapes=[
            pltpu.VMEM((3, ROWS + 8, LANES), F32),
            pltpu.VMEM((ROWS, 2 * LANES), BF16),
            pltpu.VMEM((TILE_GROUPS * (ROWS + 2 * MODES), 3 * LANES), BF16),
            pltpu.VMEM((3 * ROWS, 2 * LANES), BF16),
            pltpu.VMEM((TILE_GROUPS * ROWS, 2 * LANES), BF16),
            pltpu.VMEM((2 * ROWS, 2 * LANES), BF16),
        ],
        compiler_params=pltpu.CompilerParams(vmem_limit_bytes=48 * 2**20),
        name="local",
    )(tokens, cotangent, before, wide)


def state_kernel(n, ends_ref, decay_ref, into_ref, cross_ref, got, back, s_out, r_out, s_in, r_in):
    me = lax.axis_index("ctx")

    def peer_of(k):
        return lax.rem(me + k, n)

    barrier = pltpu.get_barrier_semaphore()

    def greet(k, carry):
        pl.semaphore_signal(barrier, inc=1, device_id={"ctx": peer_of(k)}, device_id_type=MESH)
        return carry

    lax.fori_loop(1, n, greet, 0)
    got[me] = ends_ref[me]
    decay = decay_ref[me]
    pl.semaphore_wait(barrier, n - 1)

    def send_out(k):
        return pltpu.make_async_remote_copy(
            src_ref=ends_ref.at[peer_of(k)],
            dst_ref=got.at[me],
            send_sem=s_out.at[k],
            recv_sem=r_out.at[me],
            device_id={"ctx": peer_of(k)},
            device_id_type=MESH,
        )

    def receive_out(k):
        source = lax.rem(me + n - k, n)
        return pltpu.make_async_remote_copy(
            src_ref=ends_ref.at[source],
            dst_ref=got.at[source],
            send_sem=s_out.at[k],
            recv_sem=r_out.at[source],
            device_id={"ctx": source},
            device_id_type=MESH,
        )

    def send_in(k):
        return pltpu.make_async_remote_copy(
            src_ref=back.at[peer_of(k)],
            dst_ref=into_ref.at[me],
            send_sem=s_in.at[k],
            recv_sem=r_in.at[me],
            device_id={"ctx": peer_of(k)},
            device_id_type=MESH,
        )

    def receive_in(k):
        source = lax.rem(me + n - k, n)
        return pltpu.make_async_remote_copy(
            src_ref=back.at[source],
            dst_ref=into_ref.at[source],
            send_sem=s_in.at[k],
            recv_sem=r_in.at[source],
            device_id={"ctx": source},
            device_id_type=MESH,
        )

    def each(action):
        def run(k, carry):
            action(k)
            return carry

        lax.fori_loop(1, n, run, 0)

    each(lambda k: send_out(k).start())
    each(lambda k: receive_out(k).wait_recv())
    pole = jnp.exp(-decay)
    whole = jnp.exp(-decay * float(ROWS))
    zero = jnp.zeros((MODES, LANES), F32)

    def forward(d, carry):
        state, lagged, res, lag = carry
        adjoint = got[d, MODES : 2 * MODES, :]
        back[d, 0:MODES, :] = state
        res = res + adjoint * state
        lag = lag + adjoint * (state + float(ROWS) * lagged)
        return whole * state + got[d, 0:MODES, :], whole * (lagged + state), res, lag

    _, _, res, lag = lax.fori_loop(0, n, forward, (zero, zero, zero, zero))
    cross_ref[0] = pole * res
    cross_ref[1] = pole * lag

    def backward(k, state):
        d = n - 1 - k
        back[d, MODES : 2 * MODES, :] = state
        return whole * state + got[d, MODES : 2 * MODES, :]

    lax.fori_loop(0, n, backward, zero)
    each(lambda k: send_in(k).start())
    into_ref[me] = back[me]
    each(lambda k: receive_in(k).wait_recv())
    each(lambda k: send_out(k).wait_send())
    each(lambda k: send_in(k).wait_send())


def exchange_states(n, ends, decay_tiles):
    vmem = pl.BlockSpec(memory_space=pltpu.VMEM)
    return pl.pallas_call(
        partial(state_kernel, n),
        out_shape=[
            jax.ShapeDtypeStruct((n, 2 * MODES, LANES), F32),
            jax.ShapeDtypeStruct((2, MODES, LANES), F32),
        ],
        in_specs=[vmem, vmem],
        out_specs=[vmem, vmem],
        scratch_shapes=[
            pltpu.VMEM((n, 2 * MODES, LANES), F32),
            pltpu.VMEM((n, 2 * MODES, LANES), F32),
        ]
        + [pltpu.SemaphoreType.DMA((n,))] * 4,
        compiler_params=pltpu.CompilerParams(
            collective_id=1, has_side_effects=True, vmem_limit_bytes=16 * 2**20
        ),
        name="states",
    )(ends, decay_tiles)


def finish_kernel(
    tiles, me_ref, proj_ref, cot_ref, before_ref, after_ref, wide_ref, ends_ref, local_ref,
    feat_ref, near_ref, into_ref, cross_ref, gated_ref, grad_ref, sums_ref,
    pad, grads, left, right, flip_parts,
):
    step_index = pl.program_id(0)

    def one_tile(tile, carry):
        lanes = pl.ds(pl.multiple_of(tile * LANES, LANES), LANES)
        load_tokens(pad, proj_ref, before_ref, lanes)
        for i in range(3):
            pad[i, 8 + ROWS : 16 + ROWS, :] = after_ref[i, :, lanes]
        taps = tap_rows(wide_ref, lanes)
        decay = wide_ref[DECAY : DECAY + MODES, lanes]
        residue = wide_ref[RESIDUE : RESIDUE + MODES, lanes]
        decay_row = wide_ref[DECAY_GM : DECAY_GM + 1, lanes]
        residue_row = wide_ref[RESIDUE_GM : RESIDUE_GM + 1, lanes]

        ahead = (iota((ROWS, LANES), 0) + 1).astype(F32)
        high, low = split(residue_row * jnp.exp(-decay_row * ahead))
        left[:, 0:LANES] = high
        left[:, LANES : 2 * LANES] = low
        left[:, 2 * LANES : 3 * LANES] = high
        state = into_ref[tile, 0:MODES, :]
        adjoint = into_ref[tile, MODES : 2 * MODES, :]
        high, low = split(jnp.concatenate([state, adjoint], axis=1))
        for g in range(TILE_GROUPS):
            keep = in_group(MODES, 2 * LANES, g)
            chosen = jnp.where(keep, high, jnp.zeros_like(high))
            right[MODES * g : MODES * (g + 1), :] = chosen
            right[ROWS + MODES * g : ROWS + MODES * (g + 1), :] = chosen
            right[2 * ROWS + MODES * g : 2 * ROWS + MODES * (g + 1), :] = jnp.where(
                keep, low, jnp.zeros_like(low)
            )
        far = dot(left[...], right[...])
        long_conv = near_ref[0, :, lanes] + far[:, 0:LANES]
        high, low = split(near_ref[1, :, lanes] + far[:, LANES : 2 * LANES])
        flip_parts[0:ROWS, :] = high
        flip_parts[ROWS : 2 * ROWS, :] = low
        flip = flip_matrix()
        mixer_grad = dot(jnp.concatenate([flip, flip], axis=1), flip_parts[...])

        gated_ref[:, lanes] = (feat_ref[0, :, lanes] * long_conv).astype(BF16)
        grads[0, 0:ROWS, :] = cot_ref[:, lanes].astype(F32) * long_conv
        grads[1, 0:ROWS, :] = mixer_grad * feat_ref[2, :, lanes]
        grads[2, 0:ROWS, :] = mixer_grad * feat_ref[1, :, lanes]

        pole = jnp.exp(-decay)
        inverse = jnp.exp(decay)
        next_feat = [feature(pad, taps, i, ROWS, 8) for i in range(3)]
        next_cot = after_ref[3, :, lanes]
        next_in = next_feat[1] * next_feat[2]
        next_grad = next_cot * next_feat[0]
        whole = jnp.exp(-decay * float(ROWS))
        behind = residue * pole * (whole * state + ends_ref[tile, 0:MODES, :])
        beyond = residue * adjoint
        lag_pos = residue
        lag_neg = residue * inverse
        conv_rows, mixer_rows, filters, filters_neg = [], [], [], []
        for k in range(TAPS - 1):
            filters.append(jnp.sum(lag_pos, axis=0, keepdims=True))
            filters_neg.append(jnp.sum(lag_neg, axis=0, keepdims=True))
            conv = jnp.sum(behind, axis=0, keepdims=True)
            mixer = jnp.sum(beyond, axis=0, keepdims=True)
            for j in range(k + 1):
                conv = conv + filters[k - j] * next_in[j : j + 1]
            for j in range(k):
                mixer = mixer - filters_neg[k - j - 1] * next_grad[j : j + 1]
            conv_rows.append(conv)
            mixer_rows.append(mixer)
            lag_pos, lag_neg = lag_pos * pole, lag_neg * inverse
            behind, beyond = behind * pole, beyond * inverse
        blank = jnp.zeros((8 - (TAPS - 1), LANES), F32)
        next_conv = jnp.concatenate(conv_rows + [blank], axis=0)
        next_mixer = jnp.concatenate(mixer_rows + [blank], axis=0)
        grads[0, ROWS : ROWS + 8, :] = next_cot * next_conv
        grads[1, ROWS : ROWS + 8, :] = next_mixer * next_feat[2]
        grads[2, ROWS : ROWS + 8, :] = next_mixer * next_feat[1]

        step = 32
        short = []
        for i in range(3):
            sums = [None] * TAPS
            for start in range(0, ROWS, step):
                rows = slice(start, start + step)
                own = grads[i, rows, :]
                total = None
                for j in range(TAPS):
                    ahead_grad = grads[i, start + j : start + j + step, :]
                    term = taps[TAPS * i + j] * ahead_grad
                    total = term if total is None else total + term
                    product = own * pad[i, 8 + start - j : 8 + start - j + step, :]
                    part = product[0:8]
                    for r in range(8, step, 8):
                        part = part + product[r : r + 8]
                    sums[j] = part if sums[j] is None else sums[j] + part
                grad_ref[i, rows, lanes] = total.astype(BF16)
            short += [jnp.sum(part, axis=0, keepdims=True) for part in sums]
        short.append(jnp.zeros((3, LANES), F32))

        mine = step_index * tiles + tile == me_ref[0]
        res_sum = local_ref[tile, 2 * MODES : 3 * MODES, :]
        lag_sum = local_ref[tile, 3 * MODES : 4 * MODES, :]
        lag_sum = lag_sum + pole * (
            local_ref[tile, MODES : 2 * MODES, :] * state + local_ref[tile, 0:MODES, :] * adjoint
        )
        res_sum = res_sum + jnp.where(mine, cross_ref[0], 0.0)
        lag_sum = lag_sum + jnp.where(mine, cross_ref[1], 0.0)
        high, low = split(jnp.concatenate(short + [res_sum, lag_sum], axis=0))
        member = (iota((2 * LANES, LANES), 0) % LANES) // GROUP == iota((2 * LANES, LANES), 1)
        by_group = dot(
            jnp.concatenate([high, low], axis=1), member.astype(F32).astype(BF16)
        )
        packed = by_group[0:8]
        for r in range(8, TABLE_ROWS, 8):
            packed = packed + pltpu.roll(by_group[r : r + 8], r, 1)
        sums_ref[tile] = packed
        return carry

    lax.fori_loop(0, tiles, one_tile, 0)


def finish(me, tokens, cotangent, before, after, wide, ends, local, feats, near, into, cross, block):
    channels = tokens.shape[2]
    tiles = block // LANES
    count = channels // LANES

    def per_tile(rows):
        return pl.BlockSpec((tiles, rows, LANES), lambda t: (t, 0, 0))

    def stack(k, rows):
        return pl.BlockSpec((k, rows, block), lambda t: (0, 0, t))

    plane = pl.BlockSpec((ROWS, block), lambda t: (0, t))
    return pl.pallas_call(
        partial(finish_kernel, tiles),
        grid=(channels // block,),
        in_specs=[
            pl.BlockSpec(memory_space=pltpu.SMEM),
            stack(3, ROWS),
            plane,
            stack(3, 8),
            stack(4, 8),
            pl.BlockSpec((TABLE_ROWS, block), lambda t: (0, t)),
            per_tile(2 * MODES),
            per_tile(4 * MODES),
            stack(3, ROWS),
            stack(2, ROWS),
            per_tile(2 * MODES),
            pl.BlockSpec((2, MODES, LANES), lambda t: (0, 0, 0)),
        ],
        out_specs=[plane, stack(3, ROWS), per_tile(8)],
        out_shape=[
            jax.ShapeDtypeStruct((ROWS, channels), BF16),
            jax.ShapeDtypeStruct((3, ROWS, channels), BF16),
            jax.ShapeDtypeStruct((count, 8, LANES), F32),
        ],
        scratch_shapes=[
            pltpu.VMEM((3, ROWS + 16, LANES), F32),
            pltpu.VMEM((3, ROWS + 8, LANES), F32),
            pltpu.VMEM((ROWS, 3 * LANES), BF16),
            pltpu.VMEM((3 * ROWS, 2 * LANES), BF16),
            pltpu.VMEM((2 * ROWS, LANES), BF16),
        ],
        compiler_params=pltpu.CompilerParams(vmem_limit_bytes=48 * 2**20),
        name="finish",
    )(me, tokens, cotangent, before, after, wide, ends, local, feats, near, into, cross)


def total_kernel(n, m, part_ref, out_ref, got, rows, s_a, r_a, s_b, r_b, s_c, r_c):
    me, mine = lax.axis_index("ctx"), lax.axis_index("seq")
    barrier = pltpu.get_barrier_semaphore()

    def each(count, action):
        def run(k, carry):
            action(k)
            return carry

        lax.fori_loop(1, count, run, 0)

    def copy(axis, source, target, send_sem, recv_sem, to):
        return pltpu.make_async_remote_copy(
            src_ref=source,
            dst_ref=target,
            send_sem=send_sem,
            recv_sem=recv_sem,
            device_id={axis: to},
            device_id_type=MESH,
        )

    def to_ctx(k):
        return lax.rem(me + k, n)

    def from_ctx(k):
        return lax.rem(me + n - k, n)

    def to_seq(k):
        return lax.rem(mine + k, m)

    def from_seq(k):
        return lax.rem(mine + m - k, m)

    def greet(axis, to):
        pl.semaphore_signal(barrier, inc=1, device_id={axis: to}, device_id_type=MESH)

    each(n, lambda k: greet("ctx", to_ctx(k)))
    each(m, lambda k: greet("seq", to_seq(k)))
    got[me] = part_ref[me]
    pl.semaphore_wait(barrier, n - 1 + m - 1)

    def first(k, to, slot):
        return copy("ctx", part_ref.at[to], got.at[slot], s_a.at[k], r_a.at[slot], to)

    each(n, lambda k: first(k, to_ctx(k), me).start())
    each(n, lambda k: first(k, from_ctx(k), from_ctx(k)).wait_recv())
    total = got[0]
    for d in range(1, n):
        total = total + got[d]
    rows[mine] = total

    def second(k, to, slot):
        return copy("seq", rows.at[mine], rows.at[slot], s_b.at[k], r_b.at[slot], to)

    each(m, lambda k: second(k, to_seq(k), mine).start())
    each(m, lambda k: second(k, from_seq(k), from_seq(k)).wait_recv())
    total = rows[0]
    for d in range(1, m):
        total = total + rows[d]
    out_ref[me] = total

    def third(k, to, slot):
        return copy("ctx", out_ref.at[me], out_ref.at[slot], s_c.at[k], r_c.at[slot], to)

    each(n, lambda k: third(k, to_ctx(k), me).start())
    each(n, lambda k: third(k, from_ctx(k), from_ctx(k)).wait_recv())
    each(n, lambda k: first(k, to_ctx(k), me).wait_send())
    each(m, lambda k: second(k, to_seq(k), mine).wait_send())
    each(n, lambda k: third(k, to_ctx(k), me).wait_send())


def total_sums(n, m, parts):
    vmem = pl.BlockSpec(memory_space=pltpu.VMEM)
    return pl.pallas_call(
        partial(total_kernel, n, m),
        out_shape=jax.ShapeDtypeStruct((n, 8, LANES), F32),
        in_specs=[vmem],
        out_specs=vmem,
        scratch_shapes=[pltpu.VMEM((n, 8, LANES), F32), pltpu.VMEM((m, 8, LANES), F32)]
        + [pltpu.SemaphoreType.DMA((n,))] * 2
        + [pltpu.SemaphoreType.DMA((m,))] * 2
        + [pltpu.SemaphoreType.DMA((n,))] * 2,
        compiler_params=pltpu.CompilerParams(
            collective_id=2, has_side_effects=True, vmem_limit_bytes=16 * 2**20
        ),
        name="totals",
    )(parts)


def per_device(projected, cotangent, short_filter, residue, decay_rate):
    n, m = lax.axis_size("ctx"), lax.axis_size("seq")
    tokens, upstream = projected[0], cotangent[0]
    channels = tokens.shape[2]
    groups = residue.shape[1]
    block = min(channels, 512)
    by_group = jnp.concatenate([decay_rate, residue, short_filter.reshape(3 * TAPS, groups)])
    wide = jnp.concatenate(
        [
            jnp.repeat(by_group, GROUP, axis=1),
            decay_rate.T.reshape(1, channels),
            residue.T.reshape(1, channels),
            jnp.zeros((1, channels), F32),
        ]
    )
    decay_tiles = wide[0:MODES].reshape(MODES, n, LANES).transpose(1, 0, 2)
    me = lax.axis_index("ctx").astype(jnp.int32).reshape(1)

    before, after = exchange_halo(n, tokens, upstream)
    ends, local, feats, near = local_part(tokens, upstream, before, wide, block)
    into, cross = exchange_states(n, ends, decay_tiles)
    gated, grad_tokens, sums = finish(
        me, tokens, upstream, before, after, wide, ends, local, feats, near, into, cross, block
    )
    sums = total_sums(n, m, sums)
    blocks = TABLE_ROWS // 8
    sums = sums[:, :, 0 : blocks * TILE_GROUPS].reshape(n, 8, blocks, TILE_GROUPS)
    sums = sums.transpose(2, 1, 0, 3).reshape(TABLE_ROWS, groups)
    sums = sums / float(ROWS * n * m)
    grad_short = sums[0 : 3 * TAPS].reshape(3, TAPS, groups)
    grad_residue = sums[24 : 24 + MODES]
    grad_log_decay = -residue * decay_rate * sums[40 : 40 + MODES]
    return gated[None], grad_tokens[None], grad_short, grad_residue, grad_log_decay


def solution(mesh):
    placed = (P("seq", None, "ctx", None), P("seq", "ctx", None), P(), P(), P())
    return jax.shard_map(
        per_device,
        mesh=mesh,
        in_specs=placed,
        out_specs=(P("seq", "ctx", None), P("seq", None, "ctx", None), P(), P(), P()),
        check_vma=False,
    )
```

```python
from functools import partial

import jax
import jax.numpy as jnp
from jax import lax
from jax.experimental import pallas as pl
from jax.experimental.pallas import tpu as pltpu
from jax.sharding import PartitionSpec as P

GROUP = 16
MODES = 16
TAPS = 7
LANES = 128
TILE_GROUPS = LANES // GROUP
ROWS = 128
F32, BF16 = jnp.float32, jnp.bfloat16
MESH = pl.DeviceIdType.MESH

HALF = ROWS // 2
WAYS = 2

DECAY, RESIDUE, SHORT, TABLE_ROWS = 0, 16, 32, 56


def split(value):
    high = value.astype(BF16)
    return high, (value - high.astype(F32)).astype(BF16)


def iota(shape, dim):
    return lax.broadcasted_iota(jnp.int32, shape, dim)


def dot(left, right):
    return jnp.dot(left, right, preferred_element_type=F32)


def in_group(rows, width, group):
    return (iota((rows, width), 1) % LANES) // GROUP == group


def flip_matrix():
    return (iota((ROWS, ROWS), 0) + iota((ROWS, ROWS), 1) == ROWS - 1).astype(BF16)


def load_tokens(pad, proj_ref, before_ref, lanes):
    for i in range(3):
        pad[i, 0:8, :] = before_ref[i, :, lanes]
        pad[i, 8 : 8 + ROWS, :] = proj_ref[i, :, lanes].astype(F32)


def feature(pad, taps, i, start, count):
    total = None
    for j in range(TAPS):
        term = taps[TAPS * i + j] * pad[i, 8 + start - j : 8 + start - j + count, :]
        total = term if total is None else total + term
    return total


def tap_rows(wide_ref, lanes):
    return [wide_ref[SHORT + k : SHORT + k + 1, lanes] for k in range(3 * TAPS)]


def expand_table(wide_ref, small, decay_ref, residue_ref, short_ref):
    small[DECAY : DECAY + MODES, :] = decay_ref[...]
    small[RESIDUE : RESIDUE + MODES, :] = residue_ref[...]
    for i in range(3):
        small[SHORT + TAPS * i : SHORT + TAPS * (i + 1), :] = short_ref[i]
    used = SHORT + 3 * TAPS
    groups = small.shape[1]
    small[used:TABLE_ROWS, :] = jnp.zeros((TABLE_ROWS - used, groups), F32)
    value = small[...]
    high = value.astype(BF16).astype(F32)
    middle = (value - high).astype(BF16).astype(F32)
    low = value - high - middle
    pieces = jnp.concatenate([high, middle, low], axis=0).astype(BF16)
    width = min(1024, wide_ref.shape[1])
    for start in range(0, wide_ref.shape[1], width):
        owner = (iota((groups, width), 1) + start) // GROUP
        spread = (iota((groups, width), 0) == owner).astype(F32).astype(BF16)
        got = dot(pieces, spread)
        wide_ref[:, start : start + width] = got[0:TABLE_ROWS] + (
            got[TABLE_ROWS : 2 * TABLE_ROWS] + got[2 * TABLE_ROWS :]
        )


def lanes_of(tile):
    return pl.ds(pl.multiple_of(tile * LANES, LANES), LANES)


def select_groups(source, begin, count, rows, columns):
    total = source[begin + rows.start : begin + rows.stop, columns]
    for g in range(1, TILE_GROUPS):
        at = begin + g * count
        total = jnp.where(
            in_group(rows.stop - rows.start, columns.stop - columns.start, g),
            source[at + rows.start : at + rows.stop, columns],
            total,
        )
    return total


def local_kernel(
    n, proj_ref, cot_ref, decay_ref, residue_ref, short_ref,
    wide_ref, before_ref, after_ref, ends_ref, local_ref, near_ref, into_ref,
    small, out_f, out_b, got_f, got_b, got, back, tables, rights, pad, parts, *scratch,
):
    products, left_pairs, right_pairs, pair_sums = (
        scratch[k * WAYS : (k + 1) * WAYS] for k in range(4)
    )
    halo_send, halo_recv, s_out, r_out, s_in, r_in = scratch[4 * WAYS :]
    me = lax.axis_index("ctx")
    right_dev, left_dev = lax.rem(me + 1, n), lax.rem(me + n - 1, n)
    far_back = (LANES - 1 - iota((MODES, LANES), 1)).astype(F32)

    def peer_of(k):
        return lax.rem(me + k, n)

    def each(action):
        def run(k, carry):
            action(k)
            return carry

        lax.fori_loop(1, n, run, 0)

    def remote(source, target, send_sem, recv_sem, to):
        return pltpu.make_async_remote_copy(
            src_ref=source,
            dst_ref=target,
            send_sem=send_sem,
            recv_sem=recv_sem,
            device_id={"ctx": to},
            device_id_type=MESH,
        )

    barrier = pltpu.get_barrier_semaphore()
    each(
        lambda k: pl.semaphore_signal(
            barrier, inc=1, device_id={"ctx": peer_of(k)}, device_id_type=MESH
        )
    )
    width = out_f.shape[2]
    for i in range(3):
        tail = proj_ref[i, ROWS - 16 : ROWS, :].astype(F32)[8:16]
        out_f[i] = jnp.concatenate([tail[:, :width], tail[:, width:]], axis=0).astype(BF16)
    for i in range(4):
        head = (cot_ref[0:16, :] if i == 3 else proj_ref[i, 0:16, :]).astype(F32)[0:8]
        out_b[i] = jnp.concatenate([head[:, :width], head[:, width:]], axis=0).astype(BF16)
    expand_table(wide_ref, small, decay_ref, residue_ref, short_ref)
    pl.semaphore_wait(barrier, n - 1)
    halo = [
        remote(out_f, got_f, halo_send.at[0], halo_recv.at[0], right_dev),
        remote(out_b, got_b, halo_send.at[1], halo_recv.at[1], left_dev),
    ]
    for copy in halo:
        copy.start()

    def power_of(tile, g):
        column = GROUP * g
        decay = wide_ref[DECAY : DECAY + MODES, lanes_of(tile)]
        return jnp.exp(-decay[:, column : column + 1] * far_back)

    def store_table(tile, at, value):
        high, low = split(value)
        tables[tile, at, 0:LANES] = high
        tables[tile, at, LANES : 2 * LANES] = low
        tables[tile, at, 2 * LANES : 3 * LANES] = high

    def build_tables(tile, carry):
        residue = wide_ref[RESIDUE : RESIDUE + MODES, lanes_of(tile)]
        for g in range(TILE_GROUPS):
            column = GROUP * g
            power = power_of(tile, g)
            filter_row = jnp.sum(residue[:, column : column + 1] * power, axis=0, keepdims=True)
            base = pltpu.roll(
                jnp.broadcast_to(filter_row, (8, LANES)), 1, 1, stride=1, stride_axis=0
            )
            for q in range(HALF, ROWS, 16):
                block = jnp.concatenate(
                    [pltpu.roll(base, q, 1), pltpu.roll(base, q + 8, 1)], axis=0
                )
                keep = iota((16, LANES), 1) <= iota((16, LANES), 0) + q
                begin = HALF * g + q - HALF
                store_table(tile, slice(begin, begin + 16), jnp.where(keep, block, 0.0))
            for k, value in enumerate((power, far_back * power)):
                begin = TILE_GROUPS * (HALF + k * MODES) + MODES * g
                store_table(tile, slice(begin, begin + MODES), value)
        return carry

    lax.fori_loop(0, n, build_tables, 0)

    for copy in halo:
        copy.wait()
    first, last = me == 0, me == n - 1
    for i in range(3):
        part = jnp.where(first, 0.0, got_f[i].astype(F32))
        before_ref[i, :, 0:width] = part[0:8]
        before_ref[i, :, width : 2 * width] = part[8:16]
    for i in range(4):
        part = jnp.where(last, 0.0, got_b[i].astype(F32))
        after_ref[i, :, 0:width] = part[0:8]
        after_ref[i, :, width : 2 * width] = part[8:16]

    def features(tile, way):
        lanes = lanes_of(tile)
        load_tokens(pad, proj_ref, before_ref, lanes)
        taps = tap_rows(wide_ref, lanes)
        step = 32
        for start in range(0, ROWS, step):
            rows = slice(start, start + step)
            f = [feature(pad, taps, i, start, step) for i in range(3)]
            high, low = split(f[1] * f[2])
            for k, value in enumerate((high, high, low)):
                begin = ROWS * k + start
                rights[tile, begin : begin + step, 0:LANES] = value
                if start < HALF:
                    begin = begin + HALF
                    rights[tile, begin : begin + step, 2 * LANES : 3 * LANES] = value
            high, low = split(cot_ref[rows, lanes].astype(F32) * f[0])
            begin = 2 * LANES * way
            parts[rows, begin : begin + LANES] = high
            parts[rows, begin + LANES : begin + 2 * LANES] = low

    def place(tile, flipped):
        blank = jnp.zeros((HALF, 2 * LANES), BF16)
        for k, column in enumerate((0, 0, LANES)):
            value = flipped[:, column : column + LANES]
            begin = ROWS * k
            rights[tile, begin : begin + ROWS, LANES : 2 * LANES] = value
            rights[tile, begin : begin + HALF, 2 * LANES : 4 * LANES] = blank
            rights[tile, begin + HALF : begin + ROWS, 3 * LANES : 4 * LANES] = value[0:HALF]

    modes, both = slice(0, MODES), slice(0, 2 * LANES)

    def send_out(k):
        return remote(
            ends_ref.at[peer_of(k)], got.at[me], s_out.at[k], r_out.at[me], peer_of(k)
        )

    group = 4 if n % 4 == 0 else 2

    def begin_tiles(step, carry):
        ks = [step * group + way for way in range(group)]
        for way, k in enumerate(ks):
            features(peer_of(k), way)
        flipped = dot(flip_matrix(), parts[:, 0 : 2 * LANES * group]).astype(BF16)
        for way, k in enumerate(ks):
            place(peer_of(k), flipped[:, 2 * LANES * way : 2 * LANES * (way + 1)])
        states = [
            dot(tables[peer_of(k), TILE_GROUPS * HALF :, :], rights[peer_of(k), :, both])
            for k in ks
        ]
        for k, state in zip(ks, states):
            tile = peer_of(k)
            ends = select_groups(state, 0, MODES, modes, both)
            ends_ref[tile, 0:MODES, :] = ends[:, 0:LANES]
            ends_ref[tile, MODES : 2 * MODES, :] = ends[:, LANES : 2 * LANES]
            lags = select_groups(state, TILE_GROUPS * MODES, MODES, modes, both)
            local_ref[tile, 0:MODES, :] = lags[:, 0:LANES]
            local_ref[tile, MODES : 2 * MODES, :] = lags[:, LANES : 2 * LANES]
        for k in ks:

            @pl.when(k != 0)
            def _():
                send_out(k).start()

        return carry

    lax.fori_loop(0, n // group, begin_tiles, 0)

    def convolve(step, carry):
        tiles = [step * WAYS + way for way in range(WAYS)]
        for way, tile in enumerate(tiles):
            products[way][...] = dot(tables[tile, 0 : TILE_GROUPS * HALF, :], rights[tile])
        for way, tile in enumerate(tiles):
            for start in range(0, ROWS, 32):
                source = start % HALF
                columns = slice(0, 2 * LANES) if start >= HALF else slice(2 * LANES, 4 * LANES)
                near = select_groups(
                    products[way], 0, HALF, slice(source, source + 32), columns
                )
                near_ref[0, start : start + 32, lanes_of(tile)] = near[:, 0:LANES]
                near_ref[1, start : start + 32, lanes_of(tile)] = near[:, LANES : 2 * LANES]
        return carry

    lax.fori_loop(0, n // WAYS, convolve, 0)

    def receive_out(k):
        source = lax.rem(me + n - k, n)
        return remote(ends_ref.at[source], got.at[source], s_out.at[k], r_out.at[source], source)

    def send_in(k):
        return remote(back.at[peer_of(k)], into_ref.at[me], s_in.at[k], r_in.at[me], peer_of(k))

    def receive_in(k):
        source = lax.rem(me + n - k, n)
        return remote(back.at[source], into_ref.at[source], s_in.at[k], r_in.at[source], source)

    got[me] = ends_ref[me]
    each(lambda k: receive_out(k).wait_recv())
    decay = wide_ref[DECAY : DECAY + MODES, lanes_of(me)]
    pole = jnp.exp(-decay)
    whole = jnp.exp(-decay * float(ROWS))
    zero = jnp.zeros((MODES, LANES), F32)

    def scan(step, carry):
        state, lagged, res, lag, beyond = carry
        for k in range(2):
            d = step * 2 + k
            adjoint = got[d, MODES : 2 * MODES, :]
            back[d, 0:MODES, :] = state
            res = res + adjoint * state
            lag = lag + adjoint * (state + float(ROWS) * lagged)
            state, lagged = whole * state + got[d, 0:MODES, :], whole * (lagged + state)
            d = n - 1 - d
            back[d, MODES : 2 * MODES, :] = beyond
            beyond = whole * beyond + got[d, MODES : 2 * MODES, :]
        return state, lagged, res, lag, beyond

    _, _, cross_res, cross_lag, _ = lax.fori_loop(0, n // 2, scan, (zero,) * 5)
    each(lambda k: send_in(k).start())
    into_ref[me] = back[me]

    lane = iota((MODES, LANES), 1)

    def correlate(step, carry):
        tiles = [step * WAYS + way for way in range(WAYS)]
        for way, tile in enumerate(tiles):
            flipped = jnp.concatenate(
                [
                    rights[tile, 0:ROWS, LANES : 2 * LANES],
                    rights[tile, 2 * ROWS : 3 * ROWS, LANES : 2 * LANES],
                ],
                axis=1,
            )
            for g in range(TILE_GROUPS):
                left_pairs[way][ROWS * g : ROWS * (g + 1), :] = jnp.where(
                    in_group(ROWS, 2 * LANES, g), flipped, jnp.zeros_like(flipped)
                )
            for k in range(2):
                value = rights[tile, 2 * ROWS * k : 2 * ROWS * k + ROWS, 0:LANES]
                right_pairs[way][ROWS * k : ROWS * (k + 1), 0:LANES] = value
                right_pairs[way][ROWS * k : ROWS * (k + 1), LANES : 2 * LANES] = value
        for way in range(WAYS):
            pair_sums[way][...] = lax.dot_general(
                left_pairs[way][...],
                right_pairs[way][...],
                (((1,), (1,)), ((), ())),
                preferred_element_type=F32,
            )
        for way, tile in enumerate(tiles):
            res_sum = jnp.zeros((MODES, LANES), F32)
            lag_sum = jnp.zeros((MODES, LANES), F32)
            for g in range(TILE_GROUPS):
                total = None
                for q in range(0, ROWS, 8):
                    at = slice(ROWS * g + q, ROWS * g + q + 8)
                    block = pair_sums[way][at, 0:LANES] + pair_sums[way][at, LANES : 2 * LANES]
                    keep = iota((8, LANES), 1) + iota((8, LANES), 0) <= ROWS - 1 - q
                    block = jnp.where(keep, block, 0.0)
                    if q:
                        block = pltpu.roll(block, q, 1)
                    total = block if total is None else total + block
                by_lag = jnp.sum(
                    pltpu.roll(total, 0, 1, stride=1, stride_axis=0), axis=0, keepdims=True
                )
                weighted = power_of(tile, g) * by_lag
                res_sum = jnp.where(
                    lane == GROUP * g, jnp.sum(weighted, axis=1, keepdims=True), res_sum
                )
                lag_sum = jnp.where(
                    lane == GROUP * g,
                    jnp.sum(far_back * weighted, axis=1, keepdims=True),
                    lag_sum,
                )
            local_ref[tile, 2 * MODES : 3 * MODES, :] = res_sum
            local_ref[tile, 3 * MODES : 4 * MODES, :] = lag_sum
        return carry

    lax.fori_loop(0, n // WAYS, correlate, 0)
    local_ref[me, 2 * MODES : 3 * MODES, :] = (
        local_ref[me, 2 * MODES : 3 * MODES, :] + pole * cross_res
    )
    local_ref[me, 3 * MODES : 4 * MODES, :] = (
        local_ref[me, 3 * MODES : 4 * MODES, :] + pole * cross_lag
    )
    each(lambda k: receive_in(k).wait_recv())
    each(lambda k: send_out(k).wait_send())
    each(lambda k: send_in(k).wait_send())


def local_part(n, tokens, cotangent, decay_rate, residue, short_filter):
    channels = tokens.shape[2]
    groups = residue.shape[1]
    half = channels // 2
    vmem = pl.BlockSpec(memory_space=pltpu.VMEM)
    wide_rows = TILE_GROUPS * (HALF + 2 * MODES)
    return pl.pallas_call(
        partial(local_kernel, n),
        in_specs=[vmem] * 5,
        out_specs=[vmem] * 7,
        out_shape=[
            jax.ShapeDtypeStruct(shape, F32)
            for shape in (
                (TABLE_ROWS, channels),
                (3, 8, channels),
                (4, 8, channels),
                (n, 2 * MODES, LANES),
                (n, 4 * MODES, LANES),
                (2, ROWS, channels),
                (n, 2 * MODES, LANES),
            )
        ],
        scratch_shapes=[
            pltpu.VMEM((TABLE_ROWS, groups), F32),
            pltpu.VMEM((3, 16, half), BF16),
            pltpu.VMEM((4, 16, half), BF16),
            pltpu.VMEM((3, 16, half), BF16),
            pltpu.VMEM((4, 16, half), BF16),
            pltpu.VMEM((n, 2 * MODES, LANES), F32),
            pltpu.VMEM((n, 2 * MODES, LANES), F32),
            pltpu.VMEM((n, wide_rows, 3 * LANES), BF16),
            pltpu.VMEM((n, 3 * ROWS, 4 * LANES), BF16),
            pltpu.VMEM((3, ROWS + 8, LANES), F32),
            pltpu.VMEM((ROWS, 2 * LANES * 4), BF16),
        ]
        + [pltpu.VMEM((TILE_GROUPS * HALF, 4 * LANES), F32)] * WAYS
        + [pltpu.VMEM((TILE_GROUPS * ROWS, 2 * LANES), BF16)] * WAYS
        + [pltpu.VMEM((2 * ROWS, 2 * LANES), BF16)] * WAYS
        + [pltpu.VMEM((TILE_GROUPS * ROWS, 2 * LANES), F32)] * WAYS
        + [pltpu.SemaphoreType.DMA((2,))] * 2
        + [pltpu.SemaphoreType.DMA((n,))] * 4,
        compiler_params=pltpu.CompilerParams(
            collective_id=0, has_side_effects=True, vmem_limit_bytes=60 * 2**20
        ),
        name="local",
    )(tokens, cotangent, decay_rate, residue, short_filter)


def finish_kernel(
    tiles, proj_ref, cot_ref, before_ref, after_ref, wide_ref, ends_ref, local_ref,
    near_ref, into_ref, gated_ref, grad_ref, sums_ref,
    pads, feats, grads, lefts, rights, fars, flip_parts, mixers, sums,
):
    def spans(tile):
        return slice(tile * LANES, (tile + 1) * LANES)

    for tile in range(tiles):
        lanes = spans(tile)
        pad = pads.at[tile]
        load_tokens(pad, proj_ref, before_ref, lanes)
        for i in range(3):
            pad[i, 8 + ROWS : 16 + ROWS, :] = after_ref[i, :, lanes]
        taps = tap_rows(wide_ref, lanes)
        for start in range(0, ROWS, 32):
            for i in range(3):
                feats[tile, i, start : start + 32, :] = feature(pad, taps, i, start, 32)
        pick = iota((MODES, LANES), 1) % MODES == iota((MODES, LANES), 0)

        def across(row):
            block = wide_ref[row : row + MODES, lanes]
            return jnp.sum(jnp.where(pick, block, 0.0), axis=0, keepdims=True)

        ahead = (iota((ROWS, LANES), 0) + 1).astype(F32)
        high, low = split(across(RESIDUE) * jnp.exp(-across(DECAY) * ahead))
        lefts[tile, :, 0:LANES] = high
        lefts[tile, :, LANES : 2 * LANES] = low
        lefts[tile, :, 2 * LANES : 3 * LANES] = high
        high, low = split(
            jnp.concatenate(
                [into_ref[tile, 0:MODES, :], into_ref[tile, MODES : 2 * MODES, :]], axis=1
            )
        )
        for g in range(TILE_GROUPS):
            keep = in_group(MODES, 2 * LANES, g)
            chosen = jnp.where(keep, high, jnp.zeros_like(high))
            begin = MODES * g
            rights[tile, begin : begin + MODES, :] = chosen
            rights[tile, ROWS + begin : ROWS + begin + MODES, :] = chosen
            rights[tile, 2 * ROWS + begin : 2 * ROWS + begin + MODES, :] = jnp.where(
                keep, low, jnp.zeros_like(low)
            )
    for tile in range(tiles):
        fars[tile] = dot(lefts[tile], rights[tile])
    for tile in range(tiles):
        lanes = spans(tile)
        long_conv = near_ref[0, :, lanes] + fars[tile, :, 0:LANES]
        high, low = split(near_ref[1, :, lanes] + fars[tile, :, LANES : 2 * LANES])
        flip_parts[0:ROWS, lanes] = high
        flip_parts[ROWS : 2 * ROWS, lanes] = low
        gated_ref[:, lanes] = (feats[tile, 0] * long_conv).astype(BF16)
        grads[tile, 0, 0:ROWS, :] = cot_ref[:, lanes].astype(F32) * long_conv
    flip = flip_matrix()
    mixers[...] = dot(jnp.concatenate([flip, flip], axis=1), flip_parts[...])

    for tile in range(tiles):
        lanes = spans(tile)
        pad = pads.at[tile]
        grad = grads.at[tile]
        taps = tap_rows(wide_ref, lanes)
        decay = wide_ref[DECAY : DECAY + MODES, lanes]
        residue = wide_ref[RESIDUE : RESIDUE + MODES, lanes]
        state = into_ref[tile, 0:MODES, :]
        adjoint = into_ref[tile, MODES : 2 * MODES, :]
        grad[1, 0:ROWS, :] = mixers[:, lanes] * feats[tile, 2]
        grad[2, 0:ROWS, :] = mixers[:, lanes] * feats[tile, 1]

        pole = jnp.exp(-decay)
        inverse = jnp.exp(decay)
        next_feat = [feature(pad, taps, i, ROWS, 8) for i in range(3)]
        next_cot = after_ref[3, :, lanes]
        next_in = next_feat[1] * next_feat[2]
        next_grad = next_cot * next_feat[0]
        whole = jnp.exp(-decay * float(ROWS))
        behind = residue * pole * (whole * state + ends_ref[tile, 0:MODES, :])
        beyond = residue * adjoint
        lag_pos = residue
        lag_neg = residue * inverse
        conv_rows, mixer_rows, filters, filters_neg = [], [], [], []
        for k in range(TAPS - 1):
            filters.append(jnp.sum(lag_pos, axis=0, keepdims=True))
            filters_neg.append(jnp.sum(lag_neg, axis=0, keepdims=True))
            conv = jnp.sum(behind, axis=0, keepdims=True)
            mixer = jnp.sum(beyond, axis=0, keepdims=True)
            for j in range(k + 1):
                conv = conv + filters[k - j] * next_in[j : j + 1]
            for j in range(k):
                mixer = mixer - filters_neg[k - j - 1] * next_grad[j : j + 1]
            conv_rows.append(conv)
            mixer_rows.append(mixer)
            lag_pos, lag_neg = lag_pos * pole, lag_neg * inverse
            behind, beyond = behind * pole, beyond * inverse
        blank = jnp.zeros((8 - (TAPS - 1), LANES), F32)
        next_conv = jnp.concatenate(conv_rows + [blank], axis=0)
        next_mixer = jnp.concatenate(mixer_rows + [blank], axis=0)
        grad[0, ROWS : ROWS + 8, :] = next_cot * next_conv
        grad[1, ROWS : ROWS + 8, :] = next_mixer * next_feat[2]
        grad[2, ROWS : ROWS + 8, :] = next_mixer * next_feat[1]

        step = 32
        short = []
        for i in range(3):
            totals = [None] * TAPS
            for start in range(0, ROWS, step):
                rows = slice(start, start + step)
                own = grad[i, rows, :]
                total = None
                for j in range(TAPS):
                    term = taps[TAPS * i + j] * grad[i, start + j : start + j + step, :]
                    total = term if total is None else total + term
                    product = own * pad[i, 8 + start - j : 8 + start - j + step, :]
                    part = product[0:8]
                    for r in range(8, step, 8):
                        part = part + product[r : r + 8]
                    totals[j] = part if totals[j] is None else totals[j] + part
                grad_ref[i, rows, lanes] = total.astype(BF16)
            short += [jnp.sum(part, axis=0, keepdims=True) for part in totals]
        short.append(jnp.zeros((3, LANES), F32))
        lag_sum = local_ref[tile, 3 * MODES : 4 * MODES, :] + pole * (
            local_ref[tile, MODES : 2 * MODES, :] * state + local_ref[tile, 0:MODES, :] * adjoint
        )
        begin = TABLE_ROWS * tile
        sums[begin : begin + 24, :] = jnp.concatenate(short, axis=0)
        sums[begin + 24 : begin + 40, :] = local_ref[tile, 2 * MODES : 3 * MODES, :]
        sums[begin + 40 : begin + 56, :] = lag_sum

    high, low = split(sums[...])
    member = (iota((2 * LANES, LANES), 0) % LANES) // GROUP == iota((2 * LANES, LANES), 1)
    by_group = dot(jnp.concatenate([high, low], axis=1), member.astype(F32).astype(BF16))
    for tile in range(tiles):
        begin = TABLE_ROWS * tile
        packed = by_group[begin : begin + 8]
        for r in range(8, TABLE_ROWS, 8):
            packed = packed + pltpu.roll(by_group[begin + r : begin + r + 8], r, 1)
        sums_ref[tile] = packed


def finish(tokens, cotangent, wide, before, after, ends, local, near, into, block):
    channels = tokens.shape[2]
    tiles = block // LANES
    count = channels // LANES

    def per_tile(rows):
        return pl.BlockSpec((tiles, rows, LANES), lambda t: (t, 0, 0))

    def stack(k, rows):
        return pl.BlockSpec((k, rows, block), lambda t: (0, 0, t))

    plane = pl.BlockSpec((ROWS, block), lambda t: (0, t))
    return pl.pallas_call(
        partial(finish_kernel, tiles),
        grid=(channels // block,),
        in_specs=[
            stack(3, ROWS),
            plane,
            stack(3, 8),
            stack(4, 8),
            pl.BlockSpec((TABLE_ROWS, block), lambda t: (0, t)),
            per_tile(2 * MODES),
            per_tile(4 * MODES),
            stack(2, ROWS),
            per_tile(2 * MODES),
        ],
        out_specs=[plane, stack(3, ROWS), per_tile(8)],
        out_shape=[
            jax.ShapeDtypeStruct((ROWS, channels), BF16),
            jax.ShapeDtypeStruct((3, ROWS, channels), BF16),
            jax.ShapeDtypeStruct((count, 8, LANES), F32),
        ],
        scratch_shapes=[
            pltpu.VMEM((tiles, 3, ROWS + 16, LANES), F32),
            pltpu.VMEM((tiles, 3, ROWS, LANES), F32),
            pltpu.VMEM((tiles, 3, ROWS + 8, LANES), F32),
            pltpu.VMEM((tiles, ROWS, 3 * LANES), BF16),
            pltpu.VMEM((tiles, 3 * ROWS, 2 * LANES), BF16),
            pltpu.VMEM((tiles, ROWS, 2 * LANES), F32),
            pltpu.VMEM((2 * ROWS, tiles * LANES), BF16),
            pltpu.VMEM((ROWS, tiles * LANES), F32),
            pltpu.VMEM((tiles * TABLE_ROWS, LANES), F32),
        ],
        compiler_params=pltpu.CompilerParams(vmem_limit_bytes=48 * 2**20),
        name="finish",
    )(tokens, cotangent, before, after, wide, ends, local, near, into)


def total_kernel(
    n, m, nx, ny, part_ref, out_ref, packed, got, mine_sum, rows, s_a, r_a, s_b, r_b, s_c, r_c
):
    me, genome = lax.axis_index("ctx"), lax.axis_index("seq")
    x, y, z = lax.rem(me, nx), lax.rem(lax.div(me, nx), ny), lax.div(me, nx * ny)
    a, b = ny * m, n // ny
    my_a, my_b = y * m + genome, z * nx + x

    def id_a(k):
        return {"ctx": (z * ny + lax.div(k, m)) * nx + x, "seq": lax.rem(k, m)}

    def id_b(k):
        return {"ctx": (lax.div(k, nx) * ny + y) * nx + lax.rem(k, nx), "seq": genome}

    def ahead(mine, count, k):
        return lax.rem(mine + k, count)

    def behind(mine, count, k):
        return lax.rem(mine + count - k, count)

    def each(count, action):
        def run(k, carry):
            action(k)
            return carry

        lax.fori_loop(1, count, run, 0)

    def remote(source, target, send_sem, recv_sem, to):
        return pltpu.make_async_remote_copy(
            src_ref=source,
            dst_ref=target,
            send_sem=send_sem,
            recv_sem=recv_sem,
            device_id=to,
            device_id_type=MESH,
        )

    barrier = pltpu.get_barrier_semaphore()

    def greet(to):
        pl.semaphore_signal(barrier, inc=1, device_id=to, device_id_type=MESH)

    each(a, lambda k: greet(id_a(ahead(my_a, a, k))))
    each(b, lambda k: greet(id_b(ahead(my_b, b, k))))
    share = n // 2 // a
    for k in range(n // 2):
        packed[k // share, k % share] = part_ref[2 * k] + pltpu.roll(
            part_ref[2 * k + 1], LANES // 2, 1
        )
    got[my_a] = packed[my_a]
    pl.semaphore_wait(barrier, a - 1 + b - 1)

    def first(k, to, slot):
        return remote(packed.at[to], got.at[slot], s_a.at[k], r_a.at[slot], id_a(to))

    def second(k, to, slot):
        return remote(mine_sum, rows.at[slot], s_b.at[k], r_b.at[slot], id_b(to))

    def third(k, to, slot):
        return remote(out_ref.at[my_a], out_ref.at[slot], s_c.at[k], r_c.at[slot], id_a(to))

    def start(mine, count, copy):
        each(count, lambda k: copy(k, ahead(mine, count, k), mine).start())

    def arrive(mine, count, copy):
        each(
            count,
            lambda k: copy(k, behind(mine, count, k), behind(mine, count, k)).wait_recv(),
        )

    def sent(mine, count, copy):
        each(count, lambda k: copy(k, ahead(mine, count, k), mine).wait_send())

    start(my_a, a, first)
    arrive(my_a, a, first)
    total = got[0]
    for d in range(1, a):
        total = total + got[d]
    mine_sum[...] = total
    rows[my_b] = total
    start(my_b, b, second)
    arrive(my_b, b, second)
    total = rows[0]
    for d in range(1, b):
        total = total + rows[d]
    out_ref[my_a] = total
    start(my_a, a, third)
    arrive(my_a, a, third)
    sent(my_a, a, first)
    sent(my_b, b, second)
    sent(my_a, a, third)


def total_sums(n, m, parts):
    ny = 2
    nx = min(4, n // ny)
    a, b = ny * m, n // ny
    share = n // 2 // a
    vmem = pl.BlockSpec(memory_space=pltpu.VMEM)
    dma = pltpu.SemaphoreType.DMA
    return pl.pallas_call(
        partial(total_kernel, n, m, nx, ny),
        out_shape=jax.ShapeDtypeStruct((a, share, 8, LANES), F32),
        in_specs=[vmem],
        out_specs=vmem,
        scratch_shapes=[
            pltpu.VMEM((a, share, 8, LANES), F32),
            pltpu.VMEM((a, share, 8, LANES), F32),
            pltpu.VMEM((share, 8, LANES), F32),
            pltpu.VMEM((b, share, 8, LANES), F32),
            dma((a,)),
            dma((a,)),
            dma((b,)),
            dma((b,)),
            dma((a,)),
            dma((a,)),
        ],
        compiler_params=pltpu.CompilerParams(
            collective_id=1, has_side_effects=True, vmem_limit_bytes=16 * 2**20
        ),
        name="totals",
    )(parts)


def per_device(projected, cotangent, short_filter, residue, decay_rate):
    n, m = lax.axis_size("ctx"), lax.axis_size("seq")
    tokens, upstream = projected[0], cotangent[0]
    groups = residue.shape[1]
    block = min(tokens.shape[2], 512)
    known = local_part(n, tokens, upstream, decay_rate, residue, short_filter)
    gated, grad_tokens, sums = finish(tokens, upstream, *known, block)
    sums = total_sums(n, m, sums)
    sums = sums.reshape(n // 2, 8, 2, 8, TILE_GROUPS).transpose(3, 1, 0, 2, 4)
    sums = sums.reshape(64, groups) / float(ROWS * n * m)
    grad_short = sums[0 : 3 * TAPS].reshape(3, TAPS, groups)
    grad_residue = sums[24 : 24 + MODES]
    grad_log_decay = -residue * decay_rate * sums[40 : 40 + MODES]
    return gated[None], grad_tokens[None], grad_short, grad_residue, grad_log_decay


def solution(mesh):
    placed = (P("seq", None, "ctx", None), P("seq", "ctx", None), P(), P(), P())
    return jax.shard_map(
        per_device,
        mesh=mesh,
        in_specs=placed,
        out_specs=(P("seq", "ctx", None), P("seq", None, "ctx", None), P(), P(), P()),
        check_vma=False,
    )
```

```python
from functools import partial

import jax
import jax.numpy as jnp
from jax import lax
from jax.experimental import pallas as pl
from jax.experimental.pallas import tpu as pltpu
from jax.sharding import PartitionSpec as P

GROUP = 16
MODES = 16
TAPS = 7
LANES = 128
TILE_GROUPS = LANES // GROUP
ROWS = 128
F32, BF16 = jnp.float32, jnp.bfloat16
MESH = pl.DeviceIdType.MESH

HALF = ROWS // 2
QUARTER = ROWS // 4
GROUPED = 4
WAYS = 2

DECAY, RESIDUE, SHORT, TABLE_ROWS = 0, 16, 32, 56
SUM_ROWS = 64


def split(value):
    high = value.astype(BF16)
    return high, (value - high.astype(F32)).astype(BF16)


def iota(shape, dim):
    return lax.broadcasted_iota(jnp.int32, shape, dim)


def dot(left, right):
    return jnp.dot(left, right, preferred_element_type=F32)


def in_group(rows, width, group):
    return (iota((rows, width), 1) % LANES) // GROUP == group


def flip_matrix():
    return (iota((ROWS, ROWS), 0) + iota((ROWS, ROWS), 1) == ROWS - 1).astype(BF16)


def load_tokens(pad, proj_ref, before_ref, lanes):
    for i in range(3):
        pad[i, 0:8, :] = before_ref[i, :, lanes]
        pad[i, 8 : 8 + ROWS, :] = proj_ref[i, :, lanes].astype(F32)


def feature(pad, taps, i, start, count):
    total = None
    for j in range(TAPS):
        term = taps[TAPS * i + j] * pad[i, 8 + start - j : 8 + start - j + count, :]
        total = term if total is None else total + term
    return total


def tap_rows(wide_ref, lanes):
    return [wide_ref[SHORT + k : SHORT + k + 1, lanes] for k in range(3 * TAPS)]


def expand_table(wide_ref, small, decay_ref, residue_ref, short_ref):
    small[DECAY : DECAY + MODES, :] = decay_ref[...]
    small[RESIDUE : RESIDUE + MODES, :] = residue_ref[...]
    for i in range(3):
        small[SHORT + TAPS * i : SHORT + TAPS * (i + 1), :] = short_ref[i]
    used = SHORT + 3 * TAPS
    groups = small.shape[1]
    small[used:TABLE_ROWS, :] = jnp.zeros((TABLE_ROWS - used, groups), F32)
    value = small[...]
    high = value.astype(BF16).astype(F32)
    middle = (value - high).astype(BF16).astype(F32)
    low = value - high - middle
    pieces = jnp.concatenate([high, middle, low], axis=0).astype(BF16)
    width = min(1024, wide_ref.shape[1])
    for start in range(0, wide_ref.shape[1], width):
        owner = (iota((groups, width), 1) + start) // GROUP
        spread = (iota((groups, width), 0) == owner).astype(F32).astype(BF16)
        got = dot(pieces, spread)
        wide_ref[:, start : start + width] = got[0:TABLE_ROWS] + (
            got[TABLE_ROWS : 2 * TABLE_ROWS] + got[2 * TABLE_ROWS :]
        )


def lanes_of(tile):
    return pl.ds(pl.multiple_of(tile * LANES, LANES), LANES)


def select_groups(source, begin, count, rows, columns):
    total = source[begin + rows.start : begin + rows.stop, columns]
    for g in range(1, TILE_GROUPS):
        at = begin + g * count
        total = jnp.where(
            in_group(rows.stop - rows.start, columns.stop - columns.start, g),
            source[at + rows.start : at + rows.stop, columns],
            total,
        )
    return total


def local_kernel(
    n, proj_ref, cot_ref, decay_ref, residue_ref, short_ref,
    wide_ref, before_ref, after_ref, ends_ref, local_ref, near_ref, into_ref,
    small, out_f, out_b, got_f, got_b, got, back, tables, streams, pad, parts, *scratch,
):
    left_pairs, right_pairs, pair_sums = (scratch[k * WAYS : (k + 1) * WAYS] for k in range(3))
    scratch = scratch[3 * WAYS :]
    rights, products, products_low = (scratch[k * GROUPED : (k + 1) * GROUPED] for k in range(3))
    halo_send, halo_recv, s_out, r_out, s_in, r_in = scratch[3 * GROUPED :]
    me = lax.axis_index("ctx")
    right_dev, left_dev = lax.rem(me + 1, n), lax.rem(me + n - 1, n)
    far_back = (LANES - 1 - iota((MODES, LANES), 1)).astype(F32)

    def peer_of(k):
        return lax.rem(me + k, n)

    def each(action):
        def run(k, carry):
            action(k)
            return carry

        lax.fori_loop(1, n, run, 0)

    def remote(source, target, send_sem, recv_sem, to):
        return pltpu.make_async_remote_copy(
            src_ref=source,
            dst_ref=target,
            send_sem=send_sem,
            recv_sem=recv_sem,
            device_id={"ctx": to},
            device_id_type=MESH,
        )

    barrier = pltpu.get_barrier_semaphore()
    each(
        lambda k: pl.semaphore_signal(
            barrier, inc=1, device_id={"ctx": peer_of(k)}, device_id_type=MESH
        )
    )
    width = out_f.shape[2]
    for i in range(3):
        tail = proj_ref[i, ROWS - 16 : ROWS, :].astype(F32)[8:16]
        out_f[i] = jnp.concatenate([tail[:, :width], tail[:, width:]], axis=0).astype(BF16)
    for i in range(4):
        head = (cot_ref[0:16, :] if i == 3 else proj_ref[i, 0:16, :]).astype(F32)[0:8]
        out_b[i] = jnp.concatenate([head[:, :width], head[:, width:]], axis=0).astype(BF16)
    expand_table(wide_ref, small, decay_ref, residue_ref, short_ref)
    pl.semaphore_wait(barrier, n - 1)
    halo = [
        remote(out_f, got_f, halo_send.at[0], halo_recv.at[0], right_dev),
        remote(out_b, got_b, halo_send.at[1], halo_recv.at[1], left_dev),
    ]
    for copy in halo:
        copy.start()

    def power_of(tile, g):
        column = GROUP * g
        decay = wide_ref[DECAY : DECAY + MODES, lanes_of(tile)]
        return jnp.exp(-decay[:, column : column + 1] * far_back)

    def store_table(tile, at, value):
        high, low = split(value)
        tables[tile, at, 0:LANES] = high
        tables[tile, at, LANES : 2 * LANES] = low
        tables[tile, at, 2 * LANES : 3 * LANES] = high

    def build_tables(tile, carry):
        residue = wide_ref[RESIDUE : RESIDUE + MODES, lanes_of(tile)]
        for g in range(TILE_GROUPS):
            column = GROUP * g
            power = power_of(tile, g)
            filter_row = jnp.sum(residue[:, column : column + 1] * power, axis=0, keepdims=True)
            base = pltpu.roll(
                jnp.broadcast_to(filter_row, (8, LANES)), 1, 1, stride=1, stride_axis=0
            )
            for q in range(HALF, ROWS, 16):
                block = jnp.concatenate(
                    [pltpu.roll(base, q, 1), pltpu.roll(base, q + 8, 1)], axis=0
                )
                keep = iota((16, LANES), 1) <= iota((16, LANES), 0) + q
                begin = HALF * g + q - HALF
                store_table(tile, slice(begin, begin + 16), jnp.where(keep, block, 0.0))
            for k, value in enumerate((power, far_back * power)):
                begin = TILE_GROUPS * (HALF + k * MODES) + MODES * g
                store_table(tile, slice(begin, begin + MODES), value)
        return carry

    lax.fori_loop(0, n, build_tables, 0)
    for way in range(GROUPED):
        for k in range(3):
            begin = ROWS * k
            rights[way][begin : begin + HALF, 2 * LANES : 4 * LANES] = jnp.zeros(
                (HALF, 2 * LANES), BF16
            )
    for way in range(WAYS):
        right_pairs[way][...] = jnp.zeros((2 * ROWS, 8 * LANES), BF16)

    for copy in halo:
        copy.wait()
    first, last = me == 0, me == n - 1
    for i in range(3):
        part = jnp.where(first, 0.0, got_f[i].astype(F32))
        before_ref[i, :, 0:width] = part[0:8]
        before_ref[i, :, width : 2 * width] = part[8:16]
    for i in range(4):
        part = jnp.where(last, 0.0, got_b[i].astype(F32))
        after_ref[i, :, 0:width] = part[0:8]
        after_ref[i, :, width : 2 * width] = part[8:16]

    def features(tile, way):
        lanes = lanes_of(tile)
        load_tokens(pad, proj_ref, before_ref, lanes)
        taps = tap_rows(wide_ref, lanes)
        step = 32
        for start in range(0, ROWS, step):
            rows = slice(start, start + step)
            f = [feature(pad, taps, i, start, step) for i in range(3)]
            high, low = split(f[1] * f[2])
            streams[tile, rows, 0:LANES] = high
            streams[tile, rows, LANES : 2 * LANES] = low
            for k, value in enumerate((high, high, low)):
                begin = ROWS * k + start
                rights[way][begin : begin + step, 0:LANES] = value
                if start < HALF:
                    begin = begin + HALF
                    rights[way][begin : begin + step, 2 * LANES : 3 * LANES] = value
            high, low = split(cot_ref[rows, lanes].astype(F32) * f[0])
            begin = 2 * LANES * way
            parts[rows, begin : begin + LANES] = high
            parts[rows, begin + LANES : begin + 2 * LANES] = low

    def place(tile, way, flipped):
        streams[tile, :, 2 * LANES : 4 * LANES] = flipped
        for k, column in enumerate((0, 0, LANES)):
            value = flipped[:, column : column + LANES]
            begin = ROWS * k
            rights[way][begin : begin + ROWS, LANES : 2 * LANES] = value
            rights[way][begin + HALF : begin + ROWS, 3 * LANES : 4 * LANES] = value[0:HALF]

    modes, both = slice(0, MODES), slice(0, 2 * LANES)

    def send_out(k):
        return remote(
            ends_ref.at[peer_of(k)], got.at[me], s_out.at[k], r_out.at[me], peer_of(k)
        )

    def begin_tiles(step, carry):
        ks = [step * GROUPED + way for way in range(GROUPED)]
        for way, k in enumerate(ks):
            features(peer_of(k), way)
        flipped = dot(flip_matrix(), parts[...]).astype(BF16)
        for way, k in enumerate(ks):
            place(peer_of(k), way, flipped[:, 2 * LANES * way : 2 * LANES * (way + 1)])
        for way, k in enumerate(ks):
            tile = peer_of(k)
            products[way][...] = dot(tables[tile], rights[way][:, 0 : 2 * LANES])
            products_low[way][...] = dot(
                tables[tile, 0 : TILE_GROUPS * HALF, :], rights[way][:, 2 * LANES : 4 * LANES]
            )
        for way, k in enumerate(ks):
            tile = peer_of(k)
            first_end = TILE_GROUPS * HALF
            ends = select_groups(products[way], first_end, MODES, modes, both)
            ends_ref[tile, 0:MODES, :] = ends[:, 0:LANES]
            ends_ref[tile, MODES : 2 * MODES, :] = ends[:, LANES : 2 * LANES]
            first_lag = first_end + TILE_GROUPS * MODES
            lags = select_groups(products[way], first_lag, MODES, modes, both)
            local_ref[tile, 0:MODES, :] = lags[:, 0:LANES]
            local_ref[tile, MODES : 2 * MODES, :] = lags[:, LANES : 2 * LANES]
            for start in range(0, ROWS, 32):
                source = products[way] if start >= HALF else products_low[way]
                begin = start % HALF
                near = select_groups(source, 0, HALF, slice(begin, begin + 32), both)
                near_ref[0, start : start + 32, lanes_of(tile)] = near[:, 0:LANES]
                near_ref[1, start : start + 32, lanes_of(tile)] = near[:, LANES : 2 * LANES]
        for k in ks:

            @pl.when(k != 0)
            def _():
                send_out(k).start()

        return carry

    lax.fori_loop(0, n // GROUPED, begin_tiles, 0)

    lane = iota((MODES, LANES), 1)

    def correlate(step, carry):
        tiles = [step * WAYS + way for way in range(WAYS)]
        for way, tile in enumerate(tiles):
            for h in range(4):
                at = slice(QUARTER * h, QUARTER * (h + 1))
                columns = slice(2 * LANES * h, 2 * LANES * (h + 1))
                flipped = streams[tile, at, 2 * LANES : 4 * LANES]
                for g in range(TILE_GROUPS):
                    left_pairs[way][QUARTER * g : QUARTER * (g + 1), columns] = jnp.where(
                        in_group(QUARTER, 2 * LANES, g), flipped, jnp.zeros_like(flipped)
                    )
                keep = ROWS - QUARTER * h
                for k in range(2):
                    value = streams[tile, 0:keep, LANES * k : LANES * (k + 1)]
                    at = slice(ROWS * (k + 1) - keep, ROWS * (k + 1))
                    for column in (2 * LANES * h, 2 * LANES * h + LANES):
                        right_pairs[way][at, column : column + LANES] = value
        for way in range(WAYS):
            pair_sums[way][...] = lax.dot_general(
                left_pairs[way][...],
                right_pairs[way][...],
                (((1,), (1,)), ((), ())),
                preferred_element_type=F32,
            )
        for way, tile in enumerate(tiles):
            res_sum = jnp.zeros((MODES, LANES), F32)
            lag_sum = jnp.zeros((MODES, LANES), F32)
            for g in range(TILE_GROUPS):
                total = None
                for q in range(0, QUARTER, 8):
                    at = slice(QUARTER * g + q, QUARTER * g + q + 8)
                    block = pair_sums[way][at, 0:LANES] + pair_sums[way][at, LANES : 2 * LANES]
                    keep = iota((8, LANES), 1) + iota((8, LANES), 0) <= ROWS - 1 - q
                    block = jnp.where(keep, block, 0.0)
                    if q:
                        block = pltpu.roll(block, q, 1)
                    total = block if total is None else total + block
                by_lag = jnp.sum(
                    pltpu.roll(total, 0, 1, stride=1, stride_axis=0), axis=0, keepdims=True
                )
                weighted = power_of(tile, g) * by_lag
                res_sum = jnp.where(
                    lane == GROUP * g, jnp.sum(weighted, axis=1, keepdims=True), res_sum
                )
                lag_sum = jnp.where(
                    lane == GROUP * g,
                    jnp.sum(far_back * weighted, axis=1, keepdims=True),
                    lag_sum,
                )
            local_ref[tile, 2 * MODES : 3 * MODES, :] = res_sum
            local_ref[tile, 3 * MODES : 4 * MODES, :] = lag_sum
        return carry

    lax.fori_loop(0, n // WAYS // 2, correlate, 0)

    def receive_out(k):
        source = lax.rem(me + n - k, n)
        return remote(ends_ref.at[source], got.at[source], s_out.at[k], r_out.at[source], source)

    def send_in(k):
        return remote(back.at[peer_of(k)], into_ref.at[me], s_in.at[k], r_in.at[me], peer_of(k))

    def receive_in(k):
        source = lax.rem(me + n - k, n)
        return remote(back.at[source], into_ref.at[source], s_in.at[k], r_in.at[source], source)

    got[me] = ends_ref[me]
    each(lambda k: receive_out(k).wait_recv())
    decay = wide_ref[DECAY : DECAY + MODES, lanes_of(me)]
    pole = jnp.exp(-decay)
    whole = jnp.exp(-decay * float(ROWS))
    zero = jnp.zeros((MODES, LANES), F32)

    def scan(step, carry):
        state, lagged, res, lag, beyond = carry
        for k in range(2):
            d = step * 2 + k
            adjoint = got[d, MODES : 2 * MODES, :]
            back[d, 0:MODES, :] = state
            res = res + adjoint * state
            lag = lag + adjoint * (state + float(ROWS) * lagged)
            state, lagged = whole * state + got[d, 0:MODES, :], whole * (lagged + state)
            d = n - 1 - d
            back[d, MODES : 2 * MODES, :] = beyond
            beyond = whole * beyond + got[d, MODES : 2 * MODES, :]
        return state, lagged, res, lag, beyond

    _, _, cross_res, cross_lag, _ = lax.fori_loop(0, n // 2, scan, (zero,) * 5)
    each(lambda k: send_in(k).start())
    into_ref[me] = back[me]

    lax.fori_loop(n // WAYS // 2, n // WAYS, correlate, 0)
    local_ref[me, 2 * MODES : 3 * MODES, :] = (
        local_ref[me, 2 * MODES : 3 * MODES, :] + pole * cross_res
    )
    local_ref[me, 3 * MODES : 4 * MODES, :] = (
        local_ref[me, 3 * MODES : 4 * MODES, :] + pole * cross_lag
    )
    each(lambda k: receive_in(k).wait_recv())
    each(lambda k: send_out(k).wait_send())
    each(lambda k: send_in(k).wait_send())


def local_part(n, tokens, cotangent, decay_rate, residue, short_filter):
    channels = tokens.shape[2]
    groups = residue.shape[1]
    half = channels // 2
    vmem = pl.BlockSpec(memory_space=pltpu.VMEM)
    wide_rows = TILE_GROUPS * (HALF + 2 * MODES)
    return pl.pallas_call(
        partial(local_kernel, n),
        in_specs=[vmem] * 5,
        out_specs=[vmem] * 7,
        out_shape=[
            jax.ShapeDtypeStruct(shape, F32)
            for shape in (
                (TABLE_ROWS, channels),
                (3, 8, channels),
                (4, 8, channels),
                (n, 2 * MODES, LANES),
                (n, 4 * MODES, LANES),
                (2, ROWS, channels),
                (n, 2 * MODES, LANES),
            )
        ],
        scratch_shapes=[
            pltpu.VMEM((TABLE_ROWS, groups), F32),
            pltpu.VMEM((3, 16, half), BF16),
            pltpu.VMEM((4, 16, half), BF16),
            pltpu.VMEM((3, 16, half), BF16),
            pltpu.VMEM((4, 16, half), BF16),
            pltpu.VMEM((n, 2 * MODES, LANES), F32),
            pltpu.VMEM((n, 2 * MODES, LANES), F32),
            pltpu.VMEM((n, wide_rows, 3 * LANES), BF16),
            pltpu.VMEM((n, ROWS, 4 * LANES), BF16),
            pltpu.VMEM((3, ROWS + 8, LANES), F32),
            pltpu.VMEM((ROWS, 2 * LANES * GROUPED), BF16),
        ]
        + [pltpu.VMEM((TILE_GROUPS * QUARTER, 8 * LANES), BF16)] * WAYS
        + [pltpu.VMEM((2 * ROWS, 8 * LANES), BF16)] * WAYS
        + [pltpu.VMEM((TILE_GROUPS * QUARTER, 2 * LANES), F32)] * WAYS
        + [pltpu.VMEM((3 * ROWS, 4 * LANES), BF16)] * GROUPED
        + [pltpu.VMEM((wide_rows, 2 * LANES), F32)] * GROUPED
        + [pltpu.VMEM((TILE_GROUPS * HALF, 2 * LANES), F32)] * GROUPED
        + [pltpu.SemaphoreType.DMA((2,))] * 2
        + [pltpu.SemaphoreType.DMA((n,))] * 4,
        compiler_params=pltpu.CompilerParams(
            collective_id=0, has_side_effects=True, vmem_limit_bytes=60 * 2**20
        ),
        name="local",
    )(tokens, cotangent, decay_rate, residue, short_filter)


def finish_kernel(
    tiles, proj_ref, cot_ref, before_ref, after_ref, wide_ref, ends_ref, local_ref,
    near_ref, into_ref, gated_ref, grad_ref, sums_ref,
    pads, feats, grads, lefts, rights, fars, flip_parts, mixers, sums,
):
    step_index = pl.program_id(0)

    @pl.when(step_index == 0)
    def _():
        sums_ref[...] = jnp.zeros(sums_ref.shape, F32)

    def spans(tile):
        return slice(tile * LANES, (tile + 1) * LANES)

    for tile in range(tiles):
        lanes = spans(tile)
        pad = pads.at[tile]
        load_tokens(pad, proj_ref, before_ref, lanes)
        for i in range(3):
            pad[i, 8 + ROWS : 16 + ROWS, :] = after_ref[i, :, lanes]
        taps = tap_rows(wide_ref, lanes)
        for start in range(0, ROWS, 32):
            for i in range(3):
                feats[tile, i, start : start + 32, :] = feature(pad, taps, i, start, 32)
        pick = iota((MODES, LANES), 1) % MODES == iota((MODES, LANES), 0)

        def across(row):
            block = wide_ref[row : row + MODES, lanes]
            return jnp.sum(jnp.where(pick, block, 0.0), axis=0, keepdims=True)

        ahead = (iota((ROWS, LANES), 0) + 1).astype(F32)
        high, low = split(across(RESIDUE) * jnp.exp(-across(DECAY) * ahead))
        lefts[tile, :, 0:LANES] = high
        lefts[tile, :, LANES : 2 * LANES] = low
        lefts[tile, :, 2 * LANES : 3 * LANES] = high
        high, low = split(
            jnp.concatenate(
                [into_ref[tile, 0:MODES, :], into_ref[tile, MODES : 2 * MODES, :]], axis=1
            )
        )
        for g in range(TILE_GROUPS):
            keep = in_group(MODES, 2 * LANES, g)
            chosen = jnp.where(keep, high, jnp.zeros_like(high))
            begin = MODES * g
            rights[tile, begin : begin + MODES, :] = chosen
            rights[tile, ROWS + begin : ROWS + begin + MODES, :] = chosen
            rights[tile, 2 * ROWS + begin : 2 * ROWS + begin + MODES, :] = jnp.where(
                keep, low, jnp.zeros_like(low)
            )
    for tile in range(tiles):
        fars[tile] = dot(lefts[tile], rights[tile])
    for tile in range(tiles):
        lanes = spans(tile)
        long_conv = near_ref[0, :, lanes] + fars[tile, :, 0:LANES]
        high, low = split(near_ref[1, :, lanes] + fars[tile, :, LANES : 2 * LANES])
        flip_parts[0:ROWS, lanes] = high
        flip_parts[ROWS : 2 * ROWS, lanes] = low
        gated_ref[:, lanes] = (feats[tile, 0] * long_conv).astype(BF16)
        grads[tile, 0, 0:ROWS, :] = cot_ref[:, lanes].astype(F32) * long_conv
    flip = flip_matrix()
    mixers[...] = dot(jnp.concatenate([flip, flip], axis=1), flip_parts[...])

    for tile in range(tiles):
        lanes = spans(tile)
        pad = pads.at[tile]
        grad = grads.at[tile]
        taps = tap_rows(wide_ref, lanes)
        decay = wide_ref[DECAY : DECAY + MODES, lanes]
        residue = wide_ref[RESIDUE : RESIDUE + MODES, lanes]
        state = into_ref[tile, 0:MODES, :]
        adjoint = into_ref[tile, MODES : 2 * MODES, :]
        grad[1, 0:ROWS, :] = mixers[:, lanes] * feats[tile, 2]
        grad[2, 0:ROWS, :] = mixers[:, lanes] * feats[tile, 1]

        pole = jnp.exp(-decay)
        inverse = jnp.exp(decay)
        next_feat = [feature(pad, taps, i, ROWS, 8) for i in range(3)]
        next_cot = after_ref[3, :, lanes]
        next_in = next_feat[1] * next_feat[2]
        next_grad = next_cot * next_feat[0]
        whole = jnp.exp(-decay * float(ROWS))
        behind = residue * pole * (whole * state + ends_ref[tile, 0:MODES, :])
        beyond = residue * adjoint
        lag_pos = residue
        lag_neg = residue * inverse
        conv_rows, mixer_rows, filters, filters_neg = [], [], [], []
        for k in range(TAPS - 1):
            filters.append(jnp.sum(lag_pos, axis=0, keepdims=True))
            filters_neg.append(jnp.sum(lag_neg, axis=0, keepdims=True))
            conv = jnp.sum(behind, axis=0, keepdims=True)
            mixer = jnp.sum(beyond, axis=0, keepdims=True)
            for j in range(k + 1):
                conv = conv + filters[k - j] * next_in[j : j + 1]
            for j in range(k):
                mixer = mixer - filters_neg[k - j - 1] * next_grad[j : j + 1]
            conv_rows.append(conv)
            mixer_rows.append(mixer)
            lag_pos, lag_neg = lag_pos * pole, lag_neg * inverse
            behind, beyond = behind * pole, beyond * inverse
        blank = jnp.zeros((8 - (TAPS - 1), LANES), F32)
        next_conv = jnp.concatenate(conv_rows + [blank], axis=0)
        next_mixer = jnp.concatenate(mixer_rows + [blank], axis=0)
        grad[0, ROWS : ROWS + 8, :] = next_cot * next_conv
        grad[1, ROWS : ROWS + 8, :] = next_mixer * next_feat[2]
        grad[2, ROWS : ROWS + 8, :] = next_mixer * next_feat[1]

        step = 32
        short = []
        for i in range(3):
            totals = [None] * TAPS
            for start in range(0, ROWS, step):
                rows = slice(start, start + step)
                own = grad[i, rows, :]
                total = None
                for j in range(TAPS):
                    term = taps[TAPS * i + j] * grad[i, start + j : start + j + step, :]
                    total = term if total is None else total + term
                    product = own * pad[i, 8 + start - j : 8 + start - j + step, :]
                    part = product[0:8]
                    for r in range(8, step, 8):
                        part = part + product[r : r + 8]
                    totals[j] = part if totals[j] is None else totals[j] + part
                grad_ref[i, rows, lanes] = total.astype(BF16)
            short += [jnp.sum(part, axis=0, keepdims=True) for part in totals]
        short.append(jnp.zeros((3, LANES), F32))
        lag_sum = local_ref[tile, 3 * MODES : 4 * MODES, :] + pole * (
            local_ref[tile, MODES : 2 * MODES, :] * state + local_ref[tile, 0:MODES, :] * adjoint
        )
        res_sum = local_ref[tile, 2 * MODES : 3 * MODES, :]
        rest = jnp.zeros((SUM_ROWS - TABLE_ROWS, LANES), F32)
        high, low = split(jnp.concatenate(short + [res_sum, lag_sum, rest], axis=0))
        begin = 2 * LANES * tile
        sums[:, begin : begin + LANES] = high
        sums[:, begin + LANES : begin + 2 * LANES] = low

    shape = (tiles * 2 * LANES, sums_ref.shape[1])
    row = iota(shape, 0)
    owner = (row // (2 * LANES) + step_index * tiles) * TILE_GROUPS + (row % LANES) // GROUP
    member = (owner == iota(shape, 1)).astype(F32).astype(BF16)
    sums_ref[...] = sums_ref[...] + dot(sums[...], member)


def finish(tokens, cotangent, wide, before, after, ends, local, near, into, block):
    channels = tokens.shape[2]
    tiles = block // LANES
    groups = channels // GROUP

    def per_tile(rows):
        return pl.BlockSpec((tiles, rows, LANES), lambda t: (t, 0, 0))

    def stack(k, rows):
        return pl.BlockSpec((k, rows, block), lambda t: (0, 0, t))

    plane = pl.BlockSpec((ROWS, block), lambda t: (0, t))
    return pl.pallas_call(
        partial(finish_kernel, tiles),
        grid=(channels // block,),
        in_specs=[
            stack(3, ROWS),
            plane,
            stack(3, 8),
            stack(4, 8),
            pl.BlockSpec((TABLE_ROWS, block), lambda t: (0, t)),
            per_tile(2 * MODES),
            per_tile(4 * MODES),
            stack(2, ROWS),
            per_tile(2 * MODES),
        ],
        out_specs=[plane, stack(3, ROWS), pl.BlockSpec((SUM_ROWS, groups), lambda t: (0, 0))],
        out_shape=[
            jax.ShapeDtypeStruct((ROWS, channels), BF16),
            jax.ShapeDtypeStruct((3, ROWS, channels), BF16),
            jax.ShapeDtypeStruct((SUM_ROWS, groups), F32),
        ],
        scratch_shapes=[
            pltpu.VMEM((tiles, 3, ROWS + 16, LANES), F32),
            pltpu.VMEM((tiles, 3, ROWS, LANES), F32),
            pltpu.VMEM((tiles, 3, ROWS + 8, LANES), F32),
            pltpu.VMEM((tiles, ROWS, 3 * LANES), BF16),
            pltpu.VMEM((tiles, 3 * ROWS, 2 * LANES), BF16),
            pltpu.VMEM((tiles, ROWS, 2 * LANES), F32),
            pltpu.VMEM((2 * ROWS, tiles * LANES), BF16),
            pltpu.VMEM((ROWS, tiles * LANES), F32),
            pltpu.VMEM((SUM_ROWS, tiles * 2 * LANES), BF16),
        ],
        compiler_params=pltpu.CompilerParams(vmem_limit_bytes=62 * 2**20),
        name="finish",
    )(tokens, cotangent, before, after, wide, ends, local, near, into)


def total_kernel(
    n, m, nx, ny, part_ref, decay_ref, residue_ref, short_ref, res_ref, log_ref,
    got, mine_sum, rows, full, s_a, r_a, s_b, r_b, s_c, r_c,
):
    me, genome = lax.axis_index("ctx"), lax.axis_index("seq")
    x, y, z = lax.rem(me, nx), lax.rem(lax.div(me, nx), ny), lax.div(me, nx * ny)
    a, b = ny * m, n // ny
    my_a, my_b = y * m + genome, z * nx + x

    def id_a(k):
        return {"ctx": (z * ny + lax.div(k, m)) * nx + x, "seq": lax.rem(k, m)}

    def id_b(k):
        return {"ctx": (lax.div(k, nx) * ny + y) * nx + lax.rem(k, nx), "seq": genome}

    def ahead(mine, count, k):
        return lax.rem(mine + k, count)

    def behind(mine, count, k):
        return lax.rem(mine + count - k, count)

    def each(count, action):
        def run(k, carry):
            action(k)
            return carry

        lax.fori_loop(1, count, run, 0)

    def remote(source, target, send_sem, recv_sem, to):
        return pltpu.make_async_remote_copy(
            src_ref=source,
            dst_ref=target,
            send_sem=send_sem,
            recv_sem=recv_sem,
            device_id=to,
            device_id_type=MESH,
        )

    barrier = pltpu.get_barrier_semaphore()

    def greet(to):
        pl.semaphore_signal(barrier, inc=1, device_id=to, device_id_type=MESH)

    each(a, lambda k: greet(id_a(ahead(my_a, a, k))))
    each(b, lambda k: greet(id_b(ahead(my_b, b, k))))
    got[my_a] = part_ref[my_a]
    pl.semaphore_wait(barrier, a - 1 + b - 1)

    def first(k, to, slot):
        return remote(part_ref.at[to], got.at[slot], s_a.at[k], r_a.at[slot], id_a(to))

    def second(k, to, slot):
        return remote(mine_sum, rows.at[slot], s_b.at[k], r_b.at[slot], id_b(to))

    def third(k, to, slot):
        return remote(full.at[my_a], full.at[slot], s_c.at[k], r_c.at[slot], id_a(to))

    def start(mine, count, copy):
        each(count, lambda k: copy(k, ahead(mine, count, k), mine).start())

    def arrive(mine, count, copy):
        each(
            count,
            lambda k: copy(k, behind(mine, count, k), behind(mine, count, k)).wait_recv(),
        )

    def sent(mine, count, copy):
        each(count, lambda k: copy(k, ahead(mine, count, k), mine).wait_send())

    start(my_a, a, first)
    arrive(my_a, a, first)
    total = got[0]
    for d in range(1, a):
        total = total + got[d]
    mine_sum[...] = total
    rows[my_b] = total
    start(my_b, b, second)
    arrive(my_b, b, second)
    total = rows[0]
    for d in range(1, b):
        total = total + rows[d]
    full[my_a] = total
    start(my_a, a, third)
    arrive(my_a, a, third)
    share = full.shape[1]
    sums = jnp.concatenate([full[k // share, k % share] for k in range(TABLE_ROWS // 8)], axis=0)
    sums = sums * (1.0 / float(ROWS * n * m))
    for i in range(3):
        short_ref[i] = sums[TAPS * i : TAPS * (i + 1)]
    res_ref[...] = sums[24 : 24 + MODES]
    log_ref[...] = -residue_ref[...] * decay_ref[...] * sums[40 : 40 + MODES]
    sent(my_a, a, first)
    sent(my_b, b, second)
    sent(my_a, a, third)


def total_sums(n, m, parts, decay_rate, residue):
    ny = 2
    nx = min(4, n // ny)
    a, b = ny * m, n // ny
    share, groups = SUM_ROWS // 8 // a, parts.shape[1]
    vmem = pl.BlockSpec(memory_space=pltpu.VMEM)
    dma = pltpu.SemaphoreType.DMA
    return pl.pallas_call(
        partial(total_kernel, n, m, nx, ny),
        out_shape=[
            jax.ShapeDtypeStruct((3, TAPS, groups), F32),
            jax.ShapeDtypeStruct((MODES, groups), F32),
            jax.ShapeDtypeStruct((MODES, groups), F32),
        ],
        in_specs=[vmem] * 3,
        out_specs=[vmem] * 3,
        scratch_shapes=[
            pltpu.VMEM((a, share, 8, groups), F32),
            pltpu.VMEM((share, 8, groups), F32),
            pltpu.VMEM((b, share, 8, groups), F32),
            pltpu.VMEM((a, share, 8, groups), F32),
            dma((a,)),
            dma((a,)),
            dma((b,)),
            dma((b,)),
            dma((a,)),
            dma((a,)),
        ],
        compiler_params=pltpu.CompilerParams(
            collective_id=1, has_side_effects=True, vmem_limit_bytes=16 * 2**20
        ),
        name="totals",
    )(parts.reshape(a, share, 8, groups), decay_rate, residue)


def per_device(projected, cotangent, short_filter, residue, decay_rate):
    n, m = lax.axis_size("ctx"), lax.axis_size("seq")
    tokens, upstream = projected[0], cotangent[0]
    block = min(tokens.shape[2], 512)
    known = local_part(n, tokens, upstream, decay_rate, residue, short_filter)
    gated, grad_tokens, sums = finish(tokens, upstream, *known, block)
    return gated[None], grad_tokens[None], *total_sums(n, m, sums, decay_rate, residue)


def solution(mesh):
    placed = (P("seq", None, "ctx", None), P("seq", "ctx", None), P(), P(), P())
    return jax.shard_map(
        per_device,
        mesh=mesh,
        in_specs=placed,
        out_specs=(P("seq", "ctx", None), P("seq", None, "ctx", None), P(), P(), P()),
        check_vma=False,
    )
```

```python
from functools import partial

import jax
import jax.numpy as jnp
from jax import lax
from jax.experimental import pallas as pl
from jax.experimental.pallas import tpu as pltpu
from jax.sharding import PartitionSpec as P

GROUP = 16
MODES = 16
TAPS = 7
LANES = 128
TILE_GROUPS = LANES // GROUP
ROWS = 128
F32, BF16 = jnp.float32, jnp.bfloat16
MESH = pl.DeviceIdType.MESH

HALF = ROWS // 2
QUARTER = ROWS // 4
GROUPED = 4
WAYS = 2

DECAY, RESIDUE, SHORT, TABLE_ROWS = 0, 16, 32, 56
SUM_ROWS = 64


def split(value):
    high = value.astype(BF16)
    return high, (value - high.astype(F32)).astype(BF16)


def iota(shape, dim):
    return lax.broadcasted_iota(jnp.int32, shape, dim)


def dot(left, right):
    return jnp.dot(left, right, preferred_element_type=F32)


def in_group(rows, width, group):
    return (iota((rows, width), 1) % LANES) // GROUP == group


def flip_matrix():
    return (iota((ROWS, ROWS), 0) + iota((ROWS, ROWS), 1) == ROWS - 1).astype(BF16)


def load_tokens(pad, proj_ref, before_ref, lanes):
    for i in range(3):
        pad[i, 0:8, :] = before_ref[i, :, lanes]
        pad[i, 8 : 8 + ROWS, :] = proj_ref[i, :, lanes].astype(F32)


def feature(pad, taps, i, start, count):
    total = None
    for j in range(TAPS):
        term = taps[TAPS * i + j] * pad[i, 8 + start - j : 8 + start - j + count, :]
        total = term if total is None else total + term
    return total


def tap_rows(wide_ref, lanes):
    return [wide_ref[SHORT + k : SHORT + k + 1, lanes] for k in range(3 * TAPS)]


def expand_table(wide_ref, small, decay_ref, residue_ref, short_ref):
    small[DECAY : DECAY + MODES, :] = decay_ref[...]
    small[RESIDUE : RESIDUE + MODES, :] = residue_ref[...]
    for i in range(3):
        small[SHORT + TAPS * i : SHORT + TAPS * (i + 1), :] = short_ref[i]
    used = SHORT + 3 * TAPS
    groups = small.shape[1]
    small[used:TABLE_ROWS, :] = jnp.zeros((TABLE_ROWS - used, groups), F32)
    value = small[...]
    high = value.astype(BF16).astype(F32)
    middle = (value - high).astype(BF16).astype(F32)
    low = value - high - middle
    pieces = jnp.concatenate([high, middle, low], axis=0).astype(BF16)
    width = min(1024, wide_ref.shape[1])
    for start in range(0, wide_ref.shape[1], width):
        owner = (iota((groups, width), 1) + start) // GROUP
        spread = (iota((groups, width), 0) == owner).astype(F32).astype(BF16)
        got = dot(pieces, spread)
        wide_ref[:, start : start + width] = got[0:TABLE_ROWS] + (
            got[TABLE_ROWS : 2 * TABLE_ROWS] + got[2 * TABLE_ROWS :]
        )


def lanes_of(tile):
    return pl.ds(pl.multiple_of(tile * LANES, LANES), LANES)


def select_groups(source, begin, count, rows, columns):
    total = source[begin + rows.start : begin + rows.stop, columns]
    for g in range(1, TILE_GROUPS):
        at = begin + g * count
        total = jnp.where(
            in_group(rows.stop - rows.start, columns.stop - columns.start, g),
            source[at + rows.start : at + rows.stop, columns],
            total,
        )
    return total


def local_kernel(
    n, proj_hbm, cot_hbm, decay_ref, residue_ref, short_ref,
    wide_ref, before_ref, after_ref, ends_ref, local_ref, near_hbm, into_ref, feat_hbm,
    proj_ref, cot_ref, near_ref, feat_ref, small, out_f, out_b, got_f, got_b, got, back, tables, streams, pad, parts, *scratch,
):
    left_pairs, right_pairs, pair_sums = (scratch[k * WAYS : (k + 1) * WAYS] for k in range(3))
    scratch = scratch[3 * WAYS :]
    rights, products, products_low = (scratch[k * GROUPED : (k + 1) * GROUPED] for k in range(3))
    local_sem, halo_send, halo_recv, s_out, r_out, s_in, r_in = scratch[3 * GROUPED :]
    me = lax.axis_index("ctx")
    right_dev, left_dev = lax.rem(me + 1, n), lax.rem(me + n - 1, n)
    far_back = (LANES - 1 - iota((MODES, LANES), 1)).astype(F32)

    def peer_of(k):
        return lax.rem(me + k, n)

    def each(action):
        def run(k, carry):
            action(k)
            return carry

        lax.fori_loop(1, n, run, 0)

    def remote(source, target, send_sem, recv_sem, to):
        return pltpu.make_async_remote_copy(
            src_ref=source,
            dst_ref=target,
            send_sem=send_sem,
            recv_sem=recv_sem,
            device_id={"ctx": to},
            device_id_type=MESH,
        )

    loads = [
        pltpu.make_async_copy(proj_hbm, proj_ref, local_sem.at[0]),
        pltpu.make_async_copy(cot_hbm, cot_ref, local_sem.at[1]),
    ]
    stores = [
        pltpu.make_async_copy(near_ref, near_hbm, local_sem.at[2]),
        pltpu.make_async_copy(feat_ref, feat_hbm, local_sem.at[3]),
    ]
    for copy in loads:
        copy.start()
    barrier = pltpu.get_barrier_semaphore()
    each(
        lambda k: pl.semaphore_signal(
            barrier, inc=1, device_id={"ctx": peer_of(k)}, device_id_type=MESH
        )
    )
    expand_table(wide_ref, small, decay_ref, residue_ref, short_ref)
    for copy in loads:
        copy.wait()
    width = out_f.shape[2]
    for i in range(3):
        tail = proj_ref[i, ROWS - 16 : ROWS, :].astype(F32)[8:16]
        out_f[i] = jnp.concatenate([tail[:, :width], tail[:, width:]], axis=0).astype(BF16)
    for i in range(4):
        head = (cot_ref[0:16, :] if i == 3 else proj_ref[i, 0:16, :]).astype(F32)[0:8]
        out_b[i] = jnp.concatenate([head[:, :width], head[:, width:]], axis=0).astype(BF16)
    pl.semaphore_wait(barrier, n - 1)
    halo = [
        remote(out_f, got_f, halo_send.at[0], halo_recv.at[0], right_dev),
        remote(out_b, got_b, halo_send.at[1], halo_recv.at[1], left_dev),
    ]
    for copy in halo:
        copy.start()

    def power_of(tile, g):
        column = GROUP * g
        decay = wide_ref[DECAY : DECAY + MODES, lanes_of(tile)]
        return jnp.exp(-decay[:, column : column + 1] * far_back)

    def store_table(tile, at, value):
        high, low = split(value)
        tables[tile, at, 0:LANES] = high
        tables[tile, at, LANES : 2 * LANES] = low
        tables[tile, at, 2 * LANES : 3 * LANES] = high

    def build_tables(tile, carry):
        residue = wide_ref[RESIDUE : RESIDUE + MODES, lanes_of(tile)]
        for g in range(TILE_GROUPS):
            column = GROUP * g
            power = power_of(tile, g)
            filter_row = jnp.sum(residue[:, column : column + 1] * power, axis=0, keepdims=True)
            base = pltpu.roll(
                jnp.broadcast_to(filter_row, (8, LANES)), 1, 1, stride=1, stride_axis=0
            )
            for q in range(HALF, ROWS, 16):
                block = jnp.concatenate(
                    [pltpu.roll(base, q, 1), pltpu.roll(base, q + 8, 1)], axis=0
                )
                keep = iota((16, LANES), 1) <= iota((16, LANES), 0) + q
                begin = HALF * g + q - HALF
                store_table(tile, slice(begin, begin + 16), jnp.where(keep, block, 0.0))
            for k, value in enumerate((power, far_back * power)):
                begin = TILE_GROUPS * (HALF + k * MODES) + MODES * g
                store_table(tile, slice(begin, begin + MODES), value)
        return carry

    lax.fori_loop(0, n, build_tables, 0)
    for way in range(GROUPED):
        for k in range(3):
            begin = ROWS * k
            rights[way][begin : begin + HALF, 2 * LANES : 4 * LANES] = jnp.zeros(
                (HALF, 2 * LANES), BF16
            )
    for way in range(WAYS):
        right_pairs[way][...] = jnp.zeros((2 * ROWS, 8 * LANES), BF16)

    for copy in halo:
        copy.wait()
    first, last = me == 0, me == n - 1
    for i in range(3):
        part = jnp.where(first, 0.0, got_f[i].astype(F32))
        before_ref[i, :, 0:width] = part[0:8]
        before_ref[i, :, width : 2 * width] = part[8:16]
    for i in range(4):
        part = jnp.where(last, 0.0, got_b[i].astype(F32))
        after_ref[i, :, 0:width] = part[0:8]
        after_ref[i, :, width : 2 * width] = part[8:16]

    def features(tile, way):
        lanes = lanes_of(tile)
        load_tokens(pad, proj_ref, before_ref, lanes)
        taps = tap_rows(wide_ref, lanes)
        step = 32
        for start in range(0, ROWS, step):
            rows = slice(start, start + step)
            f = [feature(pad, taps, i, start, step) for i in range(3)]
            for i in range(3):
                feat_ref[i, rows, lanes] = f[i]
            high, low = split(f[1] * f[2])
            streams[tile, rows, 0:LANES] = high
            streams[tile, rows, LANES : 2 * LANES] = low
            for k, value in enumerate((high, high, low)):
                begin = ROWS * k + start
                rights[way][begin : begin + step, 0:LANES] = value
                if start < HALF:
                    begin = begin + HALF
                    rights[way][begin : begin + step, 2 * LANES : 3 * LANES] = value
            high, low = split(cot_ref[rows, lanes].astype(F32) * f[0])
            begin = 2 * LANES * way
            parts[rows, begin : begin + LANES] = high
            parts[rows, begin + LANES : begin + 2 * LANES] = low

    def place(tile, way, flipped):
        streams[tile, :, 2 * LANES : 4 * LANES] = flipped
        for k, column in enumerate((0, 0, LANES)):
            value = flipped[:, column : column + LANES]
            begin = ROWS * k
            rights[way][begin : begin + ROWS, LANES : 2 * LANES] = value
            rights[way][begin + HALF : begin + ROWS, 3 * LANES : 4 * LANES] = value[0:HALF]

    modes, both = slice(0, MODES), slice(0, 2 * LANES)

    def send_out(k):
        return remote(
            ends_ref.at[peer_of(k)], got.at[me], s_out.at[k], r_out.at[me], peer_of(k)
        )

    def begin_tiles(step, carry):
        ks = [step * GROUPED + way for way in range(GROUPED)]
        for way, k in enumerate(ks):
            features(peer_of(k), way)
        flipped = dot(flip_matrix(), parts[...]).astype(BF16)
        for way, k in enumerate(ks):
            place(peer_of(k), way, flipped[:, 2 * LANES * way : 2 * LANES * (way + 1)])
        for way, k in enumerate(ks):
            tile = peer_of(k)
            products[way][...] = dot(tables[tile], rights[way][:, 0 : 2 * LANES])
            products_low[way][...] = dot(
                tables[tile, 0 : TILE_GROUPS * HALF, :], rights[way][:, 2 * LANES : 4 * LANES]
            )
        for way, k in enumerate(ks):
            tile = peer_of(k)
            first_end = TILE_GROUPS * HALF
            ends = select_groups(products[way], first_end, MODES, modes, both)
            ends_ref[tile, 0:MODES, :] = ends[:, 0:LANES]
            ends_ref[tile, MODES : 2 * MODES, :] = ends[:, LANES : 2 * LANES]
            first_lag = first_end + TILE_GROUPS * MODES
            lags = select_groups(products[way], first_lag, MODES, modes, both)
            local_ref[tile, 0:MODES, :] = lags[:, 0:LANES]
            local_ref[tile, MODES : 2 * MODES, :] = lags[:, LANES : 2 * LANES]
            for start in range(0, ROWS, 32):
                source = products[way] if start >= HALF else products_low[way]
                begin = start % HALF
                near = select_groups(source, 0, HALF, slice(begin, begin + 32), both)
                near_ref[0, start : start + 32, lanes_of(tile)] = near[:, 0:LANES]
                near_ref[1, start : start + 32, lanes_of(tile)] = near[:, LANES : 2 * LANES]
        for k in ks:

            @pl.when(k != 0)
            def _():
                send_out(k).start()

        return carry

    lax.fori_loop(0, n // GROUPED, begin_tiles, 0)
    for copy in stores:
        copy.start()

    lane = iota((MODES, LANES), 1)

    def correlate(step, carry):
        tiles = [step * WAYS + way for way in range(WAYS)]
        for way, tile in enumerate(tiles):
            for h in range(4):
                at = slice(QUARTER * h, QUARTER * (h + 1))
                columns = slice(2 * LANES * h, 2 * LANES * (h + 1))
                flipped = streams[tile, at, 2 * LANES : 4 * LANES]
                for g in range(TILE_GROUPS):
                    left_pairs[way][QUARTER * g : QUARTER * (g + 1), columns] = jnp.where(
                        in_group(QUARTER, 2 * LANES, g), flipped, jnp.zeros_like(flipped)
                    )
                keep = ROWS - QUARTER * h
                for k in range(2):
                    value = streams[tile, 0:keep, LANES * k : LANES * (k + 1)]
                    at = slice(ROWS * (k + 1) - keep, ROWS * (k + 1))
                    for column in (2 * LANES * h, 2 * LANES * h + LANES):
                        right_pairs[way][at, column : column + LANES] = value
        for way in range(WAYS):
            pair_sums[way][...] = lax.dot_general(
                left_pairs[way][...],
                right_pairs[way][...],
                (((1,), (1,)), ((), ())),
                preferred_element_type=F32,
            )
        for way, tile in enumerate(tiles):
            res_sum = jnp.zeros((MODES, LANES), F32)
            lag_sum = jnp.zeros((MODES, LANES), F32)
            for g in range(TILE_GROUPS):
                total = None
                for q in range(0, QUARTER, 8):
                    at = slice(QUARTER * g + q, QUARTER * g + q + 8)
                    block = pair_sums[way][at, 0:LANES] + pair_sums[way][at, LANES : 2 * LANES]
                    keep = iota((8, LANES), 1) + iota((8, LANES), 0) <= ROWS - 1 - q
                    block = jnp.where(keep, block, 0.0)
                    if q:
                        block = pltpu.roll(block, q, 1)
                    total = block if total is None else total + block
                by_lag = jnp.sum(
                    pltpu.roll(total, 0, 1, stride=1, stride_axis=0), axis=0, keepdims=True
                )
                weighted = power_of(tile, g) * by_lag
                res_sum = jnp.where(
                    lane == GROUP * g, jnp.sum(weighted, axis=1, keepdims=True), res_sum
                )
                lag_sum = jnp.where(
                    lane == GROUP * g,
                    jnp.sum(far_back * weighted, axis=1, keepdims=True),
                    lag_sum,
                )
            local_ref[tile, 2 * MODES : 3 * MODES, :] = res_sum
            local_ref[tile, 3 * MODES : 4 * MODES, :] = lag_sum
        return carry

    lax.fori_loop(0, n // WAYS // 2, correlate, 0)

    def receive_out(k):
        source = lax.rem(me + n - k, n)
        return remote(ends_ref.at[source], got.at[source], s_out.at[k], r_out.at[source], source)

    def send_in(k):
        return remote(back.at[peer_of(k)], into_ref.at[me], s_in.at[k], r_in.at[me], peer_of(k))

    def receive_in(k):
        source = lax.rem(me + n - k, n)
        return remote(back.at[source], into_ref.at[source], s_in.at[k], r_in.at[source], source)

    got[me] = ends_ref[me]
    each(lambda k: receive_out(k).wait_recv())
    decay = wide_ref[DECAY : DECAY + MODES, lanes_of(me)]
    pole = jnp.exp(-decay)
    whole = jnp.exp(-decay * float(ROWS))
    zero = jnp.zeros((MODES, LANES), F32)

    def scan(step, carry):
        state, lagged, res, lag, beyond = carry
        for k in range(2):
            d = step * 2 + k
            adjoint = got[d, MODES : 2 * MODES, :]
            back[d, 0:MODES, :] = state
            res = res + adjoint * state
            lag = lag + adjoint * (state + float(ROWS) * lagged)
            state, lagged = whole * state + got[d, 0:MODES, :], whole * (lagged + state)
            d = n - 1 - d
            back[d, MODES : 2 * MODES, :] = beyond
            beyond = whole * beyond + got[d, MODES : 2 * MODES, :]
        return state, lagged, res, lag, beyond

    _, _, cross_res, cross_lag, _ = lax.fori_loop(0, n // 2, scan, (zero,) * 5)
    each(lambda k: send_in(k).start())
    into_ref[me] = back[me]

    lax.fori_loop(n // WAYS // 2, n // WAYS, correlate, 0)
    local_ref[me, 2 * MODES : 3 * MODES, :] = (
        local_ref[me, 2 * MODES : 3 * MODES, :] + pole * cross_res
    )
    local_ref[me, 3 * MODES : 4 * MODES, :] = (
        local_ref[me, 3 * MODES : 4 * MODES, :] + pole * cross_lag
    )
    each(lambda k: receive_in(k).wait_recv())
    each(lambda k: send_out(k).wait_send())
    each(lambda k: send_in(k).wait_send())
    for copy in stores:
        copy.wait()


def local_part(n, tokens, cotangent, decay_rate, residue, short_filter):
    channels = tokens.shape[2]
    groups = residue.shape[1]
    half = channels // 2
    vmem = pl.BlockSpec(memory_space=pltpu.VMEM)
    wide_rows = TILE_GROUPS * (HALF + 2 * MODES)
    return pl.pallas_call(
        partial(local_kernel, n),
        in_specs=[pl.BlockSpec(memory_space=pl.ANY)] * 2 + [vmem] * 3,
        out_specs=[vmem] * 5 + [pl.BlockSpec(memory_space=pl.ANY), vmem]
        + [pl.BlockSpec(memory_space=pl.ANY)],
        out_shape=[
            jax.ShapeDtypeStruct(shape, F32)
            for shape in (
                (TABLE_ROWS, channels),
                (3, 8, channels),
                (4, 8, channels),
                (n, 2 * MODES, LANES),
                (n, 4 * MODES, LANES),
                (2, ROWS, channels),
                (n, 2 * MODES, LANES),
                (3, ROWS, channels),
            )
        ],
        scratch_shapes=[
            pltpu.VMEM((3, ROWS, channels), BF16),
            pltpu.VMEM((ROWS, channels), BF16),
            pltpu.VMEM((2, ROWS, channels), F32),
            pltpu.VMEM((3, ROWS, channels), F32),
            pltpu.VMEM((TABLE_ROWS, groups), F32),
            pltpu.VMEM((3, 16, half), BF16),
            pltpu.VMEM((4, 16, half), BF16),
            pltpu.VMEM((3, 16, half), BF16),
            pltpu.VMEM((4, 16, half), BF16),
            pltpu.VMEM((n, 2 * MODES, LANES), F32),
            pltpu.VMEM((n, 2 * MODES, LANES), F32),
            pltpu.VMEM((n, wide_rows, 3 * LANES), BF16),
            pltpu.VMEM((n, ROWS, 4 * LANES), BF16),
            pltpu.VMEM((3, ROWS + 8, LANES), F32),
            pltpu.VMEM((ROWS, 2 * LANES * GROUPED), BF16),
        ]
        + [pltpu.VMEM((TILE_GROUPS * QUARTER, 8 * LANES), BF16)] * WAYS
        + [pltpu.VMEM((2 * ROWS, 8 * LANES), BF16)] * WAYS
        + [pltpu.VMEM((TILE_GROUPS * QUARTER, 2 * LANES), F32)] * WAYS
        + [pltpu.VMEM((3 * ROWS, 4 * LANES), BF16)] * GROUPED
        + [pltpu.VMEM((wide_rows, 2 * LANES), F32)] * GROUPED
        + [pltpu.VMEM((TILE_GROUPS * HALF, 2 * LANES), F32)] * GROUPED
        + [pltpu.SemaphoreType.DMA((4,))]
        + [pltpu.SemaphoreType.DMA((2,))] * 2
        + [pltpu.SemaphoreType.DMA((n,))] * 4,
        compiler_params=pltpu.CompilerParams(
            collective_id=0, has_side_effects=True, vmem_limit_bytes=60 * 2**20
        ),
        name="local",
    )(tokens, cotangent, decay_rate, residue, short_filter)


def finish_kernel(
    tiles, proj_ref, cot_ref, before_ref, after_ref, wide_ref, ends_ref, local_ref,
    near_ref, into_ref, feat_ref, gated_ref, grad_ref, sums_ref,
    pads, grads, lefts, rights, fars, sums, placed,
):
    step_index = pl.program_id(0)

    def spans(tile):
        return slice(tile * LANES, (tile + 1) * LANES)

    for tile in range(tiles):
        lanes = spans(tile)
        pad = pads.at[tile]
        load_tokens(pad, proj_ref, before_ref, lanes)
        for i in range(3):
            pad[i, 8 + ROWS : 16 + ROWS, :] = after_ref[i, :, lanes]
        pick = iota((MODES, LANES), 1) % MODES == iota((MODES, LANES), 0)

        def across(row):
            block = wide_ref[row : row + MODES, lanes]
            return jnp.sum(jnp.where(pick, block, 0.0), axis=0, keepdims=True)

        ahead = (iota((ROWS, LANES), 0) + 1).astype(F32)
        high, low = split(across(RESIDUE) * jnp.exp(-across(DECAY) * ahead))
        lefts[tile, :, 0:LANES] = high
        lefts[tile, :, LANES : 2 * LANES] = low
        lefts[tile, :, 2 * LANES : 3 * LANES] = high
        high, low = split(
            jnp.concatenate(
                [into_ref[tile, 0:MODES, :], into_ref[tile, MODES : 2 * MODES, :]], axis=1
            )
        )
        for g in range(TILE_GROUPS):
            keep = in_group(MODES, 2 * LANES, g)
            chosen = jnp.where(keep, high, jnp.zeros_like(high))
            begin = MODES * g
            rights[tile, begin : begin + MODES, :] = chosen
            rights[tile, ROWS + begin : ROWS + begin + MODES, :] = chosen
            rights[tile, 2 * ROWS + begin : 2 * ROWS + begin + MODES, :] = jnp.where(
                keep, low, jnp.zeros_like(low)
            )
    for tile in range(tiles):
        fars[tile] = dot(lefts[tile], rights[tile])
    for tile in range(tiles):
        lanes = spans(tile)
        long_conv = near_ref[0, :, lanes] + fars[tile, :, 0:LANES]
        for start in range(0, ROWS, 8):
            rows = slice(start, start + 8)
            value = near_ref[1, rows, lanes] + fars[tile, rows, LANES : 2 * LANES]
            turned = jnp.take_along_axis(value, 7 - iota((8, LANES), 0), axis=0)
            at = slice(ROWS - 8 - start, ROWS - start)
            grads[tile, 1, at, :] = turned * feat_ref[2, at, lanes]
            grads[tile, 2, at, :] = turned * feat_ref[1, at, lanes]
        gated_ref[:, lanes] = (feat_ref[0, :, lanes] * long_conv).astype(BF16)
        grads[tile, 0, 0:ROWS, :] = cot_ref[:, lanes].astype(F32) * long_conv
    for tile in range(tiles):
        lanes = spans(tile)
        pad = pads.at[tile]
        grad = grads.at[tile]
        taps = tap_rows(wide_ref, lanes)
        decay = wide_ref[DECAY : DECAY + MODES, lanes]
        residue = wide_ref[RESIDUE : RESIDUE + MODES, lanes]
        state = into_ref[tile, 0:MODES, :]
        adjoint = into_ref[tile, MODES : 2 * MODES, :]

        pole = jnp.exp(-decay)
        inverse = jnp.exp(decay)
        next_feat = [feature(pad, taps, i, ROWS, 8) for i in range(3)]
        next_cot = after_ref[3, :, lanes]
        next_in = next_feat[1] * next_feat[2]
        next_grad = next_cot * next_feat[0]
        whole = jnp.exp(-decay * float(ROWS))
        behind = residue * pole * (whole * state + ends_ref[tile, 0:MODES, :])
        beyond = residue * adjoint
        lag_pos = residue
        lag_neg = residue * inverse
        conv_rows, mixer_rows, filters, filters_neg = [], [], [], []
        for k in range(TAPS - 1):
            filters.append(jnp.sum(lag_pos, axis=0, keepdims=True))
            filters_neg.append(jnp.sum(lag_neg, axis=0, keepdims=True))
            conv = jnp.sum(behind, axis=0, keepdims=True)
            mixer = jnp.sum(beyond, axis=0, keepdims=True)
            for j in range(k + 1):
                conv = conv + filters[k - j] * next_in[j : j + 1]
            for j in range(k):
                mixer = mixer - filters_neg[k - j - 1] * next_grad[j : j + 1]
            conv_rows.append(conv)
            mixer_rows.append(mixer)
            lag_pos, lag_neg = lag_pos * pole, lag_neg * inverse
            behind, beyond = behind * pole, beyond * inverse
        blank = jnp.zeros((8 - (TAPS - 1), LANES), F32)
        next_conv = jnp.concatenate(conv_rows + [blank], axis=0)
        next_mixer = jnp.concatenate(mixer_rows + [blank], axis=0)
        grad[0, ROWS : ROWS + 8, :] = next_cot * next_conv
        grad[1, ROWS : ROWS + 8, :] = next_mixer * next_feat[2]
        grad[2, ROWS : ROWS + 8, :] = next_mixer * next_feat[1]

        step = 32
        short = []
        for i in range(3):
            totals = [None] * TAPS
            for start in range(0, ROWS, step):
                rows = slice(start, start + step)
                own = pad[i, 8 + start : 8 + start + step, :]
                total = None
                for j in range(TAPS):
                    ahead_grad = grad[i, start + j : start + j + step, :]
                    term = taps[TAPS * i + j] * ahead_grad
                    total = term if total is None else total + term
                    product = own * ahead_grad
                    part = product[0:8]
                    for r in range(8, step, 8):
                        part = part + product[r : r + 8]
                    totals[j] = part if totals[j] is None else totals[j] + part
                grad_ref[i, rows, lanes] = total.astype(BF16)
            short += [jnp.sum(part, axis=0, keepdims=True) for part in totals]
        short.append(jnp.zeros((3, LANES), F32))
        lag_sum = local_ref[tile, 3 * MODES : 4 * MODES, :] + pole * (
            local_ref[tile, MODES : 2 * MODES, :] * state + local_ref[tile, 0:MODES, :] * adjoint
        )
        res_sum = local_ref[tile, 2 * MODES : 3 * MODES, :]
        rest = jnp.zeros((SUM_ROWS - TABLE_ROWS, LANES), F32)
        high, low = split(jnp.concatenate(short + [res_sum, lag_sum, rest], axis=0))
        at = slice(SUM_ROWS * tile, SUM_ROWS * (tile + 1))
        sums[at, 0:LANES] = high
        sums[at, LANES : 2 * LANES] = low

    member = (iota((2 * LANES, LANES), 0) % LANES) // GROUP == iota((2 * LANES, LANES), 1)
    by_group = dot(sums[...], member.astype(F32).astype(BF16))
    total = by_group[0:SUM_ROWS]
    for tile in range(1, tiles):
        part = by_group[SUM_ROWS * tile : SUM_ROWS * (tile + 1)]
        total = total + pltpu.roll(part, TILE_GROUPS * tile, 1)
    placed[step_index] = total

    @pl.when(step_index == pl.num_programs(0) - 1)
    def _():
        groups = sums_ref.shape[1]
        width = min(groups, LANES)
        stride = tiles * TILE_GROUPS
        for begin in range(0, groups, width):
            total = placed[begin // stride]
            for k in range(1, width // stride):
                total = total + pltpu.roll(placed[begin // stride + k], stride * k, 1)
            sums_ref[:, begin : begin + width] = total[:, 0:width]


def finish(tokens, cotangent, wide, before, after, ends, local, near, into, feats, block):
    channels = tokens.shape[2]
    tiles = block // LANES
    groups = channels // GROUP

    def per_tile(rows):
        return pl.BlockSpec((tiles, rows, LANES), lambda t: (t, 0, 0))

    def stack(k, rows):
        return pl.BlockSpec((k, rows, block), lambda t: (0, 0, t))

    plane = pl.BlockSpec((ROWS, block), lambda t: (0, t))
    return pl.pallas_call(
        partial(finish_kernel, tiles),
        grid=(channels // block,),
        in_specs=[
            stack(3, ROWS),
            plane,
            stack(3, 8),
            stack(4, 8),
            pl.BlockSpec((TABLE_ROWS, block), lambda t: (0, t)),
            per_tile(2 * MODES),
            per_tile(4 * MODES),
            stack(2, ROWS),
            per_tile(2 * MODES),
            stack(3, ROWS),
        ],
        out_specs=[plane, stack(3, ROWS), pl.BlockSpec((SUM_ROWS, groups), lambda t: (0, 0))],
        out_shape=[
            jax.ShapeDtypeStruct((ROWS, channels), BF16),
            jax.ShapeDtypeStruct((3, ROWS, channels), BF16),
            jax.ShapeDtypeStruct((SUM_ROWS, groups), F32),
        ],
        scratch_shapes=[
            pltpu.VMEM((tiles, 3, ROWS + 16, LANES), F32),
            pltpu.VMEM((tiles, 3, ROWS + 8, LANES), F32),
            pltpu.VMEM((tiles, ROWS, 3 * LANES), BF16),
            pltpu.VMEM((tiles, 3 * ROWS, 2 * LANES), BF16),
            pltpu.VMEM((tiles, ROWS, 2 * LANES), F32),
            pltpu.VMEM((tiles * SUM_ROWS, 2 * LANES), BF16),
            pltpu.VMEM((channels // block, SUM_ROWS, LANES), F32),
        ],
        compiler_params=pltpu.CompilerParams(vmem_limit_bytes=62 * 2**20),
        name="finish",
    )(tokens, cotangent, before, after, wide, ends, local, near, into, feats)


def total_kernel(
    n, m, nx, ny, part_ref, decay_ref, residue_ref, short_ref, res_ref, log_ref,
    got, mine_sum, rows, full, s_a, r_a, s_b, r_b, s_c, r_c,
):
    me, genome = lax.axis_index("ctx"), lax.axis_index("seq")
    x, y, z = lax.rem(me, nx), lax.rem(lax.div(me, nx), ny), lax.div(me, nx * ny)
    a, b = ny * m, n // ny
    my_a, my_b = y * m + genome, z * nx + x

    def id_a(k):
        return {"ctx": (z * ny + lax.div(k, m)) * nx + x, "seq": lax.rem(k, m)}

    def id_b(k):
        return {"ctx": (lax.div(k, nx) * ny + y) * nx + lax.rem(k, nx), "seq": genome}

    def ahead(mine, count, k):
        return lax.rem(mine + k, count)

    def behind(mine, count, k):
        return lax.rem(mine + count - k, count)

    def each(count, action):
        def run(k, carry):
            action(k)
            return carry

        lax.fori_loop(1, count, run, 0)

    def remote(source, target, send_sem, recv_sem, to):
        return pltpu.make_async_remote_copy(
            src_ref=source,
            dst_ref=target,
            send_sem=send_sem,
            recv_sem=recv_sem,
            device_id=to,
            device_id_type=MESH,
        )

    barrier = pltpu.get_barrier_semaphore()

    def greet(to):
        pl.semaphore_signal(barrier, inc=1, device_id=to, device_id_type=MESH)

    each(a, lambda k: greet(id_a(ahead(my_a, a, k))))
    each(b, lambda k: greet(id_b(ahead(my_b, b, k))))
    got[my_a] = part_ref[my_a]
    pl.semaphore_wait(barrier, a - 1 + b - 1)

    def first(k, to, slot):
        return remote(part_ref.at[to], got.at[slot], s_a.at[k], r_a.at[slot], id_a(to))

    def second(k, to, slot):
        return remote(mine_sum, rows.at[slot], s_b.at[k], r_b.at[slot], id_b(to))

    def third(k, to, slot):
        return remote(full.at[my_a], full.at[slot], s_c.at[k], r_c.at[slot], id_a(to))

    def start(mine, count, copy):
        each(count, lambda k: copy(k, ahead(mine, count, k), mine).start())

    def arrive(mine, count, copy):
        each(
            count,
            lambda k: copy(k, behind(mine, count, k), behind(mine, count, k)).wait_recv(),
        )

    def sent(mine, count, copy):
        each(count, lambda k: copy(k, ahead(mine, count, k), mine).wait_send())

    start(my_a, a, first)
    arrive(my_a, a, first)
    total = got[0]
    for d in range(1, a):
        total = total + got[d]
    mine_sum[...] = total
    rows[my_b] = total
    start(my_b, b, second)
    arrive(my_b, b, second)
    total = rows[0]
    for d in range(1, b):
        total = total + rows[d]
    full[my_a] = total
    start(my_a, a, third)
    arrive(my_a, a, third)
    share = full.shape[1]
    sums = jnp.concatenate([full[k // share, k % share] for k in range(TABLE_ROWS // 8)], axis=0)
    sums = sums * (1.0 / float(ROWS * n * m))
    for i in range(3):
        short_ref[i] = sums[TAPS * i : TAPS * (i + 1)]
    res_ref[...] = sums[24 : 24 + MODES]
    log_ref[...] = -residue_ref[...] * decay_ref[...] * sums[40 : 40 + MODES]
    sent(my_a, a, first)
    sent(my_b, b, second)
    sent(my_a, a, third)


def total_sums(n, m, parts, decay_rate, residue):
    ny = 2
    nx = min(4, n // ny)
    a, b = ny * m, n // ny
    share, groups = SUM_ROWS // 8 // a, parts.shape[1]
    vmem = pl.BlockSpec(memory_space=pltpu.VMEM)
    dma = pltpu.SemaphoreType.DMA
    return pl.pallas_call(
        partial(total_kernel, n, m, nx, ny),
        out_shape=[
            jax.ShapeDtypeStruct((3, TAPS, groups), F32),
            jax.ShapeDtypeStruct((MODES, groups), F32),
            jax.ShapeDtypeStruct((MODES, groups), F32),
        ],
        in_specs=[vmem] * 3,
        out_specs=[vmem] * 3,
        scratch_shapes=[
            pltpu.VMEM((a, share, 8, groups), F32),
            pltpu.VMEM((share, 8, groups), F32),
            pltpu.VMEM((b, share, 8, groups), F32),
            pltpu.VMEM((a, share, 8, groups), F32),
            dma((a,)),
            dma((a,)),
            dma((b,)),
            dma((b,)),
            dma((a,)),
            dma((a,)),
        ],
        compiler_params=pltpu.CompilerParams(
            collective_id=1, has_side_effects=True, vmem_limit_bytes=16 * 2**20
        ),
        name="totals",
    )(parts.reshape(a, share, 8, groups), decay_rate, residue)


def per_device(projected, cotangent, short_filter, residue, decay_rate):
    n, m = lax.axis_size("ctx"), lax.axis_size("seq")
    tokens, upstream = projected[0], cotangent[0]
    block = min(tokens.shape[2], 512)
    known = local_part(n, tokens, upstream, decay_rate, residue, short_filter)
    gated, grad_tokens, sums = finish(tokens, upstream, *known, block)
    return gated[None], grad_tokens[None], *total_sums(n, m, sums, decay_rate, residue)


def solution(mesh):
    placed = (P("seq", None, "ctx", None), P("seq", "ctx", None), P(), P(), P())
    return jax.shard_map(
        per_device,
        mesh=mesh,
        in_specs=placed,
        out_specs=(P("seq", "ctx", None), P("seq", None, "ctx", None), P(), P(), P()),
        check_vma=False,
    )
```

```python
from functools import partial

import jax
import jax.numpy as jnp
from jax import lax
from jax.experimental import pallas as pl
from jax.experimental.pallas import tpu as pltpu
from jax.sharding import PartitionSpec as P

GROUP = 16
MODES = 16
TAPS = 7
LANES = 128
TILE_GROUPS = LANES // GROUP
ROWS = 128
F32, BF16 = jnp.float32, jnp.bfloat16
MESH = pl.DeviceIdType.MESH

HALF = ROWS // 2
QUARTER = ROWS // 4
GROUPED = 4
WAYS = 2

DECAY, RESIDUE, SHORT, TABLE_ROWS = 0, 16, 32, 56
SUM_ROWS = 64


def split(value):
    high = value.astype(BF16)
    return high, (value - high.astype(F32)).astype(BF16)


def iota(shape, dim):
    return lax.broadcasted_iota(jnp.int32, shape, dim)


def dot(left, right):
    return jnp.dot(left, right, preferred_element_type=F32)


def in_group(rows, width, group):
    return (iota((rows, width), 1) % LANES) // GROUP == group


def flip_matrix():
    return (iota((ROWS, ROWS), 0) + iota((ROWS, ROWS), 1) == ROWS - 1).astype(BF16)


def load_tokens(pad, proj_ref, before_ref, lanes):
    for i in range(3):
        pad[i, 0:8, :] = before_ref[i, :, lanes]
        pad[i, 8 : 8 + ROWS, :] = proj_ref[i, :, lanes].astype(F32)


def feature(pad, taps, i, start, count):
    total = None
    for j in range(TAPS):
        term = taps[TAPS * i + j] * pad[i, 8 + start - j : 8 + start - j + count, :]
        total = term if total is None else total + term
    return total


def tap_rows(wide_ref, lanes):
    return [wide_ref[SHORT + k : SHORT + k + 1, lanes] for k in range(3 * TAPS)]


def expand_table(wide_ref, small, decay_ref, residue_ref, short_ref):
    small[DECAY : DECAY + MODES, :] = decay_ref[...]
    small[RESIDUE : RESIDUE + MODES, :] = residue_ref[...]
    for i in range(3):
        small[SHORT + TAPS * i : SHORT + TAPS * (i + 1), :] = short_ref[i]
    used = SHORT + 3 * TAPS
    groups = small.shape[1]
    small[used:TABLE_ROWS, :] = jnp.zeros((TABLE_ROWS - used, groups), F32)
    value = small[...]
    high = value.astype(BF16).astype(F32)
    middle = (value - high).astype(BF16).astype(F32)
    low = value - high - middle
    pieces = jnp.concatenate([high, middle, low], axis=0).astype(BF16)
    width = min(1024, wide_ref.shape[1])
    for start in range(0, wide_ref.shape[1], width):
        owner = (iota((groups, width), 1) + start) // GROUP
        spread = (iota((groups, width), 0) == owner).astype(F32).astype(BF16)
        got = dot(pieces, spread)
        wide_ref[:, start : start + width] = got[0:TABLE_ROWS] + (
            got[TABLE_ROWS : 2 * TABLE_ROWS] + got[2 * TABLE_ROWS :]
        )


def lanes_of(tile):
    return pl.ds(pl.multiple_of(tile * LANES, LANES), LANES)


def select_groups(source, begin, count, rows, columns):
    total = source[begin + rows.start : begin + rows.stop, columns]
    for g in range(1, TILE_GROUPS):
        at = begin + g * count
        total = jnp.where(
            in_group(rows.stop - rows.start, columns.stop - columns.start, g),
            source[at + rows.start : at + rows.stop, columns],
            total,
        )
    return total


def local_kernel(
    n, proj_hbm, cot_hbm, decay_ref, residue_ref, short_ref,
    wide_ref, before_ref, after_ref, ends_ref, local_ref, near_hbm, into_ref, feat_hbm,
    proj_ref, cot_ref, near_ref, feat_ref, small, out_f, out_b, got_f, got_b, got, back, tables, streams, pad, parts, *scratch,
):
    left_pairs, right_pairs, pair_sums = (scratch[k * WAYS : (k + 1) * WAYS] for k in range(3))
    scratch = scratch[3 * WAYS :]
    rights, products, products_low = (scratch[k * GROUPED : (k + 1) * GROUPED] for k in range(3))
    local_sem, halo_send, halo_recv, s_out, r_out, s_in, r_in = scratch[3 * GROUPED :]
    me = lax.axis_index("ctx")
    right_dev, left_dev = lax.rem(me + 1, n), lax.rem(me + n - 1, n)
    far_back = (LANES - 1 - iota((MODES, LANES), 1)).astype(F32)

    def peer_of(k):
        return lax.rem(me + k, n)

    def each(action):
        def run(k, carry):
            action(k)
            return carry

        lax.fori_loop(1, n, run, 0)

    def remote(source, target, send_sem, recv_sem, to):
        return pltpu.make_async_remote_copy(
            src_ref=source,
            dst_ref=target,
            send_sem=send_sem,
            recv_sem=recv_sem,
            device_id={"ctx": to},
            device_id_type=MESH,
        )

    loads = [
        pltpu.make_async_copy(proj_hbm, proj_ref, local_sem.at[0]),
        pltpu.make_async_copy(cot_hbm, cot_ref, local_sem.at[1]),
    ]
    stores = [
        pltpu.make_async_copy(near_ref, near_hbm, local_sem.at[2]),
        pltpu.make_async_copy(feat_ref, feat_hbm, local_sem.at[3]),
    ]
    for copy in loads:
        copy.start()
    barrier = pltpu.get_barrier_semaphore()
    each(
        lambda k: pl.semaphore_signal(
            barrier, inc=1, device_id={"ctx": peer_of(k)}, device_id_type=MESH
        )
    )
    expand_table(wide_ref, small, decay_ref, residue_ref, short_ref)
    for copy in loads:
        copy.wait()
    width = out_f.shape[2]
    for i in range(3):
        tail = proj_ref[i, ROWS - 16 : ROWS, :].astype(F32)[8:16]
        out_f[i] = jnp.concatenate([tail[:, :width], tail[:, width:]], axis=0).astype(BF16)
    for i in range(4):
        head = (cot_ref[0:16, :] if i == 3 else proj_ref[i, 0:16, :]).astype(F32)[0:8]
        out_b[i] = jnp.concatenate([head[:, :width], head[:, width:]], axis=0).astype(BF16)
    pl.semaphore_wait(barrier, n - 1)
    halo = [
        remote(out_f, got_f, halo_send.at[0], halo_recv.at[0], right_dev),
        remote(out_b, got_b, halo_send.at[1], halo_recv.at[1], left_dev),
    ]
    for copy in halo:
        copy.start()

    def power_of(tile, g):
        column = GROUP * g
        decay = wide_ref[DECAY : DECAY + MODES, lanes_of(tile)]
        return jnp.exp(-decay[:, column : column + 1] * far_back)

    def store_table(tile, at, value):
        high, low = split(value)
        tables[tile, at, 0:LANES] = high
        tables[tile, at, LANES : 2 * LANES] = low
        tables[tile, at, 2 * LANES : 3 * LANES] = high

    def build_tables(tile, carry):
        residue = wide_ref[RESIDUE : RESIDUE + MODES, lanes_of(tile)]
        for g in range(TILE_GROUPS):
            column = GROUP * g
            power = power_of(tile, g)
            filter_row = jnp.sum(residue[:, column : column + 1] * power, axis=0, keepdims=True)
            base = pltpu.roll(
                jnp.broadcast_to(filter_row, (8, LANES)), 1, 1, stride=1, stride_axis=0
            )
            for q in range(HALF, ROWS, 16):
                block = jnp.concatenate(
                    [pltpu.roll(base, q, 1), pltpu.roll(base, q + 8, 1)], axis=0
                )
                keep = iota((16, LANES), 1) <= iota((16, LANES), 0) + q
                begin = HALF * g + q - HALF
                store_table(tile, slice(begin, begin + 16), jnp.where(keep, block, 0.0))
            for k, value in enumerate((power, far_back * power)):
                begin = TILE_GROUPS * (HALF + k * MODES) + MODES * g
                store_table(tile, slice(begin, begin + MODES), value)
        return carry

    lax.fori_loop(0, n, build_tables, 0)
    for way in range(GROUPED):
        for k in range(3):
            begin = ROWS * k
            rights[way][begin : begin + HALF, 2 * LANES : 4 * LANES] = jnp.zeros(
                (HALF, 2 * LANES), BF16
            )
    for way in range(WAYS):
        right_pairs[way][...] = jnp.zeros((2 * ROWS, 8 * LANES), BF16)

    for copy in halo:
        copy.wait()
    first, last = me == 0, me == n - 1
    for i in range(3):
        part = jnp.where(first, 0.0, got_f[i].astype(F32))
        before_ref[i, :, 0:width] = part[0:8]
        before_ref[i, :, width : 2 * width] = part[8:16]
    for i in range(4):
        part = jnp.where(last, 0.0, got_b[i].astype(F32))
        after_ref[i, :, 0:width] = part[0:8]
        after_ref[i, :, width : 2 * width] = part[8:16]

    def features(tile, way):
        lanes = lanes_of(tile)
        load_tokens(pad, proj_ref, before_ref, lanes)
        taps = tap_rows(wide_ref, lanes)
        step = 32
        for start in range(0, ROWS, step):
            rows = slice(start, start + step)
            f = [feature(pad, taps, i, start, step) for i in range(3)]
            for i in range(3):
                feat_ref[i, rows, lanes] = f[i]
            high, low = split(f[1] * f[2])
            streams[tile, rows, 0:LANES] = high
            streams[tile, rows, LANES : 2 * LANES] = low
            for k, value in enumerate((high, high, low)):
                begin = ROWS * k + start
                rights[way][begin : begin + step, 0:LANES] = value
                if start < HALF:
                    begin = begin + HALF
                    rights[way][begin : begin + step, 2 * LANES : 3 * LANES] = value
            high, low = split(cot_ref[rows, lanes].astype(F32) * f[0])
            begin = 2 * LANES * way
            parts[rows, begin : begin + LANES] = high
            parts[rows, begin + LANES : begin + 2 * LANES] = low

    def place(tile, way, flipped):
        streams[tile, :, 2 * LANES : 4 * LANES] = flipped
        for k, column in enumerate((0, 0, LANES)):
            value = flipped[:, column : column + LANES]
            begin = ROWS * k
            rights[way][begin : begin + ROWS, LANES : 2 * LANES] = value
            rights[way][begin + HALF : begin + ROWS, 3 * LANES : 4 * LANES] = value[0:HALF]

    modes, both = slice(0, MODES), slice(0, 2 * LANES)

    def send_out(k):
        return remote(
            ends_ref.at[peer_of(k)], got.at[me], s_out.at[0], r_out.at[0], peer_of(k)
        )

    def begin_tiles(step, carry):
        ks = [step * GROUPED + way for way in range(GROUPED)]
        for way, k in enumerate(ks):
            features(peer_of(k), way)
        flipped = dot(flip_matrix(), parts[...]).astype(BF16)
        for way, k in enumerate(ks):
            place(peer_of(k), way, flipped[:, 2 * LANES * way : 2 * LANES * (way + 1)])
        for way, k in enumerate(ks):
            tile = peer_of(k)
            products[way][...] = dot(tables[tile], rights[way][:, 0 : 2 * LANES])
            products_low[way][...] = dot(
                tables[tile, 0 : TILE_GROUPS * HALF, :], rights[way][:, 2 * LANES : 4 * LANES]
            )
        for way, k in enumerate(ks):
            tile = peer_of(k)
            first_end = TILE_GROUPS * HALF
            ends = select_groups(products[way], first_end, MODES, modes, both)
            ends_ref[tile, 0:MODES, :] = ends[:, 0:LANES]
            ends_ref[tile, MODES : 2 * MODES, :] = ends[:, LANES : 2 * LANES]
            first_lag = first_end + TILE_GROUPS * MODES
            lags = select_groups(products[way], first_lag, MODES, modes, both)
            local_ref[tile, 0:MODES, :] = lags[:, 0:LANES]
            local_ref[tile, MODES : 2 * MODES, :] = lags[:, LANES : 2 * LANES]
            for start in range(0, ROWS, 32):
                source = products[way] if start >= HALF else products_low[way]
                begin = start % HALF
                near = select_groups(source, 0, HALF, slice(begin, begin + 32), both)
                near_ref[0, start : start + 32, lanes_of(tile)] = near[:, 0:LANES]
                near_ref[1, start : start + 32, lanes_of(tile)] = near[:, LANES : 2 * LANES]
        for k in ks:

            @pl.when(k != 0)
            def _():
                send_out(k).start()

        return carry

    lax.fori_loop(0, n // GROUPED, begin_tiles, 0)
    for copy in stores:
        copy.start()

    lane = iota((MODES, LANES), 1)

    def correlate(step, carry):
        tiles = [step * WAYS + way for way in range(WAYS)]
        for way, tile in enumerate(tiles):
            for h in range(4):
                at = slice(QUARTER * h, QUARTER * (h + 1))
                columns = slice(2 * LANES * h, 2 * LANES * (h + 1))
                flipped = streams[tile, at, 2 * LANES : 4 * LANES]
                for g in range(TILE_GROUPS):
                    left_pairs[way][QUARTER * g : QUARTER * (g + 1), columns] = jnp.where(
                        in_group(QUARTER, 2 * LANES, g), flipped, jnp.zeros_like(flipped)
                    )
                keep = ROWS - QUARTER * h
                for k in range(2):
                    value = streams[tile, 0:keep, LANES * k : LANES * (k + 1)]
                    at = slice(ROWS * (k + 1) - keep, ROWS * (k + 1))
                    for column in (2 * LANES * h, 2 * LANES * h + LANES):
                        right_pairs[way][at, column : column + LANES] = value
        for way in range(WAYS):
            pair_sums[way][...] = lax.dot_general(
                left_pairs[way][...],
                right_pairs[way][...],
                (((1,), (1,)), ((), ())),
                preferred_element_type=F32,
            )
        for way, tile in enumerate(tiles):
            res_sum = jnp.zeros((MODES, LANES), F32)
            lag_sum = jnp.zeros((MODES, LANES), F32)
            for g in range(TILE_GROUPS):
                total = None
                for q in range(0, QUARTER, 8):
                    at = slice(QUARTER * g + q, QUARTER * g + q + 8)
                    block = pair_sums[way][at, 0:LANES] + pair_sums[way][at, LANES : 2 * LANES]
                    keep = iota((8, LANES), 1) + iota((8, LANES), 0) <= ROWS - 1 - q
                    block = jnp.where(keep, block, 0.0)
                    if q:
                        block = pltpu.roll(block, q, 1)
                    total = block if total is None else total + block
                by_lag = jnp.sum(
                    pltpu.roll(total, 0, 1, stride=1, stride_axis=0), axis=0, keepdims=True
                )
                weighted = power_of(tile, g) * by_lag
                res_sum = jnp.where(
                    lane == GROUP * g, jnp.sum(weighted, axis=1, keepdims=True), res_sum
                )
                lag_sum = jnp.where(
                    lane == GROUP * g,
                    jnp.sum(far_back * weighted, axis=1, keepdims=True),
                    lag_sum,
                )
            local_ref[tile, 2 * MODES : 3 * MODES, :] = res_sum
            local_ref[tile, 3 * MODES : 4 * MODES, :] = lag_sum
        return carry

    lax.fori_loop(0, n // WAYS // 2, correlate, 0)

    def send_in(k):
        return remote(back.at[peer_of(k)], into_ref.at[me], s_in.at[0], r_in.at[0], peer_of(k))

    others = pl.ds(0, n - 1)
    all_out = remote(ends_ref.at[others], got.at[others], s_out.at[0], r_out.at[0], right_dev)
    all_in = remote(back.at[others], into_ref.at[others], s_in.at[0], r_in.at[0], right_dev)
    got[me] = ends_ref[me]
    all_out.wait_recv()
    decay = wide_ref[DECAY : DECAY + MODES, lanes_of(me)]
    pole = jnp.exp(-decay)
    whole = jnp.exp(-decay * float(ROWS))
    zero = jnp.zeros((MODES, LANES), F32)

    def scan(step, carry):
        state, lagged, res, lag, beyond = carry
        for k in range(4):
            d = step * 4 + k
            adjoint = got[d, MODES : 2 * MODES, :]
            back[d, 0:MODES, :] = state
            res = res + adjoint * state
            lag = lag + adjoint * (state + float(ROWS) * lagged)
            state, lagged = whole * state + got[d, 0:MODES, :], whole * (lagged + state)
            d = n - 1 - d
            back[d, MODES : 2 * MODES, :] = beyond
            beyond = whole * beyond + got[d, MODES : 2 * MODES, :]
        return state, lagged, res, lag, beyond

    _, _, cross_res, cross_lag, _ = lax.fori_loop(0, n // 4, scan, (zero,) * 5)
    each(lambda k: send_in(k).start())
    into_ref[me] = back[me]

    lax.fori_loop(n // WAYS // 2, n // WAYS, correlate, 0)
    local_ref[me, 2 * MODES : 3 * MODES, :] = (
        local_ref[me, 2 * MODES : 3 * MODES, :] + pole * cross_res
    )
    local_ref[me, 3 * MODES : 4 * MODES, :] = (
        local_ref[me, 3 * MODES : 4 * MODES, :] + pole * cross_lag
    )
    all_in.wait_recv()
    all_out.wait_send()
    all_in.wait_send()
    for copy in stores:
        copy.wait()


def local_part(n, tokens, cotangent, decay_rate, residue, short_filter):
    channels = tokens.shape[2]
    groups = residue.shape[1]
    half = channels // 2
    vmem = pl.BlockSpec(memory_space=pltpu.VMEM)
    wide_rows = TILE_GROUPS * (HALF + 2 * MODES)
    return pl.pallas_call(
        partial(local_kernel, n),
        in_specs=[pl.BlockSpec(memory_space=pl.ANY)] * 2 + [vmem] * 3,
        out_specs=[vmem] * 5 + [pl.BlockSpec(memory_space=pl.ANY), vmem]
        + [pl.BlockSpec(memory_space=pl.ANY)],
        out_shape=[
            jax.ShapeDtypeStruct(shape, F32)
            for shape in (
                (TABLE_ROWS, channels),
                (3, 8, channels),
                (4, 8, channels),
                (n, 2 * MODES, LANES),
                (n, 4 * MODES, LANES),
                (2, ROWS, channels),
                (n, 2 * MODES, LANES),
                (3, ROWS, channels),
            )
        ],
        scratch_shapes=[
            pltpu.VMEM((3, ROWS, channels), BF16),
            pltpu.VMEM((ROWS, channels), BF16),
            pltpu.VMEM((2, ROWS, channels), F32),
            pltpu.VMEM((3, ROWS, channels), F32),
            pltpu.VMEM((TABLE_ROWS, groups), F32),
            pltpu.VMEM((3, 16, half), BF16),
            pltpu.VMEM((4, 16, half), BF16),
            pltpu.VMEM((3, 16, half), BF16),
            pltpu.VMEM((4, 16, half), BF16),
            pltpu.VMEM((n, 2 * MODES, LANES), F32),
            pltpu.VMEM((n, 2 * MODES, LANES), F32),
            pltpu.VMEM((n, wide_rows, 3 * LANES), BF16),
            pltpu.VMEM((n, ROWS, 4 * LANES), BF16),
            pltpu.VMEM((3, ROWS + 8, LANES), F32),
            pltpu.VMEM((ROWS, 2 * LANES * GROUPED), BF16),
        ]
        + [pltpu.VMEM((TILE_GROUPS * QUARTER, 8 * LANES), BF16)] * WAYS
        + [pltpu.VMEM((2 * ROWS, 8 * LANES), BF16)] * WAYS
        + [pltpu.VMEM((TILE_GROUPS * QUARTER, 2 * LANES), F32)] * WAYS
        + [pltpu.VMEM((3 * ROWS, 4 * LANES), BF16)] * GROUPED
        + [pltpu.VMEM((wide_rows, 2 * LANES), F32)] * GROUPED
        + [pltpu.VMEM((TILE_GROUPS * HALF, 2 * LANES), F32)] * GROUPED
        + [pltpu.SemaphoreType.DMA((4,))]
        + [pltpu.SemaphoreType.DMA((2,))] * 2
        + [pltpu.SemaphoreType.DMA((1,))] * 4,
        compiler_params=pltpu.CompilerParams(
            collective_id=0, has_side_effects=True, vmem_limit_bytes=60 * 2**20
        ),
        name="local",
    )(tokens, cotangent, decay_rate, residue, short_filter)


def finish_kernel(
    tiles, proj_ref, cot_ref, before_ref, after_ref, wide_ref, ends_ref, local_ref,
    near_ref, into_ref, feat_ref, gated_ref, grad_ref, sums_ref,
    pads, grads, lefts, rights, fars, sums, placed,
):
    step_index = pl.program_id(0)

    def spans(tile):
        return slice(tile * LANES, (tile + 1) * LANES)

    for tile in range(tiles):
        lanes = spans(tile)
        pad = pads.at[tile]
        load_tokens(pad, proj_ref, before_ref, lanes)
        for i in range(3):
            pad[i, 8 + ROWS : 16 + ROWS, :] = after_ref[i, :, lanes]
        pick = iota((MODES, LANES), 1) % MODES == iota((MODES, LANES), 0)

        def across(row):
            block = wide_ref[row : row + MODES, lanes]
            return jnp.sum(jnp.where(pick, block, 0.0), axis=0, keepdims=True)

        ahead = (iota((ROWS, LANES), 0) + 1).astype(F32)
        high, low = split(across(RESIDUE) * jnp.exp(-across(DECAY) * ahead))
        lefts[tile, :, 0:LANES] = high
        lefts[tile, :, LANES : 2 * LANES] = low
        lefts[tile, :, 2 * LANES : 3 * LANES] = high
        high, low = split(
            jnp.concatenate(
                [into_ref[tile, 0:MODES, :], into_ref[tile, MODES : 2 * MODES, :]], axis=1
            )
        )
        for g in range(TILE_GROUPS):
            keep = in_group(MODES, 2 * LANES, g)
            chosen = jnp.where(keep, high, jnp.zeros_like(high))
            begin = MODES * g
            rights[tile, begin : begin + MODES, :] = chosen
            rights[tile, ROWS + begin : ROWS + begin + MODES, :] = chosen
            rights[tile, 2 * ROWS + begin : 2 * ROWS + begin + MODES, :] = jnp.where(
                keep, low, jnp.zeros_like(low)
            )
    for tile in range(tiles):
        fars[tile] = dot(lefts[tile], rights[tile])
    for tile in range(tiles):
        lanes = spans(tile)
        long_conv = near_ref[0, :, lanes] + fars[tile, :, 0:LANES]
        for start in range(0, ROWS, 8):
            rows = slice(start, start + 8)
            value = near_ref[1, rows, lanes] + fars[tile, rows, LANES : 2 * LANES]
            turned = jnp.take_along_axis(value, 7 - iota((8, LANES), 0), axis=0)
            at = slice(ROWS - 8 - start, ROWS - start)
            grads[tile, 1, at, :] = turned * feat_ref[2, at, lanes]
            grads[tile, 2, at, :] = turned * feat_ref[1, at, lanes]
        gated_ref[:, lanes] = (feat_ref[0, :, lanes] * long_conv).astype(BF16)
        grads[tile, 0, 0:ROWS, :] = cot_ref[:, lanes].astype(F32) * long_conv
    for tile in range(tiles):
        lanes = spans(tile)
        pad = pads.at[tile]
        grad = grads.at[tile]
        taps = tap_rows(wide_ref, lanes)
        decay = wide_ref[DECAY : DECAY + MODES, lanes]
        residue = wide_ref[RESIDUE : RESIDUE + MODES, lanes]
        state = into_ref[tile, 0:MODES, :]
        adjoint = into_ref[tile, MODES : 2 * MODES, :]

        pole = jnp.exp(-decay)
        inverse = jnp.exp(decay)
        next_feat = [feature(pad, taps, i, ROWS, 8) for i in range(3)]
        next_cot = after_ref[3, :, lanes]
        next_in = next_feat[1] * next_feat[2]
        next_grad = next_cot * next_feat[0]
        whole = jnp.exp(-decay * float(ROWS))
        behind = residue * pole * (whole * state + ends_ref[tile, 0:MODES, :])
        beyond = residue * adjoint
        lag_pos = residue
        lag_neg = residue * inverse
        conv_rows, mixer_rows, filters, filters_neg = [], [], [], []
        for k in range(TAPS - 1):
            filters.append(jnp.sum(lag_pos, axis=0, keepdims=True))
            filters_neg.append(jnp.sum(lag_neg, axis=0, keepdims=True))
            conv = jnp.sum(behind, axis=0, keepdims=True)
            mixer = jnp.sum(beyond, axis=0, keepdims=True)
            for j in range(k + 1):
                conv = conv + filters[k - j] * next_in[j : j + 1]
            for j in range(k):
                mixer = mixer - filters_neg[k - j - 1] * next_grad[j : j + 1]
            conv_rows.append(conv)
            mixer_rows.append(mixer)
            lag_pos, lag_neg = lag_pos * pole, lag_neg * inverse
            behind, beyond = behind * pole, beyond * inverse
        blank = jnp.zeros((8 - (TAPS - 1), LANES), F32)
        next_conv = jnp.concatenate(conv_rows + [blank], axis=0)
        next_mixer = jnp.concatenate(mixer_rows + [blank], axis=0)
        grad[0, ROWS : ROWS + 8, :] = next_cot * next_conv
        grad[1, ROWS : ROWS + 8, :] = next_mixer * next_feat[2]
        grad[2, ROWS : ROWS + 8, :] = next_mixer * next_feat[1]

        step = 32
        short = []
        for i in range(3):
            totals = [None] * TAPS
            for start in range(0, ROWS, step):
                rows = slice(start, start + step)
                own = pad[i, 8 + start : 8 + start + step, :]
                total = None
                for j in range(TAPS):
                    ahead_grad = grad[i, start + j : start + j + step, :]
                    term = taps[TAPS * i + j] * ahead_grad
                    total = term if total is None else total + term
                    product = own * ahead_grad
                    part = product[0:8]
                    for r in range(8, step, 8):
                        part = part + product[r : r + 8]
                    totals[j] = part if totals[j] is None else totals[j] + part
                grad_ref[i, rows, lanes] = total.astype(BF16)
            short += [jnp.sum(part, axis=0, keepdims=True) for part in totals]
        short.append(jnp.zeros((3, LANES), F32))
        lag_sum = local_ref[tile, 3 * MODES : 4 * MODES, :] + pole * (
            local_ref[tile, MODES : 2 * MODES, :] * state + local_ref[tile, 0:MODES, :] * adjoint
        )
        res_sum = local_ref[tile, 2 * MODES : 3 * MODES, :]
        rest = jnp.zeros((SUM_ROWS - TABLE_ROWS, LANES), F32)
        high, low = split(jnp.concatenate(short + [res_sum, lag_sum, rest], axis=0))
        at = slice(SUM_ROWS * tile, SUM_ROWS * (tile + 1))
        sums[at, 0:LANES] = high
        sums[at, LANES : 2 * LANES] = low

    member = (iota((2 * LANES, LANES), 0) % LANES) // GROUP == iota((2 * LANES, LANES), 1)
    by_group = dot(sums[...], member.astype(F32).astype(BF16))
    total = by_group[0:SUM_ROWS]
    for tile in range(1, tiles):
        part = by_group[SUM_ROWS * tile : SUM_ROWS * (tile + 1)]
        total = total + pltpu.roll(part, TILE_GROUPS * tile, 1)
    placed[step_index] = total

    @pl.when(step_index == pl.num_programs(0) - 1)
    def _():
        groups = sums_ref.shape[1]
        width = min(groups, LANES)
        stride = tiles * TILE_GROUPS
        for begin in range(0, groups, width):
            total = placed[begin // stride]
            for k in range(1, width // stride):
                total = total + pltpu.roll(placed[begin // stride + k], stride * k, 1)
            sums_ref[:, begin : begin + width] = total[:, 0:width]


def finish(tokens, cotangent, wide, before, after, ends, local, near, into, feats, block):
    channels = tokens.shape[2]
    tiles = block // LANES
    groups = channels // GROUP

    def per_tile(rows):
        return pl.BlockSpec((tiles, rows, LANES), lambda t: (t, 0, 0))

    def stack(k, rows):
        return pl.BlockSpec((k, rows, block), lambda t: (0, 0, t))

    plane = pl.BlockSpec((ROWS, block), lambda t: (0, t))
    return pl.pallas_call(
        partial(finish_kernel, tiles),
        grid=(channels // block,),
        in_specs=[
            stack(3, ROWS),
            plane,
            stack(3, 8),
            stack(4, 8),
            pl.BlockSpec((TABLE_ROWS, block), lambda t: (0, t)),
            per_tile(2 * MODES),
            per_tile(4 * MODES),
            stack(2, ROWS),
            per_tile(2 * MODES),
            stack(3, ROWS),
        ],
        out_specs=[plane, stack(3, ROWS), pl.BlockSpec((SUM_ROWS, groups), lambda t: (0, 0))],
        out_shape=[
            jax.ShapeDtypeStruct((ROWS, channels), BF16),
            jax.ShapeDtypeStruct((3, ROWS, channels), BF16),
            jax.ShapeDtypeStruct((SUM_ROWS, groups), F32),
        ],
        scratch_shapes=[
            pltpu.VMEM((tiles, 3, ROWS + 16, LANES), F32),
            pltpu.VMEM((tiles, 3, ROWS + 8, LANES), F32),
            pltpu.VMEM((tiles, ROWS, 3 * LANES), BF16),
            pltpu.VMEM((tiles, 3 * ROWS, 2 * LANES), BF16),
            pltpu.VMEM((tiles, ROWS, 2 * LANES), F32),
            pltpu.VMEM((tiles * SUM_ROWS, 2 * LANES), BF16),
            pltpu.VMEM((channels // block, SUM_ROWS, LANES), F32),
        ],
        compiler_params=pltpu.CompilerParams(vmem_limit_bytes=62 * 2**20),
        name="finish",
    )(tokens, cotangent, before, after, wide, ends, local, near, into, feats)


def total_kernel(
    n, m, nx, ny, part_ref, decay_ref, residue_ref, short_ref, res_ref, log_ref,
    got, mine_sum, rows, full, s_a, r_a, s_b, r_b, s_c, r_c,
):
    me, genome = lax.axis_index("ctx"), lax.axis_index("seq")
    x, y, z = lax.rem(me, nx), lax.rem(lax.div(me, nx), ny), lax.div(me, nx * ny)
    a, b = ny * m, n // ny
    my_a, my_b = y * m + genome, z * nx + x

    def id_a(k):
        return {"ctx": (z * ny + lax.div(k, m)) * nx + x, "seq": lax.rem(k, m)}

    def id_b(k):
        return {"ctx": (lax.div(k, nx) * ny + y) * nx + lax.rem(k, nx), "seq": genome}

    def ahead(mine, count, k):
        return lax.rem(mine + k, count)

    def each(count, action):
        def run(k, carry):
            action(k)
            return carry

        lax.fori_loop(1, count, run, 0)

    def remote(source, target, send_sem, recv_sem, to):
        return pltpu.make_async_remote_copy(
            src_ref=source,
            dst_ref=target,
            send_sem=send_sem,
            recv_sem=recv_sem,
            device_id=to,
            device_id_type=MESH,
        )

    barrier = pltpu.get_barrier_semaphore()

    def greet(to):
        pl.semaphore_signal(barrier, inc=1, device_id=to, device_id_type=MESH)

    each(a, lambda k: greet(id_a(ahead(my_a, a, k))))
    each(b, lambda k: greet(id_b(ahead(my_b, b, k))))
    got[my_a] = part_ref[my_a]
    pl.semaphore_wait(barrier, a - 1 + b - 1)

    def first(to, slot):
        return remote(part_ref.at[to], got.at[slot], s_a.at[0], r_a.at[0], id_a(to))

    def second(to, slot):
        return remote(mine_sum, rows.at[slot], s_b.at[0], r_b.at[0], id_b(to))

    def third(to, slot):
        return remote(full.at[my_a], full.at[slot], s_c.at[0], r_c.at[0], id_a(to))

    def start(mine, count, copy):
        each(count, lambda k: copy(ahead(mine, count, k), mine).start())

    in_a, in_b = pl.ds(0, a - 1), pl.ds(0, b - 1)
    next_a = id_a(ahead(my_a, a, 1))
    next_b = id_b(ahead(my_b, b, 1))
    all_first = remote(part_ref.at[in_a], got.at[in_a], s_a.at[0], r_a.at[0], next_a)
    all_second = remote(rows.at[in_b], rows.at[in_b], s_b.at[0], r_b.at[0], next_b)
    all_third = remote(full.at[in_a], full.at[in_a], s_c.at[0], r_c.at[0], next_a)

    start(my_a, a, first)
    all_first.wait_recv()
    total = got[0]
    for d in range(1, a):
        total = total + got[d]
    mine_sum[...] = total
    rows[my_b] = total
    start(my_b, b, second)
    all_second.wait_recv()
    total = rows[0]
    for d in range(1, b):
        total = total + rows[d]
    full[my_a] = total
    start(my_a, a, third)
    all_third.wait_recv()
    share = full.shape[1]
    sums = jnp.concatenate([full[k // share, k % share] for k in range(TABLE_ROWS // 8)], axis=0)
    sums = sums * (1.0 / float(ROWS * n * m))
    for i in range(3):
        short_ref[i] = sums[TAPS * i : TAPS * (i + 1)]
    res_ref[...] = sums[24 : 24 + MODES]
    log_ref[...] = -residue_ref[...] * decay_ref[...] * sums[40 : 40 + MODES]
    all_first.wait_send()
    all_second.wait_send()
    all_third.wait_send()


def total_sums(n, m, parts, decay_rate, residue):
    ny = 2
    nx = min(4, n // ny)
    a, b = ny * m, n // ny
    share, groups = SUM_ROWS // 8 // a, parts.shape[1]
    vmem = pl.BlockSpec(memory_space=pltpu.VMEM)
    dma = pltpu.SemaphoreType.DMA
    return pl.pallas_call(
        partial(total_kernel, n, m, nx, ny),
        out_shape=[
            jax.ShapeDtypeStruct((3, TAPS, groups), F32),
            jax.ShapeDtypeStruct((MODES, groups), F32),
            jax.ShapeDtypeStruct((MODES, groups), F32),
        ],
        in_specs=[vmem] * 3,
        out_specs=[vmem] * 3,
        scratch_shapes=[
            pltpu.VMEM((a, share, 8, groups), F32),
            pltpu.VMEM((share, 8, groups), F32),
            pltpu.VMEM((b, share, 8, groups), F32),
            pltpu.VMEM((a, share, 8, groups), F32),
        ]
        + [dma((1,))] * 6,
        compiler_params=pltpu.CompilerParams(
            collective_id=1, has_side_effects=True, vmem_limit_bytes=16 * 2**20
        ),
        name="totals",
    )(parts.reshape(a, share, 8, groups), decay_rate, residue)


def per_device(projected, cotangent, short_filter, residue, decay_rate):
    n, m = lax.axis_size("ctx"), lax.axis_size("seq")
    tokens, upstream = projected[0], cotangent[0]
    block = min(tokens.shape[2], 512)
    known = local_part(n, tokens, upstream, decay_rate, residue, short_filter)
    gated, grad_tokens, sums = finish(tokens, upstream, *known, block)
    return gated[None], grad_tokens[None], *total_sums(n, m, sums, decay_rate, residue)


def solution(mesh):
    placed = (P("seq", None, "ctx", None), P("seq", "ctx", None), P(), P(), P())
    return jax.shard_map(
        per_device,
        mesh=mesh,
        in_specs=placed,
        out_specs=(P("seq", "ctx", None), P("seq", None, "ctx", None), P(), P(), P()),
        check_vma=False,
    )
```

```python
from functools import partial

import jax
import jax.numpy as jnp
from jax import lax
from jax.experimental import pallas as pl
from jax.experimental.pallas import tpu as pltpu
from jax.sharding import PartitionSpec as P

GROUP = 16
MODES = 16
TAPS = 7
LANES = 128
TILE_GROUPS = LANES // GROUP
ROWS = 128
F32, BF16 = jnp.float32, jnp.bfloat16
MESH = pl.DeviceIdType.MESH

HALF = ROWS // 2
QUARTER = ROWS // 4
GROUPED = 4
WAYS = 2

DECAY, RESIDUE, SHORT, TABLE_ROWS = 0, 16, 32, 56
SUM_ROWS = 64


def split(value):
    high = value.astype(BF16)
    return high, (value - high.astype(F32)).astype(BF16)


def iota(shape, dim):
    return lax.broadcasted_iota(jnp.int32, shape, dim)


def dot(left, right):
    return jnp.dot(left, right, preferred_element_type=F32)


def in_group(rows, width, group):
    return (iota((rows, width), 1) % LANES) // GROUP == group


def load_tokens(pad, proj_ref, before_ref, lanes):
    for i in range(3):
        pad[i, 0:8, :] = before_ref[i, :, lanes]
        pad[i, 8 : 8 + ROWS, :] = proj_ref[i, :, lanes].astype(F32)


def feature(pad, taps, i, start, count):
    total = None
    for j in range(TAPS):
        term = taps[TAPS * i + j] * pad[i, 8 + start - j : 8 + start - j + count, :]
        total = term if total is None else total + term
    return total


def tap_rows(wide_ref, lanes):
    return [wide_ref[SHORT + k : SHORT + k + 1, lanes] for k in range(3 * TAPS)]


def expand_table(wide_ref, small, decay_ref, residue_ref, short_ref):
    small[DECAY : DECAY + MODES, :] = decay_ref[...]
    small[RESIDUE : RESIDUE + MODES, :] = residue_ref[...]
    for i in range(3):
        small[SHORT + TAPS * i : SHORT + TAPS * (i + 1), :] = short_ref[i]
    used = SHORT + 3 * TAPS
    groups = small.shape[1]
    small[used:TABLE_ROWS, :] = jnp.zeros((TABLE_ROWS - used, groups), F32)
    value = small[...]
    high = value.astype(BF16).astype(F32)
    middle = (value - high).astype(BF16).astype(F32)
    low = value - high - middle
    pieces = jnp.concatenate([high, middle, low], axis=0).astype(BF16)
    width = min(1024, wide_ref.shape[1])
    for start in range(0, wide_ref.shape[1], width):
        owner = (iota((groups, width), 1) + start) // GROUP
        spread = (iota((groups, width), 0) == owner).astype(F32).astype(BF16)
        got = dot(pieces, spread)
        wide_ref[:, start : start + width] = got[0:TABLE_ROWS] + (
            got[TABLE_ROWS : 2 * TABLE_ROWS] + got[2 * TABLE_ROWS :]
        )


def lanes_of(tile):
    return pl.ds(pl.multiple_of(tile * LANES, LANES), LANES)


def select_groups(source, begin, count, rows, columns):
    total = source[begin + rows.start : begin + rows.stop, columns]
    for g in range(1, TILE_GROUPS):
        at = begin + g * count
        total = jnp.where(
            in_group(rows.stop - rows.start, columns.stop - columns.start, g),
            source[at + rows.start : at + rows.stop, columns],
            total,
        )
    return total


def local_kernel(
    n, proj_hbm, cot_hbm, decay_ref, residue_ref, short_ref,
    wide_ref, before_ref, after_ref, ends_ref, local_ref, near_hbm, into_ref, feat_hbm,
    proj_ref, cot_ref, near_ref, feat_ref, small, out_f, out_b, got_f, got_b, got, back, tables, streams, pad, parts, *scratch,
):
    left_pairs, right_pairs, pair_sums = (scratch[k * WAYS : (k + 1) * WAYS] for k in range(3))
    scratch = scratch[3 * WAYS :]
    rights, products, products_low = (scratch[k * GROUPED : (k + 1) * GROUPED] for k in range(3))
    local_sem, halo_send, halo_recv, s_out, r_out, s_in, r_in = scratch[3 * GROUPED :]
    me = lax.axis_index("ctx")
    right_dev, left_dev = lax.rem(me + 1, n), lax.rem(me + n - 1, n)
    far_back = (LANES - 1 - iota((MODES, LANES), 1)).astype(F32)

    def peer_of(k):
        return lax.rem(me + k, n)

    def each(action):
        def run(k, carry):
            action(k)
            return carry

        lax.fori_loop(1, n, run, 0)

    def remote(source, target, send_sem, recv_sem, to):
        return pltpu.make_async_remote_copy(
            src_ref=source,
            dst_ref=target,
            send_sem=send_sem,
            recv_sem=recv_sem,
            device_id={"ctx": to},
            device_id_type=MESH,
        )

    loads = [
        pltpu.make_async_copy(proj_hbm, proj_ref, local_sem.at[0]),
        pltpu.make_async_copy(cot_hbm, cot_ref, local_sem.at[1]),
    ]
    stores = [
        pltpu.make_async_copy(near_ref, near_hbm, local_sem.at[2]),
        pltpu.make_async_copy(feat_ref, feat_hbm, local_sem.at[3]),
    ]
    for copy in loads:
        copy.start()
    barrier = pltpu.get_barrier_semaphore()
    each(
        lambda k: pl.semaphore_signal(
            barrier, inc=1, device_id={"ctx": peer_of(k)}, device_id_type=MESH
        )
    )
    expand_table(wide_ref, small, decay_ref, residue_ref, short_ref)
    for copy in loads:
        copy.wait()
    width = out_f.shape[2]
    for i in range(3):
        tail = proj_ref[i, ROWS - 16 : ROWS, :].astype(F32)[8:16]
        out_f[i] = jnp.concatenate([tail[:, :width], tail[:, width:]], axis=0).astype(BF16)
    for i in range(4):
        head = (cot_ref[0:16, :] if i == 3 else proj_ref[i, 0:16, :]).astype(F32)[0:8]
        out_b[i] = jnp.concatenate([head[:, :width], head[:, width:]], axis=0).astype(BF16)
    pl.semaphore_wait(barrier, n - 1)
    halo = [
        remote(out_f, got_f, halo_send.at[0], halo_recv.at[0], right_dev),
        remote(out_b, got_b, halo_send.at[1], halo_recv.at[1], left_dev),
    ]
    for copy in halo:
        copy.start()

    def power_of(tile, g):
        column = GROUP * g
        decay = wide_ref[DECAY : DECAY + MODES, lanes_of(tile)]
        return jnp.exp(-decay[:, column : column + 1] * far_back)

    def store_table(tile, at, value):
        high, low = split(value)
        tables[tile, at, 0:LANES] = high
        tables[tile, at, LANES : 2 * LANES] = low
        tables[tile, at, 2 * LANES : 3 * LANES] = high

    def build_tables(tile, carry):
        residue = wide_ref[RESIDUE : RESIDUE + MODES, lanes_of(tile)]
        for g in range(TILE_GROUPS):
            column = GROUP * g
            power = power_of(tile, g)
            filter_row = jnp.sum(residue[:, column : column + 1] * power, axis=0, keepdims=True)
            base = pltpu.roll(
                jnp.broadcast_to(filter_row, (8, LANES)), 1, 1, stride=1, stride_axis=0
            )
            for q in range(HALF, ROWS, 16):
                block = jnp.concatenate(
                    [pltpu.roll(base, q, 1), pltpu.roll(base, q + 8, 1)], axis=0
                )
                keep = iota((16, LANES), 1) <= iota((16, LANES), 0) + q
                begin = HALF * g + q - HALF
                store_table(tile, slice(begin, begin + 16), jnp.where(keep, block, 0.0))
            for k, value in enumerate((power, far_back * power)):
                begin = TILE_GROUPS * (HALF + k * MODES) + MODES * g
                store_table(tile, slice(begin, begin + MODES), value)
        return carry

    lax.fori_loop(0, n, build_tables, 0)
    for way in range(GROUPED):
        for k in range(3):
            begin = ROWS * k
            rights[way][begin : begin + HALF, 2 * LANES : 4 * LANES] = jnp.zeros(
                (HALF, 2 * LANES), BF16
            )
    for way in range(WAYS):
        right_pairs[way][...] = jnp.zeros((2 * ROWS, 8 * LANES), BF16)

    for copy in halo:
        copy.wait()
    first, last = me == 0, me == n - 1
    for i in range(3):
        part = jnp.where(first, 0.0, got_f[i].astype(F32))
        before_ref[i, :, 0:width] = part[0:8]
        before_ref[i, :, width : 2 * width] = part[8:16]
    for i in range(4):
        part = jnp.where(last, 0.0, got_b[i].astype(F32))
        after_ref[i, :, 0:width] = part[0:8]
        after_ref[i, :, width : 2 * width] = part[8:16]

    def features(tile, way):
        lanes = lanes_of(tile)
        load_tokens(pad, proj_ref, before_ref, lanes)
        taps = tap_rows(wide_ref, lanes)
        step = 32
        for start in range(0, ROWS, step):
            rows = slice(start, start + step)
            f = [feature(pad, taps, i, start, step) for i in range(3)]
            for i in range(3):
                feat_ref[i, rows, lanes] = f[i]
            high, low = split(f[1] * f[2])
            streams[tile, rows, 0:LANES] = high
            streams[tile, rows, LANES : 2 * LANES] = low
            for k, value in enumerate((high, high, low)):
                begin = ROWS * k + start
                rights[way][begin : begin + step, 0:LANES] = value
                if start < HALF:
                    begin = begin + HALF
                    rights[way][begin : begin + step, 2 * LANES : 3 * LANES] = value
            value = cot_ref[rows, lanes].astype(F32) * f[0]
            turn = 7 - iota((8, LANES), 0)
            turned = jnp.concatenate(
                [
                    jnp.take_along_axis(value[r : r + 8], turn, axis=0)
                    for r in range(step - 8, -8, -8)
                ],
                axis=0,
            )
            high, low = split(turned)
            begin = 2 * LANES * way
            at = slice(ROWS - step - start, ROWS - start)
            parts[at, begin : begin + LANES] = high
            parts[at, begin + LANES : begin + 2 * LANES] = low

    def place(tile, way, flipped):
        streams[tile, :, 2 * LANES : 4 * LANES] = flipped
        for k, column in enumerate((0, 0, LANES)):
            value = flipped[:, column : column + LANES]
            begin = ROWS * k
            rights[way][begin : begin + ROWS, LANES : 2 * LANES] = value
            rights[way][begin + HALF : begin + ROWS, 3 * LANES : 4 * LANES] = value[0:HALF]

    modes, both = slice(0, MODES), slice(0, 2 * LANES)

    def send_out(k):
        return remote(
            ends_ref.at[peer_of(k)], got.at[me], s_out.at[0], r_out.at[0], peer_of(k)
        )

    def begin_tiles(step, carry):
        ks = [step * GROUPED + way for way in range(GROUPED)]
        for way, k in enumerate(ks):
            features(peer_of(k), way)
        for way, k in enumerate(ks):
            place(peer_of(k), way, parts[:, 2 * LANES * way : 2 * LANES * (way + 1)])
        for way, k in enumerate(ks):
            tile = peer_of(k)
            products[way][...] = dot(tables[tile], rights[way][:, 0 : 2 * LANES])
            products_low[way][...] = dot(
                tables[tile, 0 : TILE_GROUPS * HALF, :], rights[way][:, 2 * LANES : 4 * LANES]
            )
        for way, k in enumerate(ks):
            tile = peer_of(k)
            first_end = TILE_GROUPS * HALF
            ends = select_groups(products[way], first_end, MODES, modes, both)
            ends_ref[tile, 0:MODES, :] = ends[:, 0:LANES]
            ends_ref[tile, MODES : 2 * MODES, :] = ends[:, LANES : 2 * LANES]
            first_lag = first_end + TILE_GROUPS * MODES
            lags = select_groups(products[way], first_lag, MODES, modes, both)
            local_ref[tile, 0:MODES, :] = lags[:, 0:LANES]
            local_ref[tile, MODES : 2 * MODES, :] = lags[:, LANES : 2 * LANES]
            for start in range(0, ROWS, 32):
                source = products[way] if start >= HALF else products_low[way]
                begin = start % HALF
                near = select_groups(source, 0, HALF, slice(begin, begin + 32), both)
                near_ref[0, start : start + 32, lanes_of(tile)] = near[:, 0:LANES]
                near_ref[1, start : start + 32, lanes_of(tile)] = near[:, LANES : 2 * LANES]
        for k in ks:

            @pl.when(k != 0)
            def _():
                send_out(k).start()

        return carry

    lax.fori_loop(0, n // GROUPED, begin_tiles, 0)
    for copy in stores:
        copy.start()

    lane = iota((MODES, LANES), 1)

    def correlate(step, carry):
        tiles = [step * WAYS + way for way in range(WAYS)]
        for way, tile in enumerate(tiles):
            for h in range(4):
                at = slice(QUARTER * h, QUARTER * (h + 1))
                columns = slice(2 * LANES * h, 2 * LANES * (h + 1))
                flipped = streams[tile, at, 2 * LANES : 4 * LANES]
                for g in range(TILE_GROUPS):
                    left_pairs[way][QUARTER * g : QUARTER * (g + 1), columns] = jnp.where(
                        in_group(QUARTER, 2 * LANES, g), flipped, jnp.zeros_like(flipped)
                    )
                keep = ROWS - QUARTER * h
                for k in range(2):
                    value = streams[tile, 0:keep, LANES * k : LANES * (k + 1)]
                    at = slice(ROWS * (k + 1) - keep, ROWS * (k + 1))
                    for column in (2 * LANES * h, 2 * LANES * h + LANES):
                        right_pairs[way][at, column : column + LANES] = value
        for way in range(WAYS):
            pair_sums[way][...] = lax.dot_general(
                left_pairs[way][...],
                right_pairs[way][...],
                (((1,), (1,)), ((), ())),
                preferred_element_type=F32,
            )
        for way, tile in enumerate(tiles):
            res_sum = jnp.zeros((MODES, LANES), F32)
            lag_sum = jnp.zeros((MODES, LANES), F32)
            for g in range(TILE_GROUPS):
                total = None
                for q in range(0, QUARTER, 8):
                    at = slice(QUARTER * g + q, QUARTER * g + q + 8)
                    block = pair_sums[way][at, 0:LANES] + pair_sums[way][at, LANES : 2 * LANES]
                    keep = iota((8, LANES), 1) + iota((8, LANES), 0) <= ROWS - 1 - q
                    block = jnp.where(keep, block, 0.0)
                    if q:
                        block = pltpu.roll(block, q, 1)
                    total = block if total is None else total + block
                by_lag = jnp.sum(
                    pltpu.roll(total, 0, 1, stride=1, stride_axis=0), axis=0, keepdims=True
                )
                weighted = power_of(tile, g) * by_lag
                res_sum = jnp.where(
                    lane == GROUP * g, jnp.sum(weighted, axis=1, keepdims=True), res_sum
                )
                lag_sum = jnp.where(
                    lane == GROUP * g,
                    jnp.sum(far_back * weighted, axis=1, keepdims=True),
                    lag_sum,
                )
            local_ref[tile, 2 * MODES : 3 * MODES, :] = res_sum
            local_ref[tile, 3 * MODES : 4 * MODES, :] = lag_sum
        return carry

    lax.fori_loop(0, n // WAYS // 2, correlate, 0)

    def send_in(k):
        return remote(back.at[peer_of(k)], into_ref.at[me], s_in.at[0], r_in.at[0], peer_of(k))

    others = pl.ds(0, n - 1)
    all_out = remote(ends_ref.at[others], got.at[others], s_out.at[0], r_out.at[0], right_dev)
    all_in = remote(back.at[others], into_ref.at[others], s_in.at[0], r_in.at[0], right_dev)
    got[me] = ends_ref[me]
    all_out.wait_recv()
    decay = wide_ref[DECAY : DECAY + MODES, lanes_of(me)]
    pole = jnp.exp(-decay)
    whole = jnp.exp(-decay * float(ROWS))
    zero = jnp.zeros((MODES, LANES), F32)

    def scan(step, carry):
        state, lagged, res, lag, beyond = carry
        for k in range(4):
            d = step * 4 + k
            adjoint = got[d, MODES : 2 * MODES, :]
            back[d, 0:MODES, :] = state
            res = res + adjoint * state
            lag = lag + adjoint * (state + float(ROWS) * lagged)
            state, lagged = whole * state + got[d, 0:MODES, :], whole * (lagged + state)
            d = n - 1 - d
            back[d, MODES : 2 * MODES, :] = beyond
            beyond = whole * beyond + got[d, MODES : 2 * MODES, :]
        return state, lagged, res, lag, beyond

    _, _, cross_res, cross_lag, _ = lax.fori_loop(0, n // 4, scan, (zero,) * 5)
    each(lambda k: send_in(k).start())
    into_ref[me] = back[me]

    lax.fori_loop(n // WAYS // 2, n // WAYS, correlate, 0)
    local_ref[me, 2 * MODES : 3 * MODES, :] = (
        local_ref[me, 2 * MODES : 3 * MODES, :] + pole * cross_res
    )
    local_ref[me, 3 * MODES : 4 * MODES, :] = (
        local_ref[me, 3 * MODES : 4 * MODES, :] + pole * cross_lag
    )
    all_in.wait_recv()
    all_out.wait_send()
    all_in.wait_send()
    for copy in stores:
        copy.wait()


def local_part(n, tokens, cotangent, decay_rate, residue, short_filter):
    channels = tokens.shape[2]
    groups = residue.shape[1]
    half = channels // 2
    vmem = pl.BlockSpec(memory_space=pltpu.VMEM)
    wide_rows = TILE_GROUPS * (HALF + 2 * MODES)
    return pl.pallas_call(
        partial(local_kernel, n),
        in_specs=[pl.BlockSpec(memory_space=pl.ANY)] * 2 + [vmem] * 3,
        out_specs=[vmem] * 5 + [pl.BlockSpec(memory_space=pl.ANY), vmem]
        + [pl.BlockSpec(memory_space=pl.ANY)],
        out_shape=[
            jax.ShapeDtypeStruct(shape, F32)
            for shape in (
                (TABLE_ROWS, channels),
                (3, 8, channels),
                (4, 8, channels),
                (n, 2 * MODES, LANES),
                (n, 4 * MODES, LANES),
                (2, ROWS, channels),
                (n, 2 * MODES, LANES),
                (3, ROWS, channels),
            )
        ],
        scratch_shapes=[
            pltpu.VMEM((3, ROWS, channels), BF16),
            pltpu.VMEM((ROWS, channels), BF16),
            pltpu.VMEM((2, ROWS, channels), F32),
            pltpu.VMEM((3, ROWS, channels), F32),
            pltpu.VMEM((TABLE_ROWS, groups), F32),
            pltpu.VMEM((3, 16, half), BF16),
            pltpu.VMEM((4, 16, half), BF16),
            pltpu.VMEM((3, 16, half), BF16),
            pltpu.VMEM((4, 16, half), BF16),
            pltpu.VMEM((n, 2 * MODES, LANES), F32),
            pltpu.VMEM((n, 2 * MODES, LANES), F32),
            pltpu.VMEM((n, wide_rows, 3 * LANES), BF16),
            pltpu.VMEM((n, ROWS, 4 * LANES), BF16),
            pltpu.VMEM((3, ROWS + 8, LANES), F32),
            pltpu.VMEM((ROWS, 2 * LANES * GROUPED), BF16),
        ]
        + [pltpu.VMEM((TILE_GROUPS * QUARTER, 8 * LANES), BF16)] * WAYS
        + [pltpu.VMEM((2 * ROWS, 8 * LANES), BF16)] * WAYS
        + [pltpu.VMEM((TILE_GROUPS * QUARTER, 2 * LANES), F32)] * WAYS
        + [pltpu.VMEM((3 * ROWS, 4 * LANES), BF16)] * GROUPED
        + [pltpu.VMEM((wide_rows, 2 * LANES), F32)] * GROUPED
        + [pltpu.VMEM((TILE_GROUPS * HALF, 2 * LANES), F32)] * GROUPED
        + [pltpu.SemaphoreType.DMA((4,))]
        + [pltpu.SemaphoreType.DMA((2,))] * 2
        + [pltpu.SemaphoreType.DMA((1,))] * 4,
        compiler_params=pltpu.CompilerParams(
            collective_id=0, has_side_effects=True, vmem_limit_bytes=60 * 2**20
        ),
        name="local",
    )(tokens, cotangent, decay_rate, residue, short_filter)


def finish_kernel(
    tiles, proj_ref, cot_ref, before_ref, after_ref, wide_ref, ends_ref, local_ref,
    near_ref, into_ref, feat_ref, gated_ref, grad_ref, sums_ref,
    pads, grads, lefts, rights, fars, sums, placed,
):
    step_index = pl.program_id(0)

    def spans(tile):
        return slice(tile * LANES, (tile + 1) * LANES)

    for tile in range(tiles):
        lanes = spans(tile)
        pad = pads.at[tile]
        load_tokens(pad, proj_ref, before_ref, lanes)
        for i in range(3):
            pad[i, 8 + ROWS : 16 + ROWS, :] = after_ref[i, :, lanes]
        pick = iota((MODES, LANES), 1) % MODES == iota((MODES, LANES), 0)

        def across(row):
            block = wide_ref[row : row + MODES, lanes]
            return jnp.sum(jnp.where(pick, block, 0.0), axis=0, keepdims=True)

        ahead = (iota((ROWS, LANES), 0) + 1).astype(F32)
        high, low = split(across(RESIDUE) * jnp.exp(-across(DECAY) * ahead))
        lefts[tile, :, 0:LANES] = high
        lefts[tile, :, LANES : 2 * LANES] = low
        lefts[tile, :, 2 * LANES : 3 * LANES] = high
        high, low = split(
            jnp.concatenate(
                [into_ref[tile, 0:MODES, :], into_ref[tile, MODES : 2 * MODES, :]], axis=1
            )
        )
        for g in range(TILE_GROUPS):
            keep = in_group(MODES, 2 * LANES, g)
            chosen = jnp.where(keep, high, jnp.zeros_like(high))
            begin = MODES * g
            rights[tile, begin : begin + MODES, :] = chosen
            rights[tile, ROWS + begin : ROWS + begin + MODES, :] = chosen
            rights[tile, 2 * ROWS + begin : 2 * ROWS + begin + MODES, :] = jnp.where(
                keep, low, jnp.zeros_like(low)
            )
    for tile in range(tiles):
        fars[tile] = dot(lefts[tile], rights[tile])
    for tile in range(tiles):
        lanes = spans(tile)
        long_conv = near_ref[0, :, lanes] + fars[tile, :, 0:LANES]
        for start in range(0, ROWS, 8):
            rows = slice(start, start + 8)
            value = near_ref[1, rows, lanes] + fars[tile, rows, LANES : 2 * LANES]
            turned = jnp.take_along_axis(value, 7 - iota((8, LANES), 0), axis=0)
            at = slice(ROWS - 8 - start, ROWS - start)
            grads[tile, 1, at, :] = turned * feat_ref[2, at, lanes]
            grads[tile, 2, at, :] = turned * feat_ref[1, at, lanes]
        gated_ref[:, lanes] = (feat_ref[0, :, lanes] * long_conv).astype(BF16)
        grads[tile, 0, 0:ROWS, :] = cot_ref[:, lanes].astype(F32) * long_conv
    for tile in range(tiles):
        lanes = spans(tile)
        pad = pads.at[tile]
        grad = grads.at[tile]
        taps = tap_rows(wide_ref, lanes)
        decay = wide_ref[DECAY : DECAY + MODES, lanes]
        residue = wide_ref[RESIDUE : RESIDUE + MODES, lanes]
        state = into_ref[tile, 0:MODES, :]
        adjoint = into_ref[tile, MODES : 2 * MODES, :]

        pole = jnp.exp(-decay)
        inverse = jnp.exp(decay)
        next_feat = [feature(pad, taps, i, ROWS, 8) for i in range(3)]
        next_cot = after_ref[3, :, lanes]
        next_in = next_feat[1] * next_feat[2]
        next_grad = next_cot * next_feat[0]
        whole = jnp.exp(-decay * float(ROWS))
        behind = residue * pole * (whole * state + ends_ref[tile, 0:MODES, :])
        beyond = residue * adjoint
        lag_pos = residue
        lag_neg = residue * inverse
        conv_rows, mixer_rows, filters, filters_neg = [], [], [], []
        for k in range(TAPS - 1):
            filters.append(jnp.sum(lag_pos, axis=0, keepdims=True))
            filters_neg.append(jnp.sum(lag_neg, axis=0, keepdims=True))
            conv = jnp.sum(behind, axis=0, keepdims=True)
            mixer = jnp.sum(beyond, axis=0, keepdims=True)
            for j in range(k + 1):
                conv = conv + filters[k - j] * next_in[j : j + 1]
            for j in range(k):
                mixer = mixer - filters_neg[k - j - 1] * next_grad[j : j + 1]
            conv_rows.append(conv)
            mixer_rows.append(mixer)
            lag_pos, lag_neg = lag_pos * pole, lag_neg * inverse
            behind, beyond = behind * pole, beyond * inverse
        blank = jnp.zeros((8 - (TAPS - 1), LANES), F32)
        next_conv = jnp.concatenate(conv_rows + [blank], axis=0)
        next_mixer = jnp.concatenate(mixer_rows + [blank], axis=0)
        grad[0, ROWS : ROWS + 8, :] = next_cot * next_conv
        grad[1, ROWS : ROWS + 8, :] = next_mixer * next_feat[2]
        grad[2, ROWS : ROWS + 8, :] = next_mixer * next_feat[1]

        step = 32
        short = []
        for i in range(3):
            totals = [None] * TAPS
            for start in range(0, ROWS, step):
                rows = slice(start, start + step)
                own = pad[i, 8 + start : 8 + start + step, :]
                total = None
                for j in range(TAPS):
                    ahead_grad = grad[i, start + j : start + j + step, :]
                    term = taps[TAPS * i + j] * ahead_grad
                    total = term if total is None else total + term
                    product = own * ahead_grad
                    part = product[0:8]
                    for r in range(8, step, 8):
                        part = part + product[r : r + 8]
                    totals[j] = part if totals[j] is None else totals[j] + part
                grad_ref[i, rows, lanes] = total.astype(BF16)
            short += [jnp.sum(part, axis=0, keepdims=True) for part in totals]
        short.append(jnp.zeros((3, LANES), F32))
        lag_sum = local_ref[tile, 3 * MODES : 4 * MODES, :] + pole * (
            local_ref[tile, MODES : 2 * MODES, :] * state + local_ref[tile, 0:MODES, :] * adjoint
        )
        res_sum = local_ref[tile, 2 * MODES : 3 * MODES, :]
        rest = jnp.zeros((SUM_ROWS - TABLE_ROWS, LANES), F32)
        high, low = split(jnp.concatenate(short + [res_sum, lag_sum, rest], axis=0))
        at = slice(SUM_ROWS * tile, SUM_ROWS * (tile + 1))
        sums[at, 0:LANES] = high
        sums[at, LANES : 2 * LANES] = low

    member = (iota((2 * LANES, LANES), 0) % LANES) // GROUP == iota((2 * LANES, LANES), 1)
    by_group = dot(sums[...], member.astype(F32).astype(BF16))
    total = by_group[0:SUM_ROWS]
    for tile in range(1, tiles):
        part = by_group[SUM_ROWS * tile : SUM_ROWS * (tile + 1)]
        total = total + pltpu.roll(part, TILE_GROUPS * tile, 1)
    placed[step_index] = total

    @pl.when(step_index == pl.num_programs(0) - 1)
    def _():
        groups = sums_ref.shape[1]
        width = min(groups, LANES)
        stride = tiles * TILE_GROUPS
        for begin in range(0, groups, width):
            total = placed[begin // stride]
            for k in range(1, width // stride):
                total = total + pltpu.roll(placed[begin // stride + k], stride * k, 1)
            sums_ref[:, begin : begin + width] = total[:, 0:width]


def finish(tokens, cotangent, wide, before, after, ends, local, near, into, feats, block):
    channels = tokens.shape[2]
    tiles = block // LANES
    groups = channels // GROUP

    def per_tile(rows):
        return pl.BlockSpec((tiles, rows, LANES), lambda t: (t, 0, 0))

    def stack(k, rows):
        return pl.BlockSpec((k, rows, block), lambda t: (0, 0, t))

    plane = pl.BlockSpec((ROWS, block), lambda t: (0, t))
    return pl.pallas_call(
        partial(finish_kernel, tiles),
        grid=(channels // block,),
        in_specs=[
            stack(3, ROWS),
            plane,
            stack(3, 8),
            stack(4, 8),
            pl.BlockSpec((TABLE_ROWS, block), lambda t: (0, t)),
            per_tile(2 * MODES),
            per_tile(4 * MODES),
            stack(2, ROWS),
            per_tile(2 * MODES),
            stack(3, ROWS),
        ],
        out_specs=[plane, stack(3, ROWS), pl.BlockSpec((SUM_ROWS, groups), lambda t: (0, 0))],
        out_shape=[
            jax.ShapeDtypeStruct((ROWS, channels), BF16),
            jax.ShapeDtypeStruct((3, ROWS, channels), BF16),
            jax.ShapeDtypeStruct((SUM_ROWS, groups), F32),
        ],
        scratch_shapes=[
            pltpu.VMEM((tiles, 3, ROWS + 16, LANES), F32),
            pltpu.VMEM((tiles, 3, ROWS + 8, LANES), F32),
            pltpu.VMEM((tiles, ROWS, 3 * LANES), BF16),
            pltpu.VMEM((tiles, 3 * ROWS, 2 * LANES), BF16),
            pltpu.VMEM((tiles, ROWS, 2 * LANES), F32),
            pltpu.VMEM((tiles * SUM_ROWS, 2 * LANES), BF16),
            pltpu.VMEM((channels // block, SUM_ROWS, LANES), F32),
        ],
        compiler_params=pltpu.CompilerParams(vmem_limit_bytes=62 * 2**20),
        name="finish",
    )(tokens, cotangent, before, after, wide, ends, local, near, into, feats)


def total_kernel(
    n, m, nx, ny, part_ref, decay_ref, residue_ref, short_ref, res_ref, log_ref,
    got, mine_sum, rows, full, s_a, r_a, s_b, r_b, s_c, r_c,
):
    me, genome = lax.axis_index("ctx"), lax.axis_index("seq")
    x, y, z = lax.rem(me, nx), lax.rem(lax.div(me, nx), ny), lax.div(me, nx * ny)
    a, b = ny * m, n // ny
    my_a, my_b = y * m + genome, z * nx + x

    def id_a(k):
        return {"ctx": (z * ny + lax.div(k, m)) * nx + x, "seq": lax.rem(k, m)}

    def id_b(k):
        return {"ctx": (lax.div(k, nx) * ny + y) * nx + lax.rem(k, nx), "seq": genome}

    def ahead(mine, count, k):
        return lax.rem(mine + k, count)

    def each(count, action):
        def run(k, carry):
            action(k)
            return carry

        lax.fori_loop(1, count, run, 0)

    def remote(source, target, send_sem, recv_sem, to):
        return pltpu.make_async_remote_copy(
            src_ref=source,
            dst_ref=target,
            send_sem=send_sem,
            recv_sem=recv_sem,
            device_id=to,
            device_id_type=MESH,
        )

    barrier = pltpu.get_barrier_semaphore()

    def greet(to):
        pl.semaphore_signal(barrier, inc=1, device_id=to, device_id_type=MESH)

    each(a, lambda k: greet(id_a(ahead(my_a, a, k))))
    each(b, lambda k: greet(id_b(ahead(my_b, b, k))))
    got[my_a] = part_ref[my_a]
    pl.semaphore_wait(barrier, a - 1 + b - 1)

    def first(to, slot):
        return remote(part_ref.at[to], got.at[slot], s_a.at[0], r_a.at[0], id_a(to))

    def second(to, slot):
        return remote(mine_sum, rows.at[slot], s_b.at[0], r_b.at[0], id_b(to))

    def third(to, slot):
        return remote(full.at[my_a], full.at[slot], s_c.at[0], r_c.at[0], id_a(to))

    def start(mine, count, copy):
        each(count, lambda k: copy(ahead(mine, count, k), mine).start())

    in_a, in_b = pl.ds(0, a - 1), pl.ds(0, b - 1)
    next_a = id_a(ahead(my_a, a, 1))
    next_b = id_b(ahead(my_b, b, 1))
    all_first = remote(part_ref.at[in_a], got.at[in_a], s_a.at[0], r_a.at[0], next_a)
    all_second = remote(rows.at[in_b], rows.at[in_b], s_b.at[0], r_b.at[0], next_b)
    all_third = remote(full.at[in_a], full.at[in_a], s_c.at[0], r_c.at[0], next_a)

    start(my_a, a, first)
    all_first.wait_recv()
    total = got[0]
    for d in range(1, a):
        total = total + got[d]
    mine_sum[...] = total
    rows[my_b] = total
    start(my_b, b, second)
    all_second.wait_recv()
    total = rows[0]
    for d in range(1, b):
        total = total + rows[d]
    full[my_a] = total
    start(my_a, a, third)
    all_third.wait_recv()
    share = full.shape[1]
    sums = jnp.concatenate([full[k // share, k % share] for k in range(TABLE_ROWS // 8)], axis=0)
    sums = sums * (1.0 / float(ROWS * n * m))
    for i in range(3):
        short_ref[i] = sums[TAPS * i : TAPS * (i + 1)]
    res_ref[...] = sums[24 : 24 + MODES]
    log_ref[...] = -residue_ref[...] * decay_ref[...] * sums[40 : 40 + MODES]
    all_first.wait_send()
    all_second.wait_send()
    all_third.wait_send()


def total_sums(n, m, parts, decay_rate, residue):
    ny = 2
    nx = min(4, n // ny)
    a, b = ny * m, n // ny
    share, groups = SUM_ROWS // 8 // a, parts.shape[1]
    vmem = pl.BlockSpec(memory_space=pltpu.VMEM)
    dma = pltpu.SemaphoreType.DMA
    return pl.pallas_call(
        partial(total_kernel, n, m, nx, ny),
        out_shape=[
            jax.ShapeDtypeStruct((3, TAPS, groups), F32),
            jax.ShapeDtypeStruct((MODES, groups), F32),
            jax.ShapeDtypeStruct((MODES, groups), F32),
        ],
        in_specs=[vmem] * 3,
        out_specs=[vmem] * 3,
        scratch_shapes=[
            pltpu.VMEM((a, share, 8, groups), F32),
            pltpu.VMEM((share, 8, groups), F32),
            pltpu.VMEM((b, share, 8, groups), F32),
            pltpu.VMEM((a, share, 8, groups), F32),
        ]
        + [dma((1,))] * 6,
        compiler_params=pltpu.CompilerParams(
            collective_id=1, has_side_effects=True, vmem_limit_bytes=16 * 2**20
        ),
        name="totals",
    )(parts.reshape(a, share, 8, groups), decay_rate, residue)


def per_device(projected, cotangent, short_filter, residue, decay_rate):
    n, m = lax.axis_size("ctx"), lax.axis_size("seq")
    tokens, upstream = projected[0], cotangent[0]
    block = min(tokens.shape[2], 512)
    known = local_part(n, tokens, upstream, decay_rate, residue, short_filter)
    gated, grad_tokens, sums = finish(tokens, upstream, *known, block)
    return gated[None], grad_tokens[None], *total_sums(n, m, sums, decay_rate, residue)


def solution(mesh):
    placed = (P("seq", None, "ctx", None), P("seq", "ctx", None), P(), P(), P())
    return jax.shard_map(
        per_device,
        mesh=mesh,
        in_specs=placed,
        out_specs=(P("seq", "ctx", None), P("seq", None, "ctx", None), P(), P(), P()),
        check_vma=False,
    )
```

```python
from functools import partial

import jax
import jax.numpy as jnp
from jax import lax
from jax.experimental import pallas as pl
from jax.experimental.pallas import tpu as pltpu
from jax.sharding import PartitionSpec as P

GROUP = 16
MODES = 16
TAPS = 7
LANES = 128
TILE_GROUPS = LANES // GROUP
ROWS = 128
F32, BF16 = jnp.float32, jnp.bfloat16
MESH = pl.DeviceIdType.MESH

HALF = ROWS // 2
QUARTER = ROWS // 4
GROUPED = 4
WAYS = 2

DECAY, RESIDUE, SHORT, TABLE_ROWS = 0, 16, 32, 56
SUM_ROWS = 64


def split(value):
    high = value.astype(BF16)
    return high, (value - high.astype(F32)).astype(BF16)


def iota(shape, dim):
    return lax.broadcasted_iota(jnp.int32, shape, dim)


def dot(left, right):
    return jnp.dot(left, right, preferred_element_type=F32)


def in_group(rows, width, group):
    return (iota((rows, width), 1) % LANES) // GROUP == group


def load_tokens(pad, proj_ref, before_ref, lanes):
    for i in range(3):
        pad[i, 0:8, :] = before_ref[i, :, lanes]
        pad[i, 8 : 8 + ROWS, :] = proj_ref[i, :, lanes].astype(F32)


def feature(pad, taps, i, start, count):
    total = None
    for j in range(TAPS):
        term = taps[TAPS * i + j] * pad[i, 8 + start - j : 8 + start - j + count, :]
        total = term if total is None else total + term
    return total


def tap_rows(wide_ref, lanes):
    return [wide_ref[SHORT + k : SHORT + k + 1, lanes] for k in range(3 * TAPS)]


def expand_table(wide_ref, small, decay_ref, residue_ref, short_ref):
    small[DECAY : DECAY + MODES, :] = decay_ref[...]
    small[RESIDUE : RESIDUE + MODES, :] = residue_ref[...]
    for i in range(3):
        small[SHORT + TAPS * i : SHORT + TAPS * (i + 1), :] = short_ref[i]
    used = SHORT + 3 * TAPS
    groups = small.shape[1]
    small[used:TABLE_ROWS, :] = jnp.zeros((TABLE_ROWS - used, groups), F32)
    value = small[...]
    high = value.astype(BF16).astype(F32)
    middle = (value - high).astype(BF16).astype(F32)
    low = value - high - middle
    pieces = jnp.concatenate([high, middle, low], axis=0).astype(BF16)
    width = min(1024, wide_ref.shape[1])
    for start in range(0, wide_ref.shape[1], width):
        owner = (iota((groups, width), 1) + start) // GROUP
        spread = (iota((groups, width), 0) == owner).astype(F32).astype(BF16)
        got = dot(pieces, spread)
        wide_ref[:, start : start + width] = got[0:TABLE_ROWS] + (
            got[TABLE_ROWS : 2 * TABLE_ROWS] + got[2 * TABLE_ROWS :]
        )


def lanes_of(tile):
    return pl.ds(pl.multiple_of(tile * LANES, LANES), LANES)


def select_groups(source, begin, count, rows, columns):
    total = source[begin + rows.start : begin + rows.stop, columns]
    for g in range(1, TILE_GROUPS):
        at = begin + g * count
        total = jnp.where(
            in_group(rows.stop - rows.start, columns.stop - columns.start, g),
            source[at + rows.start : at + rows.stop, columns],
            total,
        )
    return total


def local_kernel(
    n, proj_hbm, cot_hbm, decay_ref, residue_ref, short_ref,
    wide_ref, before_ref, after_ref, ends_ref, local_ref, near_hbm, into_ref, feat_hbm,
    proj_ref, cot_ref, near_ref, feat_ref, small, out_f, out_b, got_f, got_b, got, back, tables, streams, pad, parts, *scratch,
):
    left_pairs, right_pairs, pair_sums = (scratch[k * WAYS : (k + 1) * WAYS] for k in range(3))
    scratch = scratch[3 * WAYS :]
    rights, products, products_low = (scratch[k * GROUPED : (k + 1) * GROUPED] for k in range(3))
    local_sem, halo_send, halo_recv, s_out, r_out, s_in, r_in = scratch[3 * GROUPED :]
    me = lax.axis_index("ctx")
    right_dev, left_dev = lax.rem(me + 1, n), lax.rem(me + n - 1, n)
    far_back = (LANES - 1 - iota((MODES, LANES), 1)).astype(F32)

    def peer_of(k):
        return lax.rem(me + k, n)

    def each(action):
        def run(k, carry):
            action(k)
            return carry

        lax.fori_loop(1, n, run, 0)

    def remote(source, target, send_sem, recv_sem, to):
        return pltpu.make_async_remote_copy(
            src_ref=source,
            dst_ref=target,
            send_sem=send_sem,
            recv_sem=recv_sem,
            device_id={"ctx": to},
            device_id_type=MESH,
        )

    loads = [
        pltpu.make_async_copy(proj_hbm, proj_ref, local_sem.at[0]),
        pltpu.make_async_copy(cot_hbm, cot_ref, local_sem.at[1]),
    ]
    stores = [
        pltpu.make_async_copy(near_ref, near_hbm, local_sem.at[2]),
        pltpu.make_async_copy(feat_ref, feat_hbm, local_sem.at[3]),
    ]
    for copy in loads:
        copy.start()
    barrier = pltpu.get_barrier_semaphore()
    each(
        lambda k: pl.semaphore_signal(
            barrier, inc=1, device_id={"ctx": peer_of(k)}, device_id_type=MESH
        )
    )
    expand_table(wide_ref, small, decay_ref, residue_ref, short_ref)
    for copy in loads:
        copy.wait()
    width = out_f.shape[2]
    for i in range(3):
        tail = proj_ref[i, ROWS - 16 : ROWS, :].astype(F32)[8:16]
        out_f[i] = jnp.concatenate([tail[:, :width], tail[:, width:]], axis=0).astype(BF16)
    for i in range(4):
        head = (cot_ref[0:16, :] if i == 3 else proj_ref[i, 0:16, :]).astype(F32)[0:8]
        out_b[i] = jnp.concatenate([head[:, :width], head[:, width:]], axis=0).astype(BF16)
    pl.semaphore_wait(barrier, n - 1)
    halo = [
        remote(out_f, got_f, halo_send.at[0], halo_recv.at[0], right_dev),
        remote(out_b, got_b, halo_send.at[1], halo_recv.at[1], left_dev),
    ]
    for copy in halo:
        copy.start()

    def power_of(tile, g):
        column = GROUP * g
        decay = wide_ref[DECAY : DECAY + MODES, lanes_of(tile)]
        return jnp.exp(-decay[:, column : column + 1] * far_back)

    def store_table(tile, at, value):
        high, low = split(value)
        tables[tile, at, 0:LANES] = high
        tables[tile, at, LANES : 2 * LANES] = low
        tables[tile, at, 2 * LANES : 3 * LANES] = high

    def build_tables(tile, carry):
        residue = wide_ref[RESIDUE : RESIDUE + MODES, lanes_of(tile)]
        for g in range(TILE_GROUPS):
            column = GROUP * g
            power = power_of(tile, g)
            filter_row = jnp.sum(residue[:, column : column + 1] * power, axis=0, keepdims=True)
            base = pltpu.roll(
                jnp.broadcast_to(filter_row, (8, LANES)), 1, 1, stride=1, stride_axis=0
            )
            for q in range(HALF, ROWS, 16):
                block = jnp.concatenate(
                    [pltpu.roll(base, q, 1), pltpu.roll(base, q + 8, 1)], axis=0
                )
                keep = iota((16, LANES), 1) <= iota((16, LANES), 0) + q
                begin = HALF * g + q - HALF
                store_table(tile, slice(begin, begin + 16), jnp.where(keep, block, 0.0))
            for k, value in enumerate((power, far_back * power)):
                begin = TILE_GROUPS * (HALF + k * MODES) + MODES * g
                store_table(tile, slice(begin, begin + MODES), value)
        return carry

    def build_two(step, carry):
        return build_tables(2 * step + 1, build_tables(2 * step, carry))

    lax.fori_loop(0, n // 2, build_two, 0)
    for way in range(GROUPED):
        for k in range(3):
            begin = ROWS * k
            rights[way][begin : begin + HALF, 2 * LANES : 4 * LANES] = jnp.zeros(
                (HALF, 2 * LANES), BF16
            )
    for way in range(WAYS):
        right_pairs[way][...] = jnp.zeros((2 * ROWS, 8 * LANES), BF16)

    for copy in halo:
        copy.wait()
    first, last = me == 0, me == n - 1
    for i in range(3):
        part = jnp.where(first, 0.0, got_f[i].astype(F32))
        before_ref[i, :, 0:width] = part[0:8]
        before_ref[i, :, width : 2 * width] = part[8:16]
    for i in range(4):
        part = jnp.where(last, 0.0, got_b[i].astype(F32))
        after_ref[i, :, 0:width] = part[0:8]
        after_ref[i, :, width : 2 * width] = part[8:16]

    def features(tile, way):
        lanes = lanes_of(tile)
        load_tokens(pad, proj_ref, before_ref, lanes)
        taps = tap_rows(wide_ref, lanes)
        step = 32
        for start in range(0, ROWS, step):
            rows = slice(start, start + step)
            f = [feature(pad, taps, i, start, step) for i in range(3)]
            for i in range(3):
                feat_ref[i, rows, lanes] = f[i]
            high, low = split(f[1] * f[2])
            streams[tile, rows, 0:LANES] = high
            streams[tile, rows, LANES : 2 * LANES] = low
            for k, value in enumerate((high, high, low)):
                begin = ROWS * k + start
                rights[way][begin : begin + step, 0:LANES] = value
                if start < HALF:
                    begin = begin + HALF
                    rights[way][begin : begin + step, 2 * LANES : 3 * LANES] = value
            value = cot_ref[rows, lanes].astype(F32) * f[0]
            turn = 7 - iota((8, LANES), 0)
            turned = jnp.concatenate(
                [
                    jnp.take_along_axis(value[r : r + 8], turn, axis=0)
                    for r in range(step - 8, -8, -8)
                ],
                axis=0,
            )
            high, low = split(turned)
            begin = 2 * LANES * way
            at = slice(ROWS - step - start, ROWS - start)
            parts[at, begin : begin + LANES] = high
            parts[at, begin + LANES : begin + 2 * LANES] = low

    def place(tile, way, flipped):
        streams[tile, :, 2 * LANES : 4 * LANES] = flipped
        for k, column in enumerate((0, 0, LANES)):
            value = flipped[:, column : column + LANES]
            begin = ROWS * k
            rights[way][begin : begin + ROWS, LANES : 2 * LANES] = value
            rights[way][begin + HALF : begin + ROWS, 3 * LANES : 4 * LANES] = value[0:HALF]

    modes, both = slice(0, MODES), slice(0, 2 * LANES)

    def send_out(k):
        return remote(
            ends_ref.at[peer_of(k)], got.at[me], s_out.at[0], r_out.at[0], peer_of(k)
        )

    def begin_tiles(step, carry):
        ks = [step * GROUPED + way for way in range(GROUPED)]
        for way, k in enumerate(ks):
            features(peer_of(k), way)
        for way, k in enumerate(ks):
            place(peer_of(k), way, parts[:, 2 * LANES * way : 2 * LANES * (way + 1)])
        for way, k in enumerate(ks):
            tile = peer_of(k)
            products[way][...] = dot(tables[tile], rights[way][:, 0 : 2 * LANES])
            products_low[way][...] = dot(
                tables[tile, 0 : TILE_GROUPS * HALF, :], rights[way][:, 2 * LANES : 4 * LANES]
            )
        for way, k in enumerate(ks):
            tile = peer_of(k)
            first_end = TILE_GROUPS * HALF
            ends = select_groups(products[way], first_end, MODES, modes, both)
            ends_ref[tile, 0:MODES, :] = ends[:, 0:LANES]
            ends_ref[tile, MODES : 2 * MODES, :] = ends[:, LANES : 2 * LANES]
            first_lag = first_end + TILE_GROUPS * MODES
            lags = select_groups(products[way], first_lag, MODES, modes, both)
            local_ref[tile, 0:MODES, :] = lags[:, 0:LANES]
            local_ref[tile, MODES : 2 * MODES, :] = lags[:, LANES : 2 * LANES]
            for start in range(0, ROWS, 32):
                source = products[way] if start >= HALF else products_low[way]
                begin = start % HALF
                near = select_groups(source, 0, HALF, slice(begin, begin + 32), both)
                near_ref[0, start : start + 32, lanes_of(tile)] = near[:, 0:LANES]
                near_ref[1, start : start + 32, lanes_of(tile)] = near[:, LANES : 2 * LANES]
        for k in ks:

            @pl.when(k != 0)
            def _():
                send_out(k).start()

        return carry

    lax.fori_loop(0, n // GROUPED, begin_tiles, 0)
    for copy in stores:
        copy.start()

    lane = iota((MODES, LANES), 1)

    def correlate(step, carry):
        tiles = [step * WAYS + way for way in range(WAYS)]
        for way, tile in enumerate(tiles):
            for h in range(4):
                at = slice(QUARTER * h, QUARTER * (h + 1))
                columns = slice(2 * LANES * h, 2 * LANES * (h + 1))
                flipped = streams[tile, at, 2 * LANES : 4 * LANES]
                for g in range(TILE_GROUPS):
                    left_pairs[way][QUARTER * g : QUARTER * (g + 1), columns] = jnp.where(
                        in_group(QUARTER, 2 * LANES, g), flipped, jnp.zeros_like(flipped)
                    )
                keep = ROWS - QUARTER * h
                for k in range(2):
                    value = streams[tile, 0:keep, LANES * k : LANES * (k + 1)]
                    at = slice(ROWS * (k + 1) - keep, ROWS * (k + 1))
                    for column in (2 * LANES * h, 2 * LANES * h + LANES):
                        right_pairs[way][at, column : column + LANES] = value
        for way in range(WAYS):
            pair_sums[way][...] = lax.dot_general(
                left_pairs[way][...],
                right_pairs[way][...],
                (((1,), (1,)), ((), ())),
                preferred_element_type=F32,
            )
        for way, tile in enumerate(tiles):
            res_sum = jnp.zeros((MODES, LANES), F32)
            lag_sum = jnp.zeros((MODES, LANES), F32)
            for g in range(TILE_GROUPS):
                total = None
                for q in range(0, QUARTER, 8):
                    at = slice(QUARTER * g + q, QUARTER * g + q + 8)
                    block = pair_sums[way][at, 0:LANES] + pair_sums[way][at, LANES : 2 * LANES]
                    keep = iota((8, LANES), 1) + iota((8, LANES), 0) <= ROWS - 1 - q
                    block = jnp.where(keep, block, 0.0)
                    if q:
                        block = pltpu.roll(block, q, 1)
                    total = block if total is None else total + block
                by_lag = jnp.sum(
                    pltpu.roll(total, 0, 1, stride=1, stride_axis=0), axis=0, keepdims=True
                )
                weighted = power_of(tile, g) * by_lag
                res_sum = jnp.where(
                    lane == GROUP * g, jnp.sum(weighted, axis=1, keepdims=True), res_sum
                )
                lag_sum = jnp.where(
                    lane == GROUP * g,
                    jnp.sum(far_back * weighted, axis=1, keepdims=True),
                    lag_sum,
                )
            local_ref[tile, 2 * MODES : 3 * MODES, :] = res_sum
            local_ref[tile, 3 * MODES : 4 * MODES, :] = lag_sum
        return carry

    lax.fori_loop(0, n // WAYS // 2, correlate, 0)

    def send_in(k):
        return remote(back.at[peer_of(k)], into_ref.at[me], s_in.at[0], r_in.at[0], peer_of(k))

    others = pl.ds(0, n - 1)
    all_out = remote(ends_ref.at[others], got.at[others], s_out.at[0], r_out.at[0], right_dev)
    all_in = remote(back.at[others], into_ref.at[others], s_in.at[0], r_in.at[0], right_dev)
    got[me] = ends_ref[me]
    all_out.wait_recv()
    decay = wide_ref[DECAY : DECAY + MODES, lanes_of(me)]
    pole = jnp.exp(-decay)
    whole = jnp.exp(-decay * float(ROWS))
    zero = jnp.zeros((MODES, LANES), F32)

    def scan(step, carry):
        state, lagged, res, lag, beyond = carry
        for k in range(4):
            d = step * 4 + k
            adjoint = got[d, MODES : 2 * MODES, :]
            back[d, 0:MODES, :] = state
            res = res + adjoint * state
            lag = lag + adjoint * (state + float(ROWS) * lagged)
            state, lagged = whole * state + got[d, 0:MODES, :], whole * (lagged + state)
            d = n - 1 - d
            back[d, MODES : 2 * MODES, :] = beyond
            beyond = whole * beyond + got[d, MODES : 2 * MODES, :]
        return state, lagged, res, lag, beyond

    _, _, cross_res, cross_lag, _ = lax.fori_loop(0, n // 4, scan, (zero,) * 5)
    each(lambda k: send_in(k).start())
    into_ref[me] = back[me]

    lax.fori_loop(n // WAYS // 2, n // WAYS, correlate, 0)
    local_ref[me, 2 * MODES : 3 * MODES, :] = (
        local_ref[me, 2 * MODES : 3 * MODES, :] + pole * cross_res
    )
    local_ref[me, 3 * MODES : 4 * MODES, :] = (
        local_ref[me, 3 * MODES : 4 * MODES, :] + pole * cross_lag
    )
    all_in.wait_recv()
    all_out.wait_send()
    all_in.wait_send()
    for copy in stores:
        copy.wait()


def local_part(n, tokens, cotangent, decay_rate, residue, short_filter):
    channels = tokens.shape[2]
    groups = residue.shape[1]
    half = channels // 2
    vmem = pl.BlockSpec(memory_space=pltpu.VMEM)
    wide_rows = TILE_GROUPS * (HALF + 2 * MODES)
    return pl.pallas_call(
        partial(local_kernel, n),
        in_specs=[pl.BlockSpec(memory_space=pl.ANY)] * 2 + [vmem] * 3,
        out_specs=[vmem] * 5 + [pl.BlockSpec(memory_space=pl.ANY), vmem]
        + [pl.BlockSpec(memory_space=pl.ANY)],
        out_shape=[
            jax.ShapeDtypeStruct(shape, F32)
            for shape in (
                (TABLE_ROWS, channels),
                (3, 8, channels),
                (4, 8, channels),
                (n, 2 * MODES, LANES),
                (n, 4 * MODES, LANES),
                (2, ROWS, channels),
                (n, 2 * MODES, LANES),
                (3, ROWS, channels),
            )
        ],
        scratch_shapes=[
            pltpu.VMEM((3, ROWS, channels), BF16),
            pltpu.VMEM((ROWS, channels), BF16),
            pltpu.VMEM((2, ROWS, channels), F32),
            pltpu.VMEM((3, ROWS, channels), F32),
            pltpu.VMEM((TABLE_ROWS, groups), F32),
            pltpu.VMEM((3, 16, half), BF16),
            pltpu.VMEM((4, 16, half), BF16),
            pltpu.VMEM((3, 16, half), BF16),
            pltpu.VMEM((4, 16, half), BF16),
            pltpu.VMEM((n, 2 * MODES, LANES), F32),
            pltpu.VMEM((n, 2 * MODES, LANES), F32),
            pltpu.VMEM((n, wide_rows, 3 * LANES), BF16),
            pltpu.VMEM((n, ROWS, 4 * LANES), BF16),
            pltpu.VMEM((3, ROWS + 8, LANES), F32),
            pltpu.VMEM((ROWS, 2 * LANES * GROUPED), BF16),
        ]
        + [pltpu.VMEM((TILE_GROUPS * QUARTER, 8 * LANES), BF16)] * WAYS
        + [pltpu.VMEM((2 * ROWS, 8 * LANES), BF16)] * WAYS
        + [pltpu.VMEM((TILE_GROUPS * QUARTER, 2 * LANES), F32)] * WAYS
        + [pltpu.VMEM((3 * ROWS, 4 * LANES), BF16)] * GROUPED
        + [pltpu.VMEM((wide_rows, 2 * LANES), F32)] * GROUPED
        + [pltpu.VMEM((TILE_GROUPS * HALF, 2 * LANES), F32)] * GROUPED
        + [pltpu.SemaphoreType.DMA((4,))]
        + [pltpu.SemaphoreType.DMA((2,))] * 2
        + [pltpu.SemaphoreType.DMA((1,))] * 4,
        compiler_params=pltpu.CompilerParams(
            collective_id=0, has_side_effects=True, vmem_limit_bytes=60 * 2**20
        ),
        name="local",
    )(tokens, cotangent, decay_rate, residue, short_filter)


def finish_kernel(
    tiles, proj_ref, cot_ref, before_ref, after_ref, wide_ref, ends_ref, local_ref,
    near_ref, into_ref, feat_ref, gated_ref, grad_ref, sums_ref,
    pads, grads, lefts, rights, fars, sums, placed,
):
    step_index = pl.program_id(0)

    def spans(tile):
        return slice(tile * LANES, (tile + 1) * LANES)

    for tile in range(tiles):
        lanes = spans(tile)
        pad = pads.at[tile]
        load_tokens(pad, proj_ref, before_ref, lanes)
        for i in range(3):
            pad[i, 8 + ROWS : 16 + ROWS, :] = after_ref[i, :, lanes]
        pick = iota((MODES, LANES), 1) % MODES == iota((MODES, LANES), 0)

        def across(row):
            block = wide_ref[row : row + MODES, lanes]
            return jnp.sum(jnp.where(pick, block, 0.0), axis=0, keepdims=True)

        ahead = (iota((ROWS, LANES), 0) + 1).astype(F32)
        high, low = split(across(RESIDUE) * jnp.exp(-across(DECAY) * ahead))
        lefts[tile, :, 0:LANES] = high
        lefts[tile, :, LANES : 2 * LANES] = low
        lefts[tile, :, 2 * LANES : 3 * LANES] = high
        high, low = split(
            jnp.concatenate(
                [into_ref[tile, 0:MODES, :], into_ref[tile, MODES : 2 * MODES, :]], axis=1
            )
        )
        for g in range(TILE_GROUPS):
            keep = in_group(MODES, 2 * LANES, g)
            chosen = jnp.where(keep, high, jnp.zeros_like(high))
            begin = MODES * g
            rights[tile, begin : begin + MODES, :] = chosen
            rights[tile, ROWS + begin : ROWS + begin + MODES, :] = chosen
            rights[tile, 2 * ROWS + begin : 2 * ROWS + begin + MODES, :] = jnp.where(
                keep, low, jnp.zeros_like(low)
            )
    for tile in range(tiles):
        fars[tile] = dot(lefts[tile], rights[tile])
    for tile in range(tiles):
        lanes = spans(tile)
        long_conv = near_ref[0, :, lanes] + fars[tile, :, 0:LANES]
        for start in range(0, ROWS, 8):
            rows = slice(start, start + 8)
            value = near_ref[1, rows, lanes] + fars[tile, rows, LANES : 2 * LANES]
            turned = jnp.take_along_axis(value, 7 - iota((8, LANES), 0), axis=0)
            at = slice(ROWS - 8 - start, ROWS - start)
            grads[tile, 1, at, :] = turned * feat_ref[2, at, lanes]
            grads[tile, 2, at, :] = turned * feat_ref[1, at, lanes]
        gated_ref[:, lanes] = (feat_ref[0, :, lanes] * long_conv).astype(BF16)
        grads[tile, 0, 0:ROWS, :] = cot_ref[:, lanes].astype(F32) * long_conv
    for tile in range(tiles):
        lanes = spans(tile)
        pad = pads.at[tile]
        grad = grads.at[tile]
        taps = tap_rows(wide_ref, lanes)
        decay = wide_ref[DECAY : DECAY + MODES, lanes]
        residue = wide_ref[RESIDUE : RESIDUE + MODES, lanes]
        state = into_ref[tile, 0:MODES, :]
        adjoint = into_ref[tile, MODES : 2 * MODES, :]

        pole = jnp.exp(-decay)
        inverse = jnp.exp(decay)
        next_feat = [feature(pad, taps, i, ROWS, 8) for i in range(3)]
        next_cot = after_ref[3, :, lanes]
        next_in = next_feat[1] * next_feat[2]
        next_grad = next_cot * next_feat[0]
        whole = jnp.exp(-decay * float(ROWS))
        behind = residue * pole * (whole * state + ends_ref[tile, 0:MODES, :])
        beyond = residue * adjoint
        lag_pos = residue
        lag_neg = residue * inverse
        conv_rows, mixer_rows, filters, filters_neg = [], [], [], []
        for k in range(TAPS - 1):
            filters.append(jnp.sum(lag_pos, axis=0, keepdims=True))
            filters_neg.append(jnp.sum(lag_neg, axis=0, keepdims=True))
            conv = jnp.sum(behind, axis=0, keepdims=True)
            mixer = jnp.sum(beyond, axis=0, keepdims=True)
            for j in range(k + 1):
                conv = conv + filters[k - j] * next_in[j : j + 1]
            for j in range(k):
                mixer = mixer - filters_neg[k - j - 1] * next_grad[j : j + 1]
            conv_rows.append(conv)
            mixer_rows.append(mixer)
            lag_pos, lag_neg = lag_pos * pole, lag_neg * inverse
            behind, beyond = behind * pole, beyond * inverse
        blank = jnp.zeros((8 - (TAPS - 1), LANES), F32)
        next_conv = jnp.concatenate(conv_rows + [blank], axis=0)
        next_mixer = jnp.concatenate(mixer_rows + [blank], axis=0)
        grad[0, ROWS : ROWS + 8, :] = next_cot * next_conv
        grad[1, ROWS : ROWS + 8, :] = next_mixer * next_feat[2]
        grad[2, ROWS : ROWS + 8, :] = next_mixer * next_feat[1]

        step = 32
        short = []
        for i in range(3):
            totals = [None] * TAPS
            for start in range(0, ROWS, step):
                rows = slice(start, start + step)
                own = pad[i, 8 + start : 8 + start + step, :]
                total = None
                for j in range(TAPS):
                    ahead_grad = grad[i, start + j : start + j + step, :]
                    term = taps[TAPS * i + j] * ahead_grad
                    total = term if total is None else total + term
                    product = own * ahead_grad
                    part = product[0:8]
                    for r in range(8, step, 8):
                        part = part + product[r : r + 8]
                    totals[j] = part if totals[j] is None else totals[j] + part
                grad_ref[i, rows, lanes] = total.astype(BF16)
            short += [jnp.sum(part, axis=0, keepdims=True) for part in totals]
        short.append(jnp.zeros((3, LANES), F32))
        lag_sum = local_ref[tile, 3 * MODES : 4 * MODES, :] + pole * (
            local_ref[tile, MODES : 2 * MODES, :] * state + local_ref[tile, 0:MODES, :] * adjoint
        )
        res_sum = local_ref[tile, 2 * MODES : 3 * MODES, :]
        rest = jnp.zeros((SUM_ROWS - TABLE_ROWS, LANES), F32)
        high, low = split(jnp.concatenate(short + [res_sum, lag_sum, rest], axis=0))
        at = slice(SUM_ROWS * tile, SUM_ROWS * (tile + 1))
        sums[at, 0:LANES] = high
        sums[at, LANES : 2 * LANES] = low

    member = (iota((2 * LANES, LANES), 0) % LANES) // GROUP == iota((2 * LANES, LANES), 1)
    by_group = dot(sums[...], member.astype(F32).astype(BF16))
    total = by_group[0:SUM_ROWS]
    for tile in range(1, tiles):
        part = by_group[SUM_ROWS * tile : SUM_ROWS * (tile + 1)]
        total = total + pltpu.roll(part, TILE_GROUPS * tile, 1)
    placed[step_index] = total

    @pl.when(step_index == pl.num_programs(0) - 1)
    def _():
        groups = sums_ref.shape[1]
        width = min(groups, LANES)
        stride = tiles * TILE_GROUPS
        for begin in range(0, groups, width):
            total = placed[begin // stride]
            for k in range(1, width // stride):
                total = total + pltpu.roll(placed[begin // stride + k], stride * k, 1)
            sums_ref[:, begin : begin + width] = total[:, 0:width]


def finish(tokens, cotangent, wide, before, after, ends, local, near, into, feats, block):
    channels = tokens.shape[2]
    tiles = block // LANES
    groups = channels // GROUP

    def per_tile(rows):
        return pl.BlockSpec((tiles, rows, LANES), lambda t: (t, 0, 0))

    def stack(k, rows):
        return pl.BlockSpec((k, rows, block), lambda t: (0, 0, t))

    plane = pl.BlockSpec((ROWS, block), lambda t: (0, t))
    return pl.pallas_call(
        partial(finish_kernel, tiles),
        grid=(channels // block,),
        in_specs=[
            stack(3, ROWS),
            plane,
            stack(3, 8),
            stack(4, 8),
            pl.BlockSpec((TABLE_ROWS, block), lambda t: (0, t)),
            per_tile(2 * MODES),
            per_tile(4 * MODES),
            stack(2, ROWS),
            per_tile(2 * MODES),
            stack(3, ROWS),
        ],
        out_specs=[plane, stack(3, ROWS), pl.BlockSpec((SUM_ROWS, groups), lambda t: (0, 0))],
        out_shape=[
            jax.ShapeDtypeStruct((ROWS, channels), BF16),
            jax.ShapeDtypeStruct((3, ROWS, channels), BF16),
            jax.ShapeDtypeStruct((SUM_ROWS, groups), F32),
        ],
        scratch_shapes=[
            pltpu.VMEM((tiles, 3, ROWS + 16, LANES), F32),
            pltpu.VMEM((tiles, 3, ROWS + 8, LANES), F32),
            pltpu.VMEM((tiles, ROWS, 3 * LANES), BF16),
            pltpu.VMEM((tiles, 3 * ROWS, 2 * LANES), BF16),
            pltpu.VMEM((tiles, ROWS, 2 * LANES), F32),
            pltpu.VMEM((tiles * SUM_ROWS, 2 * LANES), BF16),
            pltpu.VMEM((channels // block, SUM_ROWS, LANES), F32),
        ],
        compiler_params=pltpu.CompilerParams(vmem_limit_bytes=62 * 2**20),
        name="finish",
    )(tokens, cotangent, before, after, wide, ends, local, near, into, feats)


def total_kernel(
    n, m, nx, ny, part_ref, decay_ref, residue_ref, short_ref, res_ref, log_ref,
    got, mine_sum, rows, full, s_a, r_a, s_b, r_b, s_c, r_c,
):
    me, genome = lax.axis_index("ctx"), lax.axis_index("seq")
    x, y, z = lax.rem(me, nx), lax.rem(lax.div(me, nx), ny), lax.div(me, nx * ny)
    a, b = ny * m, n // ny
    my_a, my_b = y * m + genome, z * nx + x

    def id_a(k):
        return {"ctx": (z * ny + lax.div(k, m)) * nx + x, "seq": lax.rem(k, m)}

    def id_b(k):
        return {"ctx": (lax.div(k, nx) * ny + y) * nx + lax.rem(k, nx), "seq": genome}

    def ahead(mine, count, k):
        return lax.rem(mine + k, count)

    def each(count, action):
        def run(k, carry):
            action(k)
            return carry

        lax.fori_loop(1, count, run, 0)

    def remote(source, target, send_sem, recv_sem, to):
        return pltpu.make_async_remote_copy(
            src_ref=source,
            dst_ref=target,
            send_sem=send_sem,
            recv_sem=recv_sem,
            device_id=to,
            device_id_type=MESH,
        )

    barrier = pltpu.get_barrier_semaphore()

    def greet(to):
        pl.semaphore_signal(barrier, inc=1, device_id=to, device_id_type=MESH)

    each(a, lambda k: greet(id_a(ahead(my_a, a, k))))
    each(b, lambda k: greet(id_b(ahead(my_b, b, k))))
    got[my_a] = part_ref[my_a]
    pl.semaphore_wait(barrier, a - 1 + b - 1)

    def first(to, slot):
        return remote(part_ref.at[to], got.at[slot], s_a.at[0], r_a.at[0], id_a(to))

    def second(to, slot):
        return remote(mine_sum, rows.at[slot], s_b.at[0], r_b.at[0], id_b(to))

    def third(to, slot):
        return remote(full.at[my_a], full.at[slot], s_c.at[0], r_c.at[0], id_a(to))

    def start(mine, count, copy):
        each(count, lambda k: copy(ahead(mine, count, k), mine).start())

    in_a, in_b = pl.ds(0, a - 1), pl.ds(0, b - 1)
    next_a = id_a(ahead(my_a, a, 1))
    next_b = id_b(ahead(my_b, b, 1))
    all_first = remote(part_ref.at[in_a], got.at[in_a], s_a.at[0], r_a.at[0], next_a)
    all_second = remote(rows.at[in_b], rows.at[in_b], s_b.at[0], r_b.at[0], next_b)
    all_third = remote(full.at[in_a], full.at[in_a], s_c.at[0], r_c.at[0], next_a)

    start(my_a, a, first)
    all_first.wait_recv()
    total = got[0]
    for d in range(1, a):
        total = total + got[d]
    mine_sum[...] = total
    rows[my_b] = total
    start(my_b, b, second)
    all_second.wait_recv()
    total = rows[0]
    for d in range(1, b):
        total = total + rows[d]
    full[my_a] = total
    start(my_a, a, third)
    all_third.wait_recv()
    share = full.shape[1]
    sums = jnp.concatenate([full[k // share, k % share] for k in range(TABLE_ROWS // 8)], axis=0)
    sums = sums * (1.0 / float(ROWS * n * m))
    for i in range(3):
        short_ref[i] = sums[TAPS * i : TAPS * (i + 1)]
    res_ref[...] = sums[24 : 24 + MODES]
    log_ref[...] = -residue_ref[...] * decay_ref[...] * sums[40 : 40 + MODES]
    all_first.wait_send()
    all_second.wait_send()
    all_third.wait_send()


def total_sums(n, m, parts, decay_rate, residue):
    ny = 2
    nx = min(4, n // ny)
    a, b = ny * m, n // ny
    share, groups = SUM_ROWS // 8 // a, parts.shape[1]
    vmem = pl.BlockSpec(memory_space=pltpu.VMEM)
    dma = pltpu.SemaphoreType.DMA
    return pl.pallas_call(
        partial(total_kernel, n, m, nx, ny),
        out_shape=[
            jax.ShapeDtypeStruct((3, TAPS, groups), F32),
            jax.ShapeDtypeStruct((MODES, groups), F32),
            jax.ShapeDtypeStruct((MODES, groups), F32),
        ],
        in_specs=[vmem] * 3,
        out_specs=[vmem] * 3,
        scratch_shapes=[
            pltpu.VMEM((a, share, 8, groups), F32),
            pltpu.VMEM((share, 8, groups), F32),
            pltpu.VMEM((b, share, 8, groups), F32),
            pltpu.VMEM((a, share, 8, groups), F32),
        ]
        + [dma((1,))] * 6,
        compiler_params=pltpu.CompilerParams(
            collective_id=1, has_side_effects=True, vmem_limit_bytes=16 * 2**20
        ),
        name="totals",
    )(parts.reshape(a, share, 8, groups), decay_rate, residue)


def per_device(projected, cotangent, short_filter, residue, decay_rate):
    n, m = lax.axis_size("ctx"), lax.axis_size("seq")
    tokens, upstream = projected[0], cotangent[0]
    block = min(tokens.shape[2], 512)
    known = local_part(n, tokens, upstream, decay_rate, residue, short_filter)
    gated, grad_tokens, sums = finish(tokens, upstream, *known, block)
    return gated[None], grad_tokens[None], *total_sums(n, m, sums, decay_rate, residue)


def solution(mesh):
    placed = (P("seq", None, "ctx", None), P("seq", "ctx", None), P(), P(), P())
    return jax.shard_map(
        per_device,
        mesh=mesh,
        in_specs=placed,
        out_specs=(P("seq", "ctx", None), P("seq", None, "ctx", None), P(), P(), P()),
        check_vma=False,
    )
```
